32 devices in a mesh: dp: 8 (over z, y), rep: 4 (over x, core).
Axes of the slice: x: 2, y: 2, z: 4, core: 2. Of those that a mesh axis runs over, the one named last changes fastest.
Arguments:
- q_tokens: bfloat16 [128, 64, 512], P(('dp', 'rep')), may hold values from -6 to 6
- p_tokens: bfloat16 [128, 256, 512], P(('dp', 'rep')), may hold values from -6 to 6
- q_cotangent: bfloat16 [128, 64, 512], P(('dp', 'rep')), may hold values from -0.29882812 to 0.29882812
- p_cotangent: bfloat16 [128, 256, 512], P(('dp', 'rep')), may hold values from -0.29882812 to 0.29882812
- positives: int32 [128, 4], P(('dp', 'rep')), may hold values from 0 to 127, all different within a row
- counts: int32 [128], P(('dp', 'rep')), may hold values from 1 to 4
- w_query: bfloat16 [2, 512, 512], replicated, may hold values from -0.25 to 0.25
- b_query: float32 [2, 512], replicated, may hold values from -1.2 to 1.2
- w_key: bfloat16 [2, 512, 512], replicated, may hold values from -0.25 to 0.25
- w_value: bfloat16 [2, 512, 512], replicated, may hold values from -0.25 to 0.25
- b_value: float32 [2, 512], replicated, may hold values from -1.2 to 1.2
- w_out: bfloat16 [2, 512, 512], replicated, may hold values from -1 to 1
- b_out: float32 [2, 512], replicated, may hold values from -1.2 to 1.2
- gain_one: float32 [2, 512], replicated, may hold values from 0.5 to 1.5
- shift_one: float32 [2, 512], replicated, may hold values from -1.2 to 1.2
- w_up: bfloat16 [2, 512, 2048], replicated, may hold values from -0.25 to 0.25
- b_up: float32 [2, 2048], replicated, may hold values from -1.2 to 1.2
- w_down: bfloat16 [2, 2048, 512], replicated, may hold values from -0.1875 to 0.1875
- b_down: float32 [2, 512], replicated, may hold values from -1.2 to 1.2
- gain_two: float32 [2, 512], replicated, may hold values from 0.5 to 1.5
- shift_two: float32 [2, 512], replicated, may hold values from -1.2 to 1.2
Outputs:
- q_out: bfloat16 [128, 64, 512], P(('dp', 'rep'))
- p_out: bfloat16 [128, 256, 512], P(('dp', 'rep'))
- loss_terms: float32 [128], P(('dp', 'rep'))
- q_grad: float32 [128, 64, 512], P(('dp', 'rep'))
- p_grad: float32 [128, 256, 512], P(('dp', 'rep'))
- grad_w_query: float32 [2, 512, 512], replicated
- grad_b_query: float32 [2, 512], replicated
- grad_w_key: float32 [2, 512, 512], replicated
- grad_w_value: float32 [2, 512, 512], replicated
- grad_b_value: float32 [2, 512], replicated
- grad_w_out: float32 [2, 512, 512], replicated
- grad_b_out: float32 [2, 512], replicated
- grad_gain_one: float32 [2, 512], replicated
- grad_shift_one: float32 [2, 512], replicated
- grad_w_up: float32 [2, 512, 2048], replicated
- grad_b_up: float32 [2, 2048], replicated
- grad_w_down: float32 [2, 2048, 512], replicated
- grad_b_down: float32 [2, 512], replicated
- grad_gain_two: float32 [2, 512], replicated
- grad_shift_two: float32 [2, 512], replicated
The draws below stay inside these ranges and needn't reach their ends.
Inputs may be any that keep to these rules, and one draw needn't show every extreme that they name: `positives`: the used slots of a question name different passages.
All inputs are finite; a program needn't handle non-finite values.
Results may differ from the reference program's by a relative error of at most 0.014.
Values may be sent and summed in bfloat16 or wider, within the bound.
No kernel may reach another device: no remote copies, remote signals or barrier semaphores. Data moves between devices by JAX's collectives and lax.ppermute only.
A program may use at most 192 MiB of HBM per device.

```python
import math
import jax
import jax.numpy as jnp
from jax import lax

H = 512
NH = 8
FF = 2048
LQ = 64
LP = 256
MAXPOS = 4
QDEV = 4
PDEV = 4
NQ = 128
NP = 128


def place_ends(array, rng, low, largest):
    extent = array.shape
    index_at = [jax.random.randint(jax.random.fold_in(rng, axis), (), 0, extent[axis]) for axis in range(len(extent))]
    array = array.at[tuple(index_at)].set(low)
    longest = extent.index(max(extent))
    index_at[longest] = (index_at[longest] + 1) % extent[longest]
    return array.at[tuple(index_at)].set(largest)


def levels(own_key, dims, shards, least, largest):
    loudness = 1.0
    for axis_at, parts in shards:
        heights = jax.random.uniform(jax.random.fold_in(jax.random.fold_in(own_key, 6), axis_at), (parts,), jnp.float32, least / len(shards), largest / len(shards))
        loudness = loudness * jnp.repeat(jnp.exp(heights), dims[axis_at] // parts).reshape((-1,) + (1,) * (len(dims) - 1 - axis_at))
    return loudness


def choose_distinct(stream_key, rows, number_of, top, lift):
    ranking = jax.random.permutation(jax.random.fold_in(stream_key, 1), number_of)
    favour = ranking
    for power in range(3):
        favour = favour * favour // number_of
    favour = favour * lift // number_of
    tickets = jax.random.randint(jax.random.fold_in(stream_key, 2), (rows, number_of), 0, 4096) + favour
    sure = jax.random.permutation(jax.random.fold_in(stream_key, 3), rows)[jnp.arange(number_of) % rows]
    tickets = jnp.where(jnp.arange(rows)[:, None] == sure[None, :], 1 << 14, tickets)
    merit = tickets * number_of + jnp.arange(number_of)
    return lax.top_k(merit.astype(jnp.int32), top)[1].astype(jnp.int32)


def noise(own_key, shape, scale, reach, shards=(), kind=jnp.bfloat16):
    values = scale * jax.random.normal(own_key, shape, jnp.float32)
    if shards:
        values = values * levels(own_key, shape, shards, -0.22, 0.18)
    return jnp.clip(values, -reach, reach).astype(kind)


def setup_inputs(seed: int = 0) -> dict:
    key_of = jax.random.split(jax.random.key(seed), 22)
    return {
        "q_tokens": noise(key_of[0], (NQ, LQ, H), 1.0, 6.0, ((0, 32),)),
        "p_tokens": noise(key_of[1], (NP, LP, H), 1.0, 6.0, ((0, 32),)),
        "q_cotangent": noise(key_of[2], (NQ, LQ, H), 0.05, 0.29882812, ((0, 32),)),
        "p_cotangent": noise(key_of[3], (NP, LP, H), 0.05, 0.29882812, ((0, 32),)),
        "positives": choose_distinct(key_of[4], NQ, NP, MAXPOS, 256),
        "counts": place_ends(jax.random.randint(key_of[5], (NQ,), 1, MAXPOS + 1), jax.random.fold_in(key_of[5], 1), 1, MAXPOS).astype(jnp.int32),
        "w_query": noise(key_of[6], (2, H, H), H ** -0.5, 0.25),
        "b_query": noise(key_of[7], (2, H), 0.2, 1.2, (), jnp.float32),
        "w_key": noise(key_of[8], (2, H, H), H ** -0.5, 0.25),
        "w_value": noise(key_of[9], (2, H, H), H ** -0.5, 0.25),
        "b_value": noise(key_of[10], (2, H), 0.2, 1.2, (), jnp.float32),
        "w_out": noise(key_of[11], (2, H, H), (H // 16) ** -0.5, 1.0),
        "b_out": noise(key_of[12], (2, H), 0.2, 1.2, (), jnp.float32),
        "gain_one": jnp.clip(1.0 + 0.1 * jax.random.normal(key_of[13], (2, H), jnp.float32), 0.5, 1.5),
        "shift_one": noise(key_of[14], (2, H), 0.2, 1.2, (), jnp.float32),
        "w_up": noise(key_of[15], (2, H, FF), H ** -0.5, 0.25),
        "b_up": noise(key_of[16], (2, FF), 0.2, 1.2, (), jnp.float32),
        "w_down": noise(key_of[17], (2, FF, H), (FF // 2) ** -0.5, 0.1875),
        "b_down": noise(key_of[18], (2, H), 0.2, 1.2, (), jnp.float32),
        "gain_two": jnp.clip(1.0 + 0.1 * jax.random.normal(key_of[19], (2, H), jnp.float32), 0.5, 1.5),
        "shift_two": noise(key_of[20], (2, H), 0.2, 1.2, (), jnp.float32),
    }


@jax.custom_vjp
def low(v):
    return lax.optimization_barrier(v.astype(jnp.bfloat16)).astype(jnp.float32)

@jax.custom_vjp
def low_back(v):
    return v

def low_keep(v):
    return (low(v), None)

def low_pass(kept, grad):
    return (grad,)

def back_keep(v):
    return (v, None)

def back_low(kept, grad):
    return (low(grad),)
low.defvjp(low_keep, low_pass)
low_back.defvjp(back_keep, back_low)
EPS = 1e-06
HIGH = lax.Precision.HIGHEST

def both_round(v):
    return low_back(low(v))

def layer_norm(v, gain, shift):
    centre = v - lax.optimization_barrier(jnp.mean(v, -1, keepdims=True))
    spread = lax.optimization_barrier(jnp.mean(centre * centre, -1, keepdims=True))
    return centre * lax.rsqrt(spread + EPS) * gain + shift

def matmul(left, right):
    return jnp.dot(left, right, precision=HIGH)

def encode_group(weights, block):
    w_query, b_query, w_key, w_value, b_value, w_out, b_out, gain_one, shift_one, w_up, b_up, w_down, b_down, gain_two, shift_two = weights
    count, length, width = block.shape
    heads = NH
    hsize = width // heads
    rows = block.reshape(count * length, width)
    query = both_round(matmul(rows, w_query) + b_query).reshape(count, length, heads, hsize)
    key = both_round(matmul(rows, w_key)).reshape(count, length, heads, hsize)
    value = both_round(matmul(rows, w_value) + b_value).reshape(count, length, heads, hsize)
    raw = jnp.einsum('blhd,bmhd->bhlm', query, key, precision=HIGH)
    scores = low_back(raw * (1.0 / math.sqrt(hsize)))
    top = lax.optimization_barrier(jnp.max(scores, -1, keepdims=True))
    expo = jnp.exp(scores - top)
    probs = expo / lax.optimization_barrier(jnp.sum(expo, -1, keepdims=True))
    attended = both_round(jnp.einsum('bhlm,bmhd->blhd', low(probs), value, precision=HIGH))
    attended = attended.reshape(count * length, width)
    branch = low_back(matmul(attended, w_out) + b_out)
    normed = layer_norm(rows + branch, gain_one, shift_one)
    inner = low_back(matmul(low(normed), w_up) + b_up)
    activated = low(jax.nn.gelu(inner, approximate=False))
    second = normed + low_back(matmul(activated, w_down) + b_down)
    output = layer_norm(second, gain_two, shift_two)
    return output.reshape(count, length, width)

def encode(tokens, weights, per_group):
    count, length, width = tokens.shape
    grouped = tokens.reshape(count // per_group, per_group, length, width)
    step = jax.checkpoint(encode_group)
    result = lax.map(lambda block: step(weights, block), grouped)
    return result.reshape(count, length, width)

def reference(q_tokens, p_tokens, q_cotangent, p_cotangent, positives, counts, w_query, b_query, w_key, w_value, b_value, w_out, b_out, gain_one, shift_one, w_up, b_up, w_down, b_down, gain_two, shift_two):
    stacked = tuple((w.astype(jnp.float32) for w in (w_query, b_query, w_key, w_value, b_value, w_out, b_out, gain_one, shift_one, w_up, b_up, w_down, b_down, gain_two, shift_two)))
    passages = p_tokens.shape[0]
    live = jnp.arange(positives.shape[1])[None, :] < counts[:, None]
    hits = (positives[:, :, None] == jnp.arange(passages)[None, None, :]) & live[:, :, None]
    mask = lax.optimization_barrier(jnp.sum(hits.astype(jnp.float32), 1))
    scale = 2.0 / math.sqrt(H)

    def forward(q_in, p_in, weights):
        q_weights = tuple((w[0] for w in weights))
        p_weights = tuple((w[1] for w in weights))
        q_result = encode(q_in, q_weights, QDEV)
        p_result = encode(p_in, p_weights, PDEV)
        cls_q = low(q_result[:, 0])
        cls_p = low(p_result[:, 0])
        sim = matmul(cls_q, cls_p.T) * scale
        top = lax.optimization_barrier(jnp.max(sim, -1, keepdims=True))
        expo = jnp.exp(sim - top)
        total = lax.optimization_barrier(jnp.sum(expo, -1))
        pos_total = lax.optimization_barrier(jnp.sum(mask * expo, -1))
        loss = jnp.log(total) - jnp.log(pos_total)
        return (q_result, p_result, loss)
    q_in = q_tokens.astype(jnp.float32)
    p_in = p_tokens.astype(jnp.float32)
    (q_result, p_result, loss), pullback = jax.vjp(forward, q_in, p_in, stacked)
    q_back, p_back, grads = pullback((q_cotangent.astype(jnp.float32), p_cotangent.astype(jnp.float32), jnp.ones_like(loss)))
    return (q_result.astype(jnp.bfloat16), p_result.astype(jnp.bfloat16), loss, q_back, p_back, grads[0], grads[1], grads[2], grads[3], grads[4], grads[5], grads[6], grads[7], grads[8], grads[9], grads[10], grads[11], grads[12], grads[13], grads[14])
```

```python
import functools

import jax
import jax.numpy as jnp
import numpy as np
from jax import lax
from jax.experimental import pallas as pl
from jax.experimental.pallas import tpu as pltpu
from jax.sharding import PartitionSpec as P

HEADS = 8
HS = 64
EPS = 1e-06
F32 = jnp.float32
B16 = jnp.bfloat16
I32 = jnp.int32
HIGH = lax.Precision.HIGHEST
AXES = ("dp", "rep")
SCALE = 0.125
MIB = 1 << 20
ANY = pl.BlockSpec(memory_space=pl.ANY)
SMEM = pl.BlockSpec(memory_space=pltpu.SMEM)
VMEM = pl.BlockSpec(memory_space=pltpu.VMEM)
SMALL = ("b_query", "b_value", "b_out", "gain_one", "shift_one", "b_down", "gain_two", "shift_two")
NSMALL = 12


def dot(a, b):
    return lax.dot_general(a, b, (((1,), (0,)), ((), ())), preferred_element_type=F32)


def dot_nt(a, b):
    return lax.dot_general(a, b, (((1,), (1,)), ((), ())), preferred_element_type=F32)


def dot_tn(a, b):
    return lax.dot_general(a, b, (((0,), (0,)), ((), ())), preferred_element_type=F32)


def dot_high(a, b):
    return lax.dot_general(
        a, b, (((1,), (0,)), ((), ())), precision=HIGH, preferred_element_type=F32
    )


def centred(v):
    c = v - jnp.mean(v, -1, keepdims=True)
    r = lax.rsqrt(jnp.mean(c * c, -1, keepdims=True) + EPS)
    return c * r, r


def norm_back(v, gain, d_out):
    hat, r = centred(v)
    g_gain = jnp.sum(d_out * hat, 0, keepdims=True)
    g_shift = jnp.sum(d_out, 0, keepdims=True)
    d_hat = d_out * gain
    mean_a = jnp.mean(d_hat, -1, keepdims=True)
    mean_b = jnp.mean(d_hat * hat, -1, keepdims=True)
    return r * (d_hat - mean_a - hat * mean_b), g_gain, g_shift, hat


def gelu_pair(x):
    e = jnp.exp(-0.5 * (x * x))
    t = 1.0 / (1.0 + 0.23164188825 * jnp.abs(x))
    poly = t * (
        0.127414796
        + t * (-0.142248368 + t * (0.7107068705 + t * (-0.7265760135 + t * 0.5307027145)))
    )
    tail = poly * e
    phi = jnp.where(x < 0, tail, 1.0 - tail)
    return x * phi, phi + x * (e * 0.3989422804014327)


def stacked(x, group):
    lane = lax.broadcasted_iota(I32, x.shape, 1) // HS
    zero = jnp.zeros_like(x)
    return jnp.concatenate([jnp.where(lane == g, x, zero) for g in range(group)], 0)


def diagonal(o, group):
    rows = o.shape[0] // group
    lane = lax.broadcasted_iota(I32, (rows, o.shape[1]), 1) // HS
    out = o[:rows]
    for g in range(1, group):
        out = jnp.where(lane == g, o[g * rows : (g + 1) * rows], out)
    return out


def softmax(s):
    e = jnp.exp(s - jnp.max(s, -1, keepdims=True))
    return e * (1.0 / jnp.sum(e, -1, keepdims=True))


def attend(q, k, v, group, keep_probs):
    wide = HS * group
    parts = []
    for t in range(HEADS // group):
        at = slice(t * wide, (t + 1) * wide)
        probs = softmax(dot_nt(stacked(q[:, at], group), k[:, at])).astype(B16)
        keep_probs(t, probs)
        parts.append(diagonal(dot(probs, v[:, at]), group))
    return jnp.concatenate(parts, 1).astype(B16)


def attend_back(q, k, v, d_att, group, probs_of):
    wide = HS * group
    dq, dk, dv = [], [], []
    for t in range(HEADS // group):
        at = slice(t * wide, (t + 1) * wide)
        probs = probs_of(t)
        d_stack = stacked(d_att[:, at], group)
        d_probs = dot_nt(d_stack, v[:, at])
        dv.append(dot_tn(probs, d_stack))
        p32 = probs.astype(F32)
        inside = jnp.sum(p32 * d_probs, -1, keepdims=True)
        d_scores = (p32 * (d_probs - inside)).astype(B16)
        dq.append(diagonal(dot(d_scores, k[:, at]), group) * SCALE)
        dk.append(dot_tn(d_scores, stacked(q[:, at], group)))
    return tuple(jnp.concatenate(x, 1).astype(B16) for x in (dq, dk, dv))


def feed(first, w_up, b_up, w_down, b_down, gain, shift, keep):
    hat, _ = centred(first)
    normed = hat * gain + shift
    low = normed.astype(B16)
    second = normed + b_down
    for j in range(w_up.shape[1] // 512):
        at = slice(j * 512, (j + 1) * 512)
        act, slope = gelu_pair(dot(low, w_up[:, at]) + b_up[:, at])
        act = act.astype(B16)
        keep(at, act, slope)
        second = second + dot(act, w_down[at, :])
    return second


def row(ref, e):
    return ref[e : e + 1, :]


def front_kernel(
    positives,
    counts,
    p_x,
    q_x,
    bq,
    bv,
    bo,
    g1,
    s1,
    bu,
    bd,
    g2,
    s2,
    wq,
    wk,
    wv,
    wo,
    wu,
    wd,
    pq,
    pk,
    pv,
    qq,
    qk,
    qv,
    q_probs,
    q_att,
    q_first,
    q_second,
    q_act,
    q_slope,
    q_out,
    payload,
    wqkv_s,
    wo_s,
    wu_s,
    wd_s,
    cls_att,
    cls_x,
    pay_s,
    sems,
):
    b = pl.program_id(0)
    nb = pl.num_programs(0)
    ql = q_x.shape[0] // nb
    copies = [
        pltpu.make_async_copy(src, dst, sems.at[i])
        for i, (src, dst) in enumerate(
            (
                (wq, wqkv_s.at[0]),
                (wk, wqkv_s.at[1]),
                (wv, wqkv_s.at[2]),
                (wo, wo_s),
                (wu, wu_s),
                (wd, wd_s),
            )
        )
    ]

    @pl.when(b == 0)
    def _():
        for c in copies:
            c.start()
        cls_att[...] = jnp.zeros_like(cls_att)
        cls_x[...] = jnp.zeros_like(cls_x)
        for c in copies[:3]:
            c.wait()
        x = q_x[...]
        qq[...] = (dot(x, wqkv_s[0, 0]) + row(bq, 0)).astype(B16) * SCALE
        qk[...] = dot(x, wqkv_s[1, 0]).astype(B16)
        qv[...] = (dot(x, wqkv_s[2, 0]) + row(bv, 0)).astype(B16)

    x = p_x[...]
    q = (dot(x, wqkv_s[0, 1]) + row(bq, 1)).astype(B16) * SCALE
    k = dot(x, wqkv_s[1, 1]).astype(B16)
    v = (dot(x, wqkv_s[2, 1]) + row(bv, 1)).astype(B16)
    pq[...], pk[...], pv[...] = q, k, v
    width = x.shape[1]
    own = (
        lax.broadcasted_iota(I32, (HEADS, width), 1) // HS
        == lax.broadcasted_iota(I32, (HEADS, width), 0)
    )
    q_rows = jnp.where(own, jnp.broadcast_to(q[0:1].astype(F32), (HEADS, width)), 0.0).astype(B16)
    probs = softmax(dot_nt(q_rows, k)).astype(B16)
    mixed = jnp.sum(jnp.where(own, dot(probs, v), 0.0), 0, keepdims=True)
    cls_att[pl.ds(b, 1), :] = mixed
    cls_x[pl.ds(b, 1), :] = x[0:1].astype(F32)

    at = pl.ds(pl.multiple_of(b * ql, ql), ql)

    def keep_probs(t, value):
        q_probs[b, t] = value

    q_att[at, :] = attend(qq[at, :], qk[at, :], qv[at, :], 4, keep_probs)

    @pl.when(b == nb - 1)
    def _():
        for c in copies[3:]:
            c.wait()
        first = cls_x[...] + dot(cls_att[...].astype(B16), wo_s[1]) + row(bo, 1)
        second = feed(
            first, wu_s.at[1], row(bu, 1), wd_s.at[1], row(bd, 1), row(g1, 1), row(s1, 1),
            lambda at, act, slope: None,
        )
        cls_p = centred(second)[0] * row(g2, 1) + row(s2, 1)
        first = q_x[...].astype(F32) + dot(q_att[...], wo_s[0]) + row(bo, 0)
        q_first[...] = first

        def keep(at, act, slope):
            q_act[:, at] = act
            q_slope[:, at] = slope.astype(B16)

        second = feed(
            first, wu_s.at[0], row(bu, 0), wd_s.at[0], row(bd, 0), row(g1, 0), row(s1, 0), keep
        )
        q_second[...] = second
        out = centred(second)[0] * row(g2, 0) + row(s2, 0)
        q_out[...] = out.astype(B16)
        pay_s[...] = jnp.zeros_like(pay_s)
        lanes = lax.broadcasted_iota(I32, (1, width), 1)
        for i in range(4):
            pay_s[i : i + 1, :] = cls_p[i : i + 1]
            pay_s[4 + i : 5 + i, :] = out[i * ql : i * ql + 1]
            mask = jnp.zeros((1, width), F32)
            for j in range(positives.shape[1]):
                mask = jnp.where((lanes == positives[i, j]) & (j < counts[i]), 1.0, mask)
            pay_s[8 + i : 9 + i, :] = mask
        payload[...] = pay_s[...].astype(B16)


def passage_attention_kernel(q, k, v, x, bo, wo, probs, att, first, wo_s, sem):
    copy = pltpu.make_async_copy(wo.at[1], wo_s, sem)

    @pl.when(pl.program_id(0) == 0)
    def _():
        copy.start()

    def keep_probs(t, value):
        probs[t] = value

    a = attend(q[...], k[...], v[...], 2, keep_probs)
    att[...] = a

    @pl.when(pl.program_id(0) == 0)
    def _():
        copy.wait()

    first[...] = x[...].astype(F32) + dot(a, wo_s[...]) + row(bo, 1)


def passage_feed_kernel(first, g1, s1, bu, bd, g2, s2, wu, wd, act, slope, second, out, wu_s, wd_s, sems):
    copies = [
        pltpu.make_async_copy(wu.at[1], wu_s, sems.at[0]),
        pltpu.make_async_copy(wd.at[1], wd_s, sems.at[1]),
    ]

    @pl.when(pl.program_id(0) == 0)
    def _():
        for c in copies:
            c.start()
        for c in copies:
            c.wait()

    def keep(at, a, s):
        act[:, at] = a
        slope[:, at] = s.astype(B16)

    result = feed(first[...], wu_s, row(bu, 1), wd_s, row(bd, 1), row(g1, 1), row(s1, 1), keep)
    second[...] = result
    out[...] = (centred(result)[0] * row(g2, 1) + row(s2, 1)).astype(B16)


def send_unit(wide, grads, table, keep, send, offset, sem_keep, sem_send):
    half, _, width = keep.shape
    blocks = 2 * half
    rows = grads.shape[0] * grads.shape[1] // (width * blocks)
    across = grads.shape[1] // width

    def start(out, base, sem):
        def body(r, carry):
            c = table[base + r]
            src = grads.at[
                pl.ds(pl.multiple_of(c // across * rows, rows), rows),
                pl.ds(pl.multiple_of(c % across * width, width), width),
            ] if wide else grads.at[pl.ds(pl.multiple_of(c * rows, rows), rows), :]
            pltpu.make_async_copy(src, out.at[r, pl.ds(offset, rows), :], sem).start()
            return carry

        lax.fori_loop(0, half, body, 0)

    start(send, half, sem_send)
    start(keep, 0, sem_keep)


def wait_units(keep, send, sem_keep, sem_send):
    pltpu.make_async_copy(send, send, sem_send).wait()
    pltpu.make_async_copy(keep, keep, sem_keep).wait()


def feed_back(d_out, second, first, slope, w_down, w_up, g2, g1, s1):
    d_second, gg2, gs2, _ = norm_back(second, g2, d_out)
    d_down = d_second.astype(B16)
    gb_down = jnp.sum(d_down.astype(F32), 0, keepdims=True)
    d_normed = d_second
    d_inner, gb_up = [], []
    for j in range(w_up.shape[1] // 512):
        at = slice(j * 512, (j + 1) * 512)
        d = (dot_nt(d_down, w_down[at, :]) * slope[:, at].astype(F32)).astype(B16)
        gb_up.append(jnp.sum(d.astype(F32), 0, keepdims=True))
        d_normed = d_normed + dot_nt(d, w_up[:, at])
        d_inner.append(d)
    d_first, gg1, gs1, hat = norm_back(first, g1, d_normed)
    low = (hat * g1 + s1).astype(B16)
    return d_down, d_inner, d_first, low, (gg1, gs1, gb_down, gg2, gs2, gb_up)


def contrast(rowsel, gathered, base, scale):
    total_rows = rowsel.shape[0]
    z = gathered[...]
    place = lax.broadcasted_iota(I32, (total_rows, z.shape[0]), 1)
    sel = rowsel[...]

    def rows_at(k):
        return dot(jnp.where(place == sel + k, 1.0, 0.0).astype(B16), z)

    all_p, all_q, mask = rows_at(0), rows_at(4), rows_at(8)[:, :total_rows]
    sim = dot_nt(all_q.astype(B16), all_p.astype(B16)) * scale
    expo = jnp.exp(sim - jnp.max(sim, -1, keepdims=True))
    total = jnp.sum(expo, -1, keepdims=True)
    hit = mask * expo
    pos_total = jnp.sum(hit, -1, keepdims=True)
    terms = jnp.log(total) - jnp.log(pos_total)
    coeff = expo / total - hit / pos_total
    mine = jnp.where(
        lax.broadcasted_iota(I32, (8, total_rows), 1)
        == base + lax.broadcasted_iota(I32, (8, total_rows), 0),
        1.0,
        0.0,
    )
    d_q = dot_high(dot_high(mine, coeff), all_p) * scale
    d_p = dot_high(dot_high(mine, coeff.T), all_q) * scale
    return dot_high(mine, jnp.broadcast_to(terms, (total_rows, 128))), d_q, d_p


def question_back_kernel(
    table,
    rowsel,
    gathered,
    x,
    cot,
    q,
    k,
    v,
    probs,
    att,
    first,
    second,
    act,
    slope,
    g1,
    s1,
    g2,
    wq,
    wk,
    wv,
    wo,
    wu,
    wd,
    terms,
    d_cls_p,
    x_grad,
    small,
    keep,
    send,
    wqkv_s,
    wo_s,
    wu_s,
    wd_s,
    g_down,
    g_up,
    g_att,
    sems,
    out_sems,
):
    copies = [
        pltpu.make_async_copy(src.at[0], dst, sems.at[i])
        for i, (src, dst) in enumerate(
            (
                (wd, wd_s),
                (wu, wu_s),
                (wo, wo_s),
                (wq, wqkv_s.at[0]),
                (wk, wqkv_s.at[1]),
                (wv, wqkv_s.at[2]),
            )
        )
    ]
    for c in copies:
        c.start()
    n = table.shape[0] - 1
    rows = 2048 // n
    count = 4
    length = x.shape[0] // count
    width = x.shape[1]
    scale = 2.0 / float(np.sqrt(width))
    loss, d_q, d_p = contrast(rowsel, gathered, table[n] * count, scale)
    terms[...] = loss
    d_cls_p[...] = d_p
    place = lax.broadcasted_iota(I32, x.shape, 0)
    d_out = cot[...].astype(F32)
    for i in range(count):
        d_out = d_out + jnp.where(place == i * length, d_q[i : i + 1], 0.0)
    for c in copies[:2]:
        c.wait()
    d_down, d_inner, d_first, low, sums = feed_back(
        d_out, second[...], first[...], slope, wd_s, wu_s, row(g2, 0), row(g1, 0), row(s1, 0)
    )
    gg1, gs1, gb_down, gg2, gs2, gb_up = sums
    g_down[...] = dot_tn(act[...], d_down).astype(B16)
    send_unit(False, g_down, table, keep, send, 0, out_sems.at[0], out_sems.at[1])
    for j, d in enumerate(d_inner):
        g_up[:, j * 512 : (j + 1) * 512] = dot_tn(low, d).astype(B16)
    send_unit(True, g_up, table, keep, send, rows, out_sems.at[0], out_sems.at[1])
    for c in copies[2:]:
        c.wait()
    d_branch = d_first.astype(B16)
    d_att = dot_nt(d_branch, wo_s[...]).astype(B16)
    dq, dk, dv = [], [], []
    for i in range(count):
        at = slice(i * length, (i + 1) * length)
        one = attend_back(
            q[at, :], k[at, :], v[at, :], d_att[at], 4, lambda t, i=i: probs[i, t]
        )
        for parts, value in zip((dq, dk, dv), one):
            parts.append(value)
    dq, dk, dv = (jnp.concatenate(p, 0) for p in (dq, dk, dv))
    rows_x = x[...]
    for i, d in enumerate((dq, dk, dv)):
        g_att[i * width : (i + 1) * width, :] = dot_tn(rows_x, d).astype(B16)
    g_att[3 * width :, :] = dot_tn(att[...], d_branch).astype(B16)
    send_unit(False, g_att, table, keep, send, 2 * rows, out_sems.at[0], out_sems.at[1])
    x_grad[...] = (
        d_first + dot_nt(dq, wqkv_s[0]) + dot_nt(dk, wqkv_s[1]) + dot_nt(dv, wqkv_s[2])
    )
    small[...] = jnp.zeros_like(small)
    values = (
        jnp.sum(dq.astype(F32), 0, keepdims=True),
        jnp.sum(dv.astype(F32), 0, keepdims=True),
        jnp.sum(d_branch.astype(F32), 0, keepdims=True),
        gg1, gs1, gb_down, gg2, gs2, *gb_up,
    )
    for i, value in enumerate(values):
        small[i : i + 1, :] = value
    wait_units(keep, send, out_sems.at[0], out_sems.at[1])


def passage_feed_back_kernel(
    table,
    d_cls,
    cot,
    first,
    second,
    slope,
    g1,
    s1,
    g2,
    act,
    wu,
    wd,
    d_first,
    small,
    keep,
    send,
    wu_s,
    wd_s,
    act_s,
    d_down_s,
    d_inner_s,
    low_s,
    g_down,
    g_up,
    sems,
    out_sems,
):
    b = pl.program_id(0)
    nb = pl.num_programs(0)
    copies = [
        pltpu.make_async_copy(src, dst, sems.at[i])
        for i, (src, dst) in enumerate(((wd.at[1], wd_s), (wu.at[1], wu_s), (act, act_s)))
    ]

    @pl.when(b == 0)
    def _():
        for c in copies:
            c.start()
        small[...] = jnp.zeros_like(small)
        for c in copies[:2]:
            c.wait()

    length = cot.shape[0]
    place = lax.broadcasted_iota(I32, cot.shape, 0)
    d_out = cot[...].astype(F32) + jnp.where(place == 0, d_cls[pl.ds(b, 1), :], 0.0)
    d_down, d_inner, d_one, low, sums = feed_back(
        d_out, second[...], first[...], slope, wd_s, wu_s, row(g2, 1), row(g1, 1), row(s1, 1)
    )
    at = pl.ds(pl.multiple_of(b * length, length), length)
    d_down_s[at, :] = d_down
    low_s[at, :] = low
    for j, d in enumerate(d_inner):
        d_inner_s[at, j * 512 : (j + 1) * 512] = d
    d_first[...] = d_one
    gg1, gs1, gb_down, gg2, gs2, gb_up = sums
    for i, value in enumerate((gg1, gs1, gb_down, gg2, gs2, *gb_up)):
        small[3 + i : 4 + i, :] += value

    @pl.when(b == nb - 1)
    def _():
        copies[2].wait()
        for j in range(4):
            at = slice(j * 512, (j + 1) * 512)
            g_down[at, :] = dot_tn(act_s[:, at], d_down_s[...]).astype(B16)
        send_unit(False, g_down, table, keep, send, 0, out_sems.at[0], out_sems.at[1])
        for j in range(4):
            at = slice(j * 512, (j + 1) * 512)
            g_up[:, at] = dot_tn(low_s[...], d_inner_s[:, at]).astype(B16)
        rows = 2048 // (table.shape[0] - 1)
        send_unit(True, g_up, table, keep, send, rows, out_sems.at[0], out_sems.at[1])
        wait_units(keep, send, out_sems.at[0], out_sems.at[1])


def passage_attention_back_kernel(
    table,
    d_first,
    q,
    k,
    v,
    probs,
    x,
    small_q,
    small_p,
    att,
    wq,
    wk,
    wv,
    wo,
    x_grad,
    keep,
    send,
    wqkv_s,
    wo_s,
    att_s,
    x_s,
    branch_s,
    d_s,
    small_s,
    sent_s,
    g_att,
    sems,
    out_sems,
):
    b = pl.program_id(0)
    nb = pl.num_programs(0)
    copies = [
        pltpu.make_async_copy(src, dst, sems.at[i])
        for i, (src, dst) in enumerate(
            (
                (wo.at[1], wo_s),
                (wq.at[1], wqkv_s.at[0]),
                (wk.at[1], wqkv_s.at[1]),
                (wv.at[1], wqkv_s.at[2]),
                (att, att_s),
            )
        )
    ]

    @pl.when(b == 0)
    def _():
        for c in copies:
            c.start()
        small_s[...] = small_p[...]
        copies[0].wait()

    length, width = d_first.shape
    d_branch = d_first[...].astype(B16)
    d_att = dot_nt(d_branch, wo_s[...]).astype(B16)
    dq, dk, dv = attend_back(q[...], k[...], v[...], d_att, 2, lambda t: probs[t])
    at = pl.ds(pl.multiple_of(b * length, length), length)
    branch_s[at, :] = d_branch
    x_s[at, :] = x[...]
    for i, d in enumerate((dq, dk, dv)):
        d_s[i, at, :] = d
    for i, d in enumerate((dq, dv, d_branch)):
        small_s[i : i + 1, :] += jnp.sum(d.astype(F32), 0, keepdims=True)

    @pl.when(b == 0)
    def _():
        for c in copies[1:4]:
            c.wait()

    x_grad[...] = (
        d_first[...] + dot_nt(dq, wqkv_s[0]) + dot_nt(dk, wqkv_s[1]) + dot_nt(dv, wqkv_s[2])
    )

    @pl.when(b == nb - 1)
    def _():
        copies[4].wait()
        for i in range(3):
            g_att[i * width : (i + 1) * width, :] = dot_tn(x_s[...], d_s[i]).astype(B16)
        g_att[3 * width :, :] = dot_tn(att_s[...], branch_s[...]).astype(B16)
        send_unit(False, g_att, table, keep, send, 0, out_sems.at[0], out_sems.at[1])
        sent_s[...] = jnp.zeros_like(sent_s)
        top = lax.broadcasted_iota(I32, (16, width), 0) == 0
        for e, ref in enumerate((small_q, small_s)):
            for i in range(NSMALL):
                sent_s[e * NSMALL + i] = jnp.where(top, ref[i : i + 1, :], 0.0).astype(B16)
        n = table.shape[0] - 1
        half = n // 2
        rows = 2048 // n

        def start(out, base, sem):
            def body(r, carry):
                pltpu.make_async_copy(
                    sent_s.at[table[base + r]], out.at[r, pl.ds(rows, 16), :], sem
                ).start()
                return carry

            lax.fori_loop(0, half, body, 0)

        start(send, half, out_sems.at[1])
        start(keep, 0, out_sems.at[0])
        wait_units(keep, send, out_sems.at[0], out_sems.at[1])


def place_kernel(e, kinds, starts, n_alias, with_small, *refs):
    table = refs[0]
    pieces = refs[1 : 1 + len(starts)]
    outs = refs[1 + len(starts) + n_alias :]
    n_out = sum(4 if kind == "att" else 1 for kind in kinds)
    n_small = 9 if with_small else 0
    targets, smalls = outs[:n_out], outs[n_out : n_out + n_small]
    scratch = outs[n_out + n_small :]
    stages, sems = scratch[: len(kinds)], scratch[len(kinds)]
    small_s = scratch[len(kinds) + 1] if with_small else None
    n = table.shape[0] - 1
    rows = 2048 // n
    for piece, start in zip(pieces, starts):

        def body(r, carry, piece=piece, start=start):
            c = table[start + r]
            k = 0
            for u, kind in enumerate(kinds):
                stage = stages[u].at[start + r]
                stage[...] = piece[r, u * rows : (u + 1) * rows, :].astype(F32)
                if kind == "down":
                    pltpu.make_async_copy(
                        stage,
                        targets[k].at[e, pl.ds(pl.multiple_of(c * rows, rows), rows), :],
                        sems.at[k],
                    ).start()
                    k += 1
                elif kind == "up":
                    pltpu.make_async_copy(
                        stage,
                        targets[k].at[
                            e,
                            pl.ds(pl.multiple_of(c // 4 * rows, rows), rows),
                            pl.ds(pl.multiple_of(c % 4 * 512, 512), 512),
                        ],
                        sems.at[k],
                    ).start()
                    k += 1
                else:
                    quarter = n // 4
                    for m in range(4):

                        @pl.when(c // quarter == m)
                        def _(m=m, k=k, stage=stage):
                            at = pl.ds(pl.multiple_of(c % quarter * rows, rows), rows)
                            pltpu.make_async_copy(
                                stage, targets[k + m].at[e, at, :], sems.at[k + m]
                            ).start()

                    k += 4
            if with_small:
                block = piece[r, len(kinds) * rows : len(kinds) * rows + 16, :].astype(F32)
                small_s[c] = block[0:8]
            return carry

        lax.fori_loop(0, piece.shape[0], body, 0)
    if with_small:
        for f in range(2):
            for i in range(8):
                smalls[i][f : f + 1, :] = small_s[f * NSMALL + i, 0:1, :]
            for j in range(4):
                smalls[8][f : f + 1, j * 512 : (j + 1) * 512] = small_s[f * NSMALL + 8 + j, 0:1, :]
    for k, target in enumerate(targets):
        pltpu.make_async_copy(target.at[e], target.at[e], sems.at[k]).wait()


def rounds_of(mesh_shape):
    dp, rep = mesh_shape["dp"], mesh_shape["rep"]
    rep_bits = [1 << i for i in range(rep.bit_length() - 1)]
    dp_bits = [rep << i for i in range(dp.bit_length() - 1)]
    even = rep_bits[:1] + rep_bits[1:] + dp_bits
    odd = rep_bits[:1] + dp_bits[:1] + rep_bits[1:] + dp_bits[1:]
    return even, odd


def order_table(rounds, n):
    depth = len(rounds[0])
    table = np.zeros((n, n), np.int32)
    for d in range(n):
        for r in range(n):
            c = d ^ (rounds[0][0] if r >> (depth - 1) & 1 else 0)
            for k in range(1, depth):
                if r >> (depth - 1 - k) & 1:
                    c ^= rounds[c & 1][k]
            table[d, r] = c
    return table


def exchange(x, rounds, k, n):
    perm = [(d, d ^ rounds[d & 1][k]) for d in range(n)]
    return lax.ppermute(x, AXES, perm)


def add(a, b):
    return (a.astype(F32) + b.astype(F32)).astype(B16)


def reduce_blocks(keep, send, rounds, n):
    depth = len(rounds[0])
    for k in range(depth):
        got = exchange(send, rounds, k, n)
        half = keep.shape[0] // 2
        if half:
            send = add(keep[half:], got[half:])
            keep = add(keep[:half], got[:half])
        else:
            keep = add(keep, got)
    return keep


def gather_blocks(block, rounds, n):
    depth = len(rounds[0])
    pieces = [block]
    for k in range(depth - 1, -1, -1):
        if k > 0 and len(pieces) > 1:
            pieces = [jnp.concatenate(pieces, 0)]
        pieces = pieces + [exchange(p, rounds, k, n) for p in pieces]
    return pieces


def gather_rows(x, n):
    got = x[None]
    bits = [1 << i for i in range(n.bit_length() - 1)]
    while bits:
        now, bits = bits[:2], bits[2:]
        masks = [0, now[0]] + ([now[1], now[0] | now[1]] if len(now) > 1 else [])
        got = jnp.concatenate(
            [got]
            + [lax.ppermute(got, AXES, [(d, d ^ m) for d in range(n)]) for m in masks[1:]],
            0,
        )
    return got


def params(limit):
    return pltpu.CompilerParams(vmem_limit_bytes=limit * MIB)


def cost(flops, nbytes):
    return pl.CostEstimate(flops=int(flops), bytes_accessed=int(nbytes), transcendentals=0)


def shape(dims, dtype=F32):
    return jax.ShapeDtypeStruct(dims, dtype)


def sem(count):
    return pltpu.SemaphoreType.DMA((count,))


def shards(
    mesh_shape,
    q_tokens,
    p_tokens,
    q_cotangent,
    p_cotangent,
    positives,
    counts,
    wq,
    bq,
    wk,
    wv,
    bv,
    wo,
    bo,
    g1,
    s1,
    wu,
    bu,
    wd,
    bd,
    g2,
    s2,
):
    n = mesh_shape["dp"] * mesh_shape["rep"]
    rounds = rounds_of(mesh_shape)
    me = lax.axis_index("dp") * mesh_shape["rep"] + lax.axis_index("rep")
    table = lax.dynamic_index_in_dim(jnp.asarray(order_table(rounds, n)), me, 0, False)
    table = jnp.concatenate([table, me[None].astype(I32)])
    qn, ql, h = q_tokens.shape
    pn, plen, _ = p_tokens.shape
    ff = wu.shape[2]
    qr, pr = qn * ql, pn * plen
    assert qn == 4 and pn == 4 and h == 512 and ff == 2048 and 24 <= n and 4 * n <= h
    q_x, p_x = q_tokens.reshape(qr, h), p_tokens.reshape(pr, h)
    q_cot, p_cot = q_cotangent.reshape(qr, h), p_cotangent.reshape(pr, h)
    every = jnp.arange(4 * n, dtype=I32)
    rowsel = ((every // 4) ^ me) * 16 + every % 4

    def seq(width=h):
        return pl.BlockSpec((plen, width), lambda b: (b, 0))

    def whole(*dims):
        return pl.BlockSpec(dims, lambda b: (0,) * len(dims))

    one = whole(2, h)
    front = pl.pallas_call(
        front_kernel,
        name="front",
        grid=(pn,),
        in_specs=[SMEM, SMEM, seq(), whole(qr, h), one, one, one, one, one, whole(2, ff), one, one, one]
        + [ANY] * 6,
        out_specs=[seq()] * 3
        + [whole(qr, h)] * 3
        + [whole(qn, 2, 4 * ql, ql), whole(qr, h), whole(qr, h), whole(qr, h)]
        + [whole(qr, ff), whole(qr, ff), whole(qr, h), whole(16, h)],
        out_shape=[shape((pr, h), B16)] * 3
        + [shape((qr, h), B16)] * 3
        + [shape((qn, 2, 4 * ql, ql), B16), shape((qr, h), B16), shape((qr, h)), shape((qr, h))]
        + [shape((qr, ff), B16), shape((qr, ff), B16), shape((qr, h), B16), shape((16, h), B16)],
        scratch_shapes=[
            pltpu.VMEM((3, 2, h, h), B16),
            pltpu.VMEM((2, h, h), B16),
            pltpu.VMEM((2, h, ff), B16),
            pltpu.VMEM((2, ff, h), B16),
            pltpu.VMEM((8, h), F32),
            pltpu.VMEM((8, h), F32),
            pltpu.VMEM((16, h), F32),
            sem(6),
        ],
        compiler_params=params(40),
        cost_estimate=cost(5e9, 25e6),
    )(positives, counts, p_x, q_x, bq, bv, bo, g1, s1, bu, bd, g2, s2, wq, wk, wv, wo, wu, wd)
    (pq, pk, pv, qq, qk, qv, q_probs, q_att, q_first, q_second, q_act, q_slope, q_out, payload) = front

    gathered = gather_rows(payload, n).reshape(n * 16, h)

    groups = HEADS // 2
    probs_spec = pl.BlockSpec((None, groups, 2 * plen, plen), lambda b: (b, 0, 0, 0))
    p_probs, p_att, p_first = pl.pallas_call(
        passage_attention_kernel,
        name="passage_attention",
        grid=(pn,),
        in_specs=[seq()] * 4 + [one, ANY],
        out_specs=[probs_spec, seq(), seq()],
        out_shape=[
            shape((pn, groups, 2 * plen, plen), B16),
            shape((pr, h), B16),
            shape((pr, h)),
        ],
        scratch_shapes=[pltpu.VMEM((h, h), B16), pltpu.SemaphoreType.DMA],
        compiler_params=params(32),
        cost_estimate=cost(4e9, 12e6),
    )(pq, pk, pv, p_x, bo, wo)
    p_act, p_slope, p_second, p_out = pl.pallas_call(
        passage_feed_kernel,
        name="passage_feed",
        grid=(pn,),
        in_specs=[seq(), one, one, whole(2, ff), one, one, one, ANY, ANY],
        out_specs=[seq(ff), seq(ff), seq(), seq()],
        out_shape=[
            shape((pr, ff), B16),
            shape((pr, ff), B16),
            shape((pr, h)),
            shape((pr, h), B16),
        ],
        scratch_shapes=[pltpu.VMEM((h, ff), B16), pltpu.VMEM((ff, h), B16), sem(2)],
        compiler_params=params(32),
        cost_estimate=cost(9e9, 18e6),
    )(p_first, g1, s1, bu, bd, g2, s2, wu, wd)

    rows = 2048 // n
    half = n // 2
    terms, d_cls_p, q_grad, small_q, q_keep, q_send = pl.pallas_call(
        question_back_kernel,
        name="question_back",
        in_specs=[SMEM] + [VMEM] * 16 + [ANY] * 6,
        out_specs=[VMEM] * 4 + [ANY] * 2,
        out_shape=[
            shape((8, 128)),
            shape((8, h)),
            shape((qr, h)),
            shape((16, h)),
            shape((half, 3 * rows, h), B16),
            shape((half, 3 * rows, h), B16),
        ],
        scratch_shapes=[
            pltpu.VMEM((3, h, h), B16),
            pltpu.VMEM((h, h), B16),
            pltpu.VMEM((h, ff), B16),
            pltpu.VMEM((ff, h), B16),
            pltpu.VMEM((ff, h), B16),
            pltpu.VMEM((h, ff), B16),
            pltpu.VMEM((4 * h, h), B16),
            sem(6),
            sem(2),
        ],
        compiler_params=params(40),
        cost_estimate=cost(5e9, 20e6),
    )(
        table, rowsel[:, None], gathered, q_x, q_cot, qq, qk, qv, q_probs, q_att, q_first, q_second,
        q_act, q_slope, g1, s1, g2, wq, wk, wv, wo, wu, wd,
    )
    q_block = reduce_blocks(q_keep, q_send, rounds, n)
    q_pieces = gather_blocks(q_block, rounds, n)

    d_first, small_p, f_keep, f_send = pl.pallas_call(
        passage_feed_back_kernel,
        name="passage_feed_back",
        grid=(pn,),
        in_specs=[SMEM, whole(8, h), seq(), seq(), seq(), seq(ff), one, one, one] + [ANY] * 3,
        out_specs=[seq(), whole(16, h), ANY, ANY],
        out_shape=[
            shape((pr, h)),
            shape((16, h)),
            shape((half, 2 * rows, h), B16),
            shape((half, 2 * rows, h), B16),
        ],
        scratch_shapes=[
            pltpu.VMEM((h, ff), B16),
            pltpu.VMEM((ff, h), B16),
            pltpu.VMEM((pr, ff), B16),
            pltpu.VMEM((pr, h), B16),
            pltpu.VMEM((pr, ff), B16),
            pltpu.VMEM((pr, h), B16),
            pltpu.VMEM((ff, h), B16),
            pltpu.VMEM((h, ff), B16),
            sem(3),
            sem(2),
        ],
        compiler_params=params(44),
        cost_estimate=cost(18e9, 22e6),
    )(table, d_cls_p, p_cot, p_first, p_second, p_slope, g1, s1, g2, p_act, wu, wd)
    f_block = reduce_blocks(f_keep, f_send, rounds, n)
    f_pieces = gather_blocks(f_block, rounds, n)

    p_grad, a_keep, a_send = pl.pallas_call(
        passage_attention_back_kernel,
        name="passage_attention_back",
        grid=(pn,),
        in_specs=[SMEM, seq(), seq(), seq(), seq(), probs_spec, seq(), whole(16, h), whole(16, h)]
        + [ANY] * 5,
        out_specs=[seq(), ANY, ANY],
        out_shape=[
            shape((pr, h)),
            shape((half, rows + 16, h), B16),
            shape((half, rows + 16, h), B16),
        ],
        scratch_shapes=[
            pltpu.VMEM((3, h, h), B16),
            pltpu.VMEM((h, h), B16),
            pltpu.VMEM((pr, h), B16),
            pltpu.VMEM((pr, h), B16),
            pltpu.VMEM((pr, h), B16),
            pltpu.VMEM((3, pr, h), B16),
            pltpu.VMEM((16, h), F32),
            pltpu.VMEM((n, 16, h), B16),
            pltpu.VMEM((4 * h, h), B16),
            sem(5),
            sem(2),
        ],
        compiler_params=params(44),
        cost_estimate=cost(10e9, 20e6),
    )(table, d_first, pq, pk, pv, p_probs, p_x, small_q, small_p, p_att, wq, wk, wv, wo)
    a_block = reduce_blocks(a_keep, a_send, rounds, n)
    a_pieces = gather_blocks(a_block, rounds, n)

    def place(e, kinds, pieces, before, with_small):
        starts, at = [], 0
        for piece in pieces:
            starts.append(at)
            at += piece.shape[0]
        dims = []
        for kind in kinds:
            dims += {"down": [(2, ff, h)], "up": [(2, h, ff)], "att": [(2, h, h)] * 4}[kind]
        outs = [shape(d) for d in dims]
        smalls = [shape((2, h))] * 8 + [shape((2, ff))] if with_small else []
        first = 1 + len(pieces)
        return pl.pallas_call(
            functools.partial(place_kernel, e, kinds, tuple(starts), len(before), with_small),
            name="place",
            in_specs=[SMEM] + [VMEM] * len(pieces) + [ANY] * len(before),
            out_specs=[ANY] * len(outs) + [VMEM] * len(smalls),
            out_shape=outs + smalls,
            input_output_aliases={first + i: i for i in range(len(before))},
            scratch_shapes=[pltpu.VMEM((n, rows, h), F32) for _ in kinds]
            + [sem(len(outs))]
            + ([pltpu.VMEM((n, 8, h), F32)] if with_small else []),
            compiler_params=params(40),
            cost_estimate=cost(1e6, len(kinds) * 6 * MIB),
        )(table, *pieces, *before)

    down, up, gq, gk, gv, go = place(0, ("down", "up", "att"), q_pieces, [], False)
    down, up = place(1, ("down", "up"), f_pieces, [down, up], False)
    gq, gk, gv, go, *smalls = place(1, ("att",), a_pieces, [gq, gk, gv, go], True)
    sbq, sbv, sbo, sg1, ss1, sbd, sg2, ss2, sbu = smalls
    return (
        q_out.reshape(qn, ql, h),
        p_out.reshape(pn, plen, h),
        terms[:qn, 0],
        q_grad.reshape(qn, ql, h),
        p_grad.reshape(pn, plen, h),
        gq, sbq, gk, gv, sbv, go, sbo, sg1, ss1, up, sbu, down, sbd, sg2, ss2,
    )


def solution(mesh):
    split = P(AXES)
    return jax.shard_map(
        functools.partial(shards, dict(mesh.shape)),
        mesh=mesh,
        in_specs=(split,) * 6 + (P(),) * 15,
        out_specs=(split,) * 5 + (P(),) * 15,
        check_vma=False,
    )
```

```python
import functools

import jax
import jax.numpy as jnp
import numpy as np
from jax import lax
from jax.experimental import pallas as pl
from jax.experimental.pallas import tpu as pltpu
from jax.sharding import PartitionSpec as P

HEADS = 8
HS = 64
EPS = 1e-06
F32 = jnp.float32
B16 = jnp.bfloat16
I32 = jnp.int32
HIGH = lax.Precision.HIGHEST
AXES = ("dp", "rep")
SCALE = 0.125
MIB = 1 << 20
FAR = -3e38
ANY = pl.BlockSpec(memory_space=pl.ANY)
SMEM = pl.BlockSpec(memory_space=pltpu.SMEM)
VMEM = pl.BlockSpec(memory_space=pltpu.VMEM)
SMALL = ("b_query", "b_value", "b_out", "gain_one", "shift_one", "b_down", "gain_two", "shift_two")
NSMALL = 12


def dot(a, b):
    return lax.dot_general(a, b, (((1,), (0,)), ((), ())), preferred_element_type=F32)


def dot_nt(a, b):
    return lax.dot_general(a, b, (((1,), (1,)), ((), ())), preferred_element_type=F32)


def dot_tn(a, b):
    return lax.dot_general(a, b, (((0,), (0,)), ((), ())), preferred_element_type=F32)


def dot_high(a, b):
    return lax.dot_general(
        a, b, (((1,), (0,)), ((), ())), precision=HIGH, preferred_element_type=F32
    )


def centred(v):
    c = v - jnp.mean(v, -1, keepdims=True)
    r = lax.rsqrt(jnp.mean(c * c, -1, keepdims=True) + EPS)
    return c * r, r


def norm_back(hat, r, gain, d_out):
    g_gain = jnp.sum(d_out * hat, 0, keepdims=True)
    g_shift = jnp.sum(d_out, 0, keepdims=True)
    d_hat = d_out * gain
    mean_a = jnp.mean(d_hat, -1, keepdims=True)
    mean_b = jnp.mean(d_hat * hat, -1, keepdims=True)
    return r * (d_hat - mean_a - hat * mean_b), g_gain, g_shift


def gelu_pair(x):
    phi = 0.5 + 0.5 * lax.erf(x * 0.7071067811865476)
    return x * phi, phi + x * (jnp.exp(x * x * -0.5) * 0.3989422804014327)


def stacked(x, group):
    lane = lax.broadcasted_iota(I32, x.shape, 1) // HS
    zero = jnp.zeros_like(x)
    return jnp.concatenate([jnp.where(lane == g, x, zero) for g in range(group)], 0)


def diagonal(o, group):
    rows = o.shape[0] // group
    lane = lax.broadcasted_iota(I32, (rows, o.shape[1]), 1) // HS
    out = o[:rows]
    for g in range(1, group):
        out = jnp.where(lane == g, o[g * rows : (g + 1) * rows], out)
    return out


def softmax(s):
    e = jnp.exp(s - jnp.max(s, -1, keepdims=True))
    return e * (1.0 / jnp.sum(e, -1, keepdims=True))


def attend(q, k, v, group, keep_probs, length=None):
    wide = HS * group
    parts = []
    for t in range(HEADS // group):
        at = slice(t * wide, (t + 1) * wide)
        scores = dot_nt(stacked(q[:, at], group), k[:, at])
        if length:
            rows = lax.broadcasted_iota(I32, scores.shape, 0) % q.shape[0]
            apart = rows // length != lax.broadcasted_iota(I32, scores.shape, 1) // length
            scores = jnp.where(apart, FAR, scores)
        probs = softmax(scores).astype(B16)
        keep_probs(t, probs)
        parts.append(diagonal(dot(probs, v[:, at]), group))
    return jnp.concatenate(parts, 1).astype(B16)


def attend_back(q, k, v, d_att, group, probs_of):
    wide = HS * group
    dq, dk, dv = [], [], []
    for t in range(HEADS // group):
        at = slice(t * wide, (t + 1) * wide)
        probs = probs_of(t)
        d_stack = stacked(d_att[:, at], group)
        d_probs = dot_nt(d_stack, v[:, at])
        dv.append(dot_tn(probs, d_stack))
        p32 = probs.astype(F32)
        inside = jnp.sum(p32 * d_probs, -1, keepdims=True)
        d_scores = (p32 * (d_probs - inside)).astype(B16)
        dq.append(diagonal(dot(d_scores, k[:, at]), group) * SCALE)
        dk.append(dot_tn(d_scores, stacked(q[:, at], group)))
    return tuple(jnp.concatenate(x, 1).astype(B16) for x in (dq, dk, dv))


def feed(first, w_up, b_up, w_down, b_down, gain, shift, keep, tile=512):
    hat, r = centred(first)
    normed = hat * gain + shift
    low = normed.astype(B16)
    second = normed + b_down
    for j in range(w_up.shape[1] // tile):
        at = slice(j * tile, (j + 1) * tile)
        act, slope = gelu_pair(dot(low, w_up[:, at]) + b_up[:, at])
        act = act.astype(B16)
        keep(at, act, slope)
        second = second + dot(act, w_down[at, :])
    return second, hat, r, low


def feed_both(first, w_up, b_up, w_down, b_down, g1, s1, g2, s2, d_out, slopes, keep_act, keep_inner):
    def keep(at, act, slope):
        keep_act(at, act)
        slopes[:, at] = slope

    ff = w_up.shape[1]
    second, hat, r, low = feed(first, w_up, b_up, w_down, b_down, g1, s1, keep, ff)
    hat2, r2 = centred(second)
    out = (hat2 * g2 + s2).astype(B16)
    d_second, gg2, gs2 = norm_back(hat2, r2, g2, d_out)
    d_down = d_second.astype(B16)
    gb_down = jnp.sum(d_down.astype(F32), 0, keepdims=True)
    d = (dot_nt(d_down, w_down[...]) * slopes[...]).astype(B16)
    keep_inner(slice(0, ff), d)
    gb_up = jnp.sum(d.astype(F32), 0, keepdims=True)
    gb_up = [gb_up[:, j * 512 : (j + 1) * 512] for j in range(ff // 512)]
    d_normed = d_second + dot_nt(d, w_up[...])
    d_first, gg1, gs1 = norm_back(hat, r, g1, d_normed)
    return out, d_down, d_first, low, (gg1, gs1, gb_down, gg2, gs2, *gb_up)


def cls_rows(q, k, v, count):
    total, width = q.shape
    length = total // count
    rows = count * HEADS
    own = (
        lax.broadcasted_iota(I32, (rows, width), 1) // HS
        == lax.broadcasted_iota(I32, (rows, width), 0) % HEADS
    )
    first = [
        jnp.broadcast_to(q[i * length : i * length + 1, :].astype(F32), (HEADS, width))
        for i in range(count)
    ]
    q_rows = jnp.where(own, jnp.concatenate(first, 0), 0.0).astype(B16)
    scores = dot_nt(q_rows, k[...])
    apart = (
        lax.broadcasted_iota(I32, scores.shape, 0) // HEADS
        != lax.broadcasted_iota(I32, scores.shape, 1) // length
    )
    probs = softmax(jnp.where(apart, FAR, scores)).astype(B16)
    mixed = jnp.where(own, dot(probs, v[...]), 0.0)
    return jnp.concatenate(
        [
            jnp.sum(mixed[i * HEADS : (i + 1) * HEADS], 0, keepdims=True)
            for i in range(count)
        ],
        0,
    )


def row(ref, e):
    return ref[e : e + 1, :]


def front_kernel(
    positives, counts, bq, bv, bo, g1, s1, bu, bd, g2, s2, p_x, q_x, wq, wk, wv, wo, wu, wd,
    pq, pk, pv, qq, qk, qv, payload,
    p_s, q_s, wqkv_s, wo_s, wu_s, wd_s, p_out, q_out, pay_s, sems, out_sems,
):
    width = q_x.shape[1]
    count = 4

    def load(i, src, dst):
        return pltpu.make_async_copy(src, dst, sems.at[i])

    w_in = (wq, wk, wv)
    first_in = [load(0, p_x, p_s)]
    first_in += [load(1 + i, w.at[1], wqkv_s.at[1, i]) for i, w in enumerate(w_in)]
    q_in = [load(4, q_x, q_s)]
    q_in += [load(5 + i, w.at[0], wqkv_s.at[0, i]) for i, w in enumerate(w_in)]
    later = [load(8, wo, wo_s), load(9, wu, wu_s), load(10, wd, wd_s)]
    for c in first_in + q_in + later:
        c.start()

    def project(x, e, held, targets):
        copies = []
        for i, (bias, target) in enumerate(zip((bq, None, bv), targets)):
            y = dot(x[...], wqkv_s[e, i])
            y = (y if bias is None else y + row(bias, e)).astype(B16)
            held[i] = y * SCALE if i == 0 else y
            copies.append(pltpu.make_async_copy(held.at[i], target, out_sems.at[3 * e + i]))
            copies[-1].start()
        return copies

    for c in first_in:
        c.wait()
    out = project(p_s, 1, p_out, (pq, pk, pv))
    for c in q_in:
        c.wait()
    out += project(q_s, 0, q_out, (qq, qk, qv))

    pay_s[...] = jnp.zeros_like(pay_s)
    lanes = lax.broadcasted_iota(I32, (1, width), 1)
    for i in range(count):
        mask = jnp.zeros((1, width), F32)
        for j in range(positives.shape[1]):
            mask = jnp.where((lanes == positives[i, j]) & (j < counts[i]), 1.0, mask)
        pay_s[8 + i : 9 + i, :] = mask
    att = [cls_rows(held.at[0], held.at[1], held.at[2], count) for held in (p_out, q_out)]
    for c in later:
        c.wait()
    for e, start, mixed, x in ((1, 0, att[0], p_s), (0, 4, att[1], q_s)):
        length = x.shape[0] // count
        own = [x[i * length : i * length + 1, :].astype(F32) for i in range(count)]
        zero = [jnp.zeros((4, width), F32)]
        mixed = jnp.concatenate([mixed] + zero, 0).astype(B16)
        first = jnp.concatenate(own + zero, 0) + dot(mixed, wo_s[e]) + row(bo, e)
        second, _, _, _ = feed(
            first, wu_s.at[e], row(bu, e), wd_s.at[e], row(bd, e), row(g1, e), row(s1, e),
            lambda at, act, slope: None, 2048,
        )
        done = centred(second)[0] * row(g2, e) + row(s2, e)
        pay_s[start : start + 4, :] = done[:4]
    payload[...] = pay_s[...].astype(B16)
    for c in out:
        c.wait()


def passage_attention_kernel(q, k, v, x, bo, wo, probs, att, first, wo_s, sem):
    copy = pltpu.make_async_copy(wo.at[1], wo_s, sem)

    @pl.when(pl.program_id(0) == 0)
    def _():
        copy.start()

    def keep_probs(t, value):
        probs[t] = value

    a = attend(q[...], k[...], v[...], 4, keep_probs)
    att[...] = a

    @pl.when(pl.program_id(0) == 0)
    def _():
        copy.wait()

    first[...] = x[...].astype(F32) + dot(a, wo_s[...]) + row(bo, 1)


def question_attention_kernel(length, q, k, v, x, bo, wo, probs, att, first):
    def keep_probs(t, value):
        probs[t] = value

    a = attend(q[...], k[...], v[...], 4, keep_probs, length)
    att[...] = a
    first[...] = x[...].astype(F32) + dot(a, wo[...]) + row(bo, 0)


def send_unit(wide, grads, table, keep, send, offset, sem_keep, sem_send):
    half, _, width = keep.shape
    blocks = 2 * half
    rows = grads.shape[0] * grads.shape[1] // (width * blocks)
    across = grads.shape[1] // width

    def start(out, base, sem):
        def body(r, carry):
            c = table[base + r]
            src = grads.at[
                pl.ds(pl.multiple_of(c // across * rows, rows), rows),
                pl.ds(pl.multiple_of(c % across * width, width), width),
            ] if wide else grads.at[pl.ds(pl.multiple_of(c * rows, rows), rows), :]
            pltpu.make_async_copy(src, out.at[r, pl.ds(offset, rows), :], sem).start()
            return carry

        lax.fori_loop(0, half, body, 0)

    start(send, half, sem_send)
    start(keep, 0, sem_keep)


def wait_units(keep, send, sem_keep, sem_send):
    pltpu.make_async_copy(send, send, sem_send).wait()
    pltpu.make_async_copy(keep, keep, sem_keep).wait()


def contrast(gathered, me, scale):
    z = jnp.concatenate([g[...] for g in gathered], 0)
    n = z.shape[0] // 16
    total_rows = 4 * n
    base = me * 4
    place = lax.broadcasted_iota(I32, (total_rows, z.shape[0]), 1)
    index = lax.broadcasted_iota(I32, (total_rows, z.shape[0]), 0)
    apart = (index // 4) ^ me
    block = jnp.zeros_like(apart)
    depth = n.bit_length() - 1
    for i in range(depth):
        block = block + (((apart >> i) & 1) << (depth - 1 - i))
    sel = block * 16 + index % 4

    def rows_at(k):
        return dot(jnp.where(place == sel + k, 1.0, 0.0).astype(B16), z)

    all_p, all_q, mask = rows_at(0), rows_at(4), rows_at(8)[:, :total_rows]
    sim = dot_nt(all_q.astype(B16), all_p.astype(B16)) * scale
    expo = jnp.exp(sim - jnp.max(sim, -1, keepdims=True))
    total = jnp.sum(expo, -1, keepdims=True)
    hit = mask * expo
    pos_total = jnp.sum(hit, -1, keepdims=True)
    terms = jnp.log(total) - jnp.log(pos_total)
    coeff = expo / total - hit / pos_total
    mine = jnp.where(
        lax.broadcasted_iota(I32, (8, total_rows), 1)
        == base + lax.broadcasted_iota(I32, (8, total_rows), 0),
        1.0,
        0.0,
    )
    d_q = dot_high(dot_high(mine, coeff), all_p) * scale
    d_p = dot_high(dot_high(mine, coeff.T), all_q) * scale
    return dot_high(mine, jnp.broadcast_to(terms, (total_rows, 128))), d_q, d_p


def question_back_kernel(
    table, gathered_a, gathered_b, x, cot, q, k, v, probs, att, first,
    g1, s1, bu, bd, g2, s2, wq, wk, wv, wo, wu, wd,
    terms, d_cls_p, x_grad, small, out, keep, send,
    wqkv_s, wo_s, wu_s, wd_s, act_s, slope_s, inner_s, g_down, g_up, g_att, sems, out_sems,
):
    copies = [
        pltpu.make_async_copy(src.at[0], dst, sems.at[i])
        for i, (src, dst) in enumerate(
            (
                (wu, wu_s),
                (wd, wd_s),
                (wo, wo_s),
                (wq, wqkv_s.at[0]),
                (wk, wqkv_s.at[1]),
                (wv, wqkv_s.at[2]),
            )
        )
    ]
    for c in copies:
        c.start()
    n = keep.shape[0] * 2
    rows = 2048 // n
    count = 4
    length = x.shape[0] // count
    width = x.shape[1]
    loss, d_q, d_p = contrast(
        (gathered_a, gathered_b), table[n], 2.0 / float(np.sqrt(width))
    )
    terms[...] = loss
    d_cls_p[...] = d_p
    place = lax.broadcasted_iota(I32, x.shape, 0)
    d_out = cot[...].astype(F32)
    for i in range(count):
        d_out = d_out + jnp.where(place == i * length, d_q[i : i + 1], 0.0)
    for c in copies[:2]:
        c.wait()

    def keep_act(at, value):
        act_s[:, at] = value

    def keep_inner(at, value):
        inner_s[:, at] = value

    out[...], d_down, d_first, low, sums = feed_both(
        first[...], wu_s, row(bu, 0), wd_s, row(bd, 0), row(g1, 0), row(s1, 0), row(g2, 0),
        row(s2, 0), d_out, slope_s, keep_act, keep_inner,
    )
    sems_out = (out_sems.at[0], out_sems.at[1])
    g_down[...] = dot_tn(act_s[...], d_down).astype(B16)
    send_unit(False, g_down, table, keep, send, 0, *sems_out)
    g_up[...] = dot_tn(low, inner_s[...]).astype(B16)
    send_unit(True, g_up, table, keep, send, rows, *sems_out)
    for c in copies[2:]:
        c.wait()
    d_branch = d_first.astype(B16)
    d_att = dot_nt(d_branch, wo_s[...]).astype(B16)
    dq, dk, dv = attend_back(q[...], k[...], v[...], d_att, 4, lambda t: probs[t])
    rows_x = x[...]
    for i, d in enumerate((dq, dk, dv)):
        g_att[i * width : (i + 1) * width, :] = dot_tn(rows_x, d).astype(B16)
    g_att[3 * width :, :] = dot_tn(att[...], d_branch).astype(B16)
    send_unit(False, g_att, table, keep, send, 2 * rows, *sems_out)
    x_grad[...] = (
        d_first + dot_nt(dq, wqkv_s[0]) + dot_nt(dk, wqkv_s[1]) + dot_nt(dv, wqkv_s[2])
    )
    small[...] = jnp.zeros_like(small)
    values = [jnp.sum(d.astype(F32), 0, keepdims=True) for d in (dq, dv, d_branch)]
    for i, value in enumerate((*values, *sums)):
        small[i : i + 1, :] = value
    wait_units(keep, send, *sems_out)


def passage_feed_kernel(
    steps, table, d_cls, cot, first, g1, s1, bu, bd, g2, s2, wu, wd,
    out, d_first, small, keep, send,
    wu_s, wd_s, slope_s, act_s, inner_s, down_s, low_s, g_down, g_up, sems, out_sems,
):
    b = pl.program_id(0)
    sems_out = (out_sems.at[0], out_sems.at[1])
    rows = 2048 // (2 * keep.shape[0])
    total_rows = act_s.shape[0]
    per = 4 // steps

    @pl.when(b < steps)
    def _():
        copies = [
            pltpu.make_async_copy(src, dst, sems.at[i])
            for i, (src, dst) in enumerate(((wu.at[1], wu_s), (wd.at[1], wd_s)))
        ]

        @pl.when(b == 0)
        def _():
            for c in copies:
                c.start()
            small[...] = jnp.zeros_like(small)
            for c in copies:
                c.wait()

        place = lax.broadcasted_iota(I32, cot.shape, 0)
        d_out = cot[...].astype(F32)
        for i in range(per):
            mine = d_cls[pl.ds(b * per + i, 1), :]
            d_out = d_out + jnp.where(place == i * (cot.shape[0] // per), mine, 0.0)
        mine = pl.ds(pl.multiple_of(b * cot.shape[0], cot.shape[0]), cot.shape[0])

        def keep_act(at, value):
            act_s[mine, at] = value

        def keep_inner(at, value):
            inner_s[mine, at] = value

        out[...], down_s[mine, :], d_first[...], low_s[mine, :], sums = feed_both(
            first[...], wu_s, row(bu, 1), wd_s, row(bd, 1), row(g1, 1), row(s1, 1), row(g2, 1),
            row(s2, 1), d_out, slope_s, keep_act, keep_inner,
        )
        for i, value in enumerate(sums):
            small[3 + i : 4 + i, :] += value

    @pl.when(b == steps)
    def _():
        g_down[...] = dot_tn(act_s[...], down_s[...]).astype(B16)
        send_unit(False, g_down, table, keep, send, 0, *sems_out)

    @pl.when(b == steps + 1)
    def _():
        g_up[...] = dot_tn(low_s[...], inner_s[...]).astype(B16)
        send_unit(True, g_up, table, keep, send, rows, *sems_out)
        wait_units(keep, send, *sems_out)


def passage_attention_back_kernel(
    table, small_q, small_p, d_first, q, k, v, probs, x, att, wq, wk, wv, wo,
    x_grad, keep, send,
    wqkv_s, wo_s, x_s, att_s, d_s, small, sent_s, g_att, sems, out_sems,
):
    b = pl.program_id(0)
    nb = pl.num_programs(0)
    length, width = d_first.shape
    n = 2 * keep.shape[0]
    rows = 2048 // n
    copies = [
        pltpu.make_async_copy(src, dst, sems.at[i])
        for i, (src, dst) in enumerate(
            (
                (wo.at[1], wo_s),
                (wq.at[1], wqkv_s.at[0]),
                (wk.at[1], wqkv_s.at[1]),
                (wv.at[1], wqkv_s.at[2]),
                (x, x_s),
                (att, att_s),
            )
        )
    ]

    @pl.when(b == 0)
    def _():
        for c in copies:
            c.start()
        small[...] = small_p[...]
        for c in copies[:4]:
            c.wait()

    d_branch = d_first[...].astype(B16)
    d_att = dot_nt(d_branch, wo_s[...]).astype(B16)
    dq, dk, dv = attend_back(q[...], k[...], v[...], d_att, 4, lambda t: probs[t])
    mine = pl.ds(pl.multiple_of(b * length, length), length)
    for i, d in enumerate((dq, dk, dv, d_branch)):
        d_s[i, mine, :] = d
    for i, d in enumerate((dq, dv, d_branch)):
        small[i : i + 1, :] += jnp.sum(d.astype(F32), 0, keepdims=True)
    x_grad[...] = (
        d_first[...] + dot_nt(dq, wqkv_s[0]) + dot_nt(dk, wqkv_s[1]) + dot_nt(dv, wqkv_s[2])
    )

    @pl.when(b == nb - 1)
    def _():
        sent_s[...] = jnp.zeros_like(sent_s)
        top = lax.broadcasted_iota(I32, (16, width), 0) == 0
        for e, ref in enumerate((small_q, small)):
            for i in range(NSMALL):
                sent_s[e * NSMALL + i] = jnp.where(top, ref[i : i + 1, :], 0.0).astype(B16)
        for base, out, sem in ((n // 2, send, out_sems.at[1]), (0, keep, out_sems.at[0])):

            def body(r, carry, base=base, out=out, sem=sem):
                pltpu.make_async_copy(
                    sent_s.at[table[base + r]], out.at[r, pl.ds(rows, 16), :], sem
                ).start()
                return carry

            lax.fori_loop(0, n // 2, body, 0)
        for c in copies[4:]:
            c.wait()
        for i in range(3):
            g_att[i * width : (i + 1) * width, :] = dot_tn(x_s[...], d_s[i]).astype(B16)
        g_att[3 * width :, :] = dot_tn(att_s[...], d_s[3]).astype(B16)
        send_unit(False, g_att, table, keep, send, 0, out_sems.at[0], out_sems.at[1])
        wait_units(keep, send, out_sems.at[0], out_sems.at[1])


def place_kernel(e, kinds, starts, n_alias, with_small, *refs):
    table = refs[0]
    pieces = refs[1 : 1 + len(starts)]
    outs = refs[1 + len(starts) + n_alias :]
    n_out = sum(4 if kind == "att" else 1 for kind in kinds)
    n_small = 9 if with_small else 0
    targets, smalls = outs[:n_out], outs[n_out : n_out + n_small]
    scratch = outs[n_out + n_small :]
    stages, sems = scratch[: len(kinds)], scratch[len(kinds)]
    small_s = scratch[len(kinds) + 1] if with_small else None
    n = starts[-1] + pieces[-1].shape[0]
    rows = 2048 // n
    for piece, start in zip(pieces, starts):

        def body(r, carry, piece=piece, start=start):
            c = table[start + r]
            k = 0
            for u, kind in enumerate(kinds):
                stage = stages[u].at[start + r]
                stage[...] = piece[r, u * rows : (u + 1) * rows, :].astype(F32)
                if kind == "down":
                    pltpu.make_async_copy(
                        stage,
                        targets[k].at[e, pl.ds(pl.multiple_of(c * rows, rows), rows), :],
                        sems.at[k],
                    ).start()
                    k += 1
                elif kind == "up":
                    pltpu.make_async_copy(
                        stage,
                        targets[k].at[
                            e,
                            pl.ds(pl.multiple_of(c // 4 * rows, rows), rows),
                            pl.ds(pl.multiple_of(c % 4 * 512, 512), 512),
                        ],
                        sems.at[k],
                    ).start()
                    k += 1
                else:
                    quarter = n // 4
                    for m in range(4):

                        @pl.when(c // quarter == m)
                        def _(m=m, k=k, stage=stage):
                            at = pl.ds(pl.multiple_of(c % quarter * rows, rows), rows)
                            pltpu.make_async_copy(
                                stage, targets[k + m].at[e, at, :], sems.at[k + m]
                            ).start()

                    k += 4
            if with_small:
                block = piece[r, len(kinds) * rows : len(kinds) * rows + 16, :].astype(F32)
                small_s[c] = block[0:8]
            return carry

        lax.fori_loop(0, piece.shape[0], body, 0)
    if with_small:
        for f in range(2):
            for i in range(8):
                smalls[i][f : f + 1, :] = small_s[f * NSMALL + i, 0:1, :]
            for j in range(4):
                smalls[8][f : f + 1, j * 512 : (j + 1) * 512] = small_s[f * NSMALL + 8 + j, 0:1, :]
    for k, target in enumerate(targets):
        pltpu.make_async_copy(target.at[e], target.at[e], sems.at[k]).wait()


def rounds_of(mesh_shape):
    dp, rep = mesh_shape["dp"], mesh_shape["rep"]
    core, *x = [1 << i for i in range(rep.bit_length() - 1)]
    y, *z = [rep << i for i in range(dp.bit_length() - 1)]
    return [core, *x, y, *z], [core, y, *x, *z]


def order_table(rounds, n):
    depth = len(rounds[0])
    table = np.zeros((n, n), np.int32)
    for d in range(n):
        for r in range(n):
            c = d ^ (rounds[0][0] if r >> (depth - 1) & 1 else 0)
            for k in range(1, depth):
                if r >> (depth - 1 - k) & 1:
                    c ^= rounds[c & 1][k]
            table[d, r] = c
    return table


def exchange(x, masks, n):
    return lax.ppermute(x, AXES, [(d, d ^ masks[d & 1]) for d in range(n)])


def total(parts):
    return sum(p.astype(F32) for p in parts).astype(B16)


def steps_of(rounds, pairs):
    even, odd = rounds
    steps, k = [], 0
    while k < len(even):
        if even[k] in pairs:
            steps.append(((even[k], odd[k]), (even[k + 1], odd[k + 1])))
            k += 2
        else:
            steps.append(((even[k], odd[k]),))
            k += 1
    return steps


def partners(step):
    if len(step) == 1:
        return [step[0]]
    high, low = step
    return [low, high, (low[0] ^ high[0], low[1] ^ high[1])]


def join_kernel(*refs):
    *parts, out = refs
    m = parts[0].shape[0]
    for i, part in enumerate(parts):
        out[i * m : (i + 1) * m] = part[...]


class Order:
    def __init__(self):
        self.token = None

    def fence(self, arrays):
        *arrays, self.token = lax.optimization_barrier((*arrays, self.token))
        return arrays

    def __call__(self, kernel, *operands, in_specs, out_specs, out_shape, **kwargs):
        skip = 0 if self.token is None else 1
        last = skip + len(operands) + len(out_shape)

        def body(*refs):
            kernel(*refs[skip:last], *refs[last + 1 :])

        aliases = kwargs.pop("input_output_aliases", {})
        call = pl.pallas_call(
            body,
            in_specs=[ANY] * skip + in_specs,
            out_specs=list(out_specs) + [ANY],
            out_shape=list(out_shape) + [shape((8, 128))],
            input_output_aliases={k + skip: v for k, v in aliases.items()},
            **kwargs,
        )
        *outs, self.token = call(*([self.token] if skip else []), *operands)
        return outs


class Sum:
    def __init__(self, order, halving, doubling, n, keep, send):
        self.order, self.n = order, n
        self.halving, self.doubling = list(halving), list(doubling)
        self.parts, self.m, self.pieces = [keep], keep.shape[0], None
        self.got, self.out, self.now = None, [send], self.halving.pop(0)

    def start(self):
        masks = partners(self.now)
        if self.pieces is None:
            self.got = [exchange(x, m, self.n) for x, m in zip(self.out, masks)]
        else:
            self.got = [exchange(x, m, self.n) for m in masks for x in self.out]

    def take(self):
        if self.pieces is None:
            self.parts += self.got
            if self.halving:
                self.now = self.halving.pop(0)
                ways = 2 ** len(self.now)
                q = self.m // ways
                self.out = [
                    total([p[i * q : (i + 1) * q] for p in self.parts]) for i in range(1, ways)
                ]
                self.m = q
                return True
            self.out = self.pieces = [total([p[:1] for p in self.parts])]
        else:
            self.pieces = self.pieces + self.got
            if not self.doubling:
                return False
            if len(self.doubling) > 1:
                self.pieces = [jnp.concatenate(self.pieces, 0)]
            self.out = self.pieces
        self.now = self.doubling.pop()
        return True


def tail_order(sums, ready):
    unit, x_y, z = 23.3, "xy", "z"

    def durations(item, units):
        left = []
        size = item.m / item.n
        for step in item.halving:
            size /= 2 ** len(step)
            left.append((z, 4 * size) if len(step) == 2 else (x_y, size))
        size = 1 / item.n
        for step in reversed(item.doubling):
            left.append((z, 4 * size) if len(step) == 2 else (x_y, size))
            size *= 2 ** len(step)
        left[-1] = ("core", left[-1][1] / 3)
        return [(kind, d * units * unit) for kind, d in left]

    todo = {k: durations(*v) for k, v in sums.items()}
    done_at = dict(ready)
    busy = {x_y: 0.0, z: 0.0, "core": 0.0}
    now, order = 0.0, []
    going = set(todo)
    while going:
        here = [k for k in going if done_at[k] <= now]
        if not here:
            now = min(done_at[k] for k in going)
            continue
        k = max(here, key=lambda k: sum(d for _, d in todo[k]) + 3 * len(todo[k]))
        order.append(k)
        if not todo[k]:
            going.remove(k)
            continue
        kind, d = todo[k].pop(0)
        now += 5.0 if kind == z else 3.0
        start = max(now, busy[kind])
        busy[kind] = done_at[k] = start + d
    return order


def advance(order, sums, starting=()):
    flat = [x for s in sums for x in s.got]
    if flat:
        flat = order.fence(flat)
    for s in sums:
        s.got, flat = flat[: len(s.got)], flat[len(s.got) :]
    for s in sums:
        s.going = s.take()
    going = [s for s in sums if s.going] + list(starting)
    if not going:
        return
    flat = order.fence([x for s in going for x in s.out])
    for s in going:
        s.out, flat = flat[: len(s.out)], flat[len(s.out) :]
        if s.pieces is not None:
            s.pieces = s.out
        s.start()


class Gather:
    def __init__(self, order, x, n):
        bits = [1 << i for i in reversed(range(n.bit_length() - 1))]
        assert len(bits) % 2 == 1
        self.order, self.n = order, n
        self.stages = [bits[i : i + 2] for i in range(0, len(bits), 2)]
        self.pieces = [x[None]]
        self.issue()

    def issue(self):
        (mine,) = self.order.fence(self.pieces)
        now = self.stages.pop(0)
        masks = now if len(now) == 1 else [now[0], now[1], now[0] | now[1]]
        self.pieces = [mine] + [
            lax.ppermute(mine, AXES, [(d, d ^ m) for d in range(self.n)]) for m in masks
        ]

    def step(self):
        m, rows, width = self.pieces[0].shape
        count = len(self.pieces)
        self.pieces = self.order(
            join_kernel,
            *self.order.fence(self.pieces),
            name="join",
            in_specs=[VMEM] * count,
            out_specs=[VMEM],
            out_shape=[shape((count * m, rows, width), B16)],
            compiler_params=params(62),
            cost_estimate=SHORT,
        )
        self.issue()

    def result(self):
        return self.order.fence(self.pieces)


def params(limit):
    return pltpu.CompilerParams(vmem_limit_bytes=limit * MIB)


LONG = pl.CostEstimate(flops=200_000_000_000, bytes_accessed=1000, transcendentals=0)


SHORT = pl.CostEstimate(flops=1000, bytes_accessed=1000, transcendentals=0)


def shape(dims, dtype=F32):
    return jax.ShapeDtypeStruct(dims, dtype)


def sem(count):
    return pltpu.SemaphoreType.DMA((count,))


def shards(
    mesh_shape,
    q_tokens,
    p_tokens,
    q_cotangent,
    p_cotangent,
    positives,
    counts,
    wq,
    bq,
    wk,
    wv,
    bv,
    wo,
    bo,
    g1,
    s1,
    wu,
    bu,
    wd,
    bd,
    g2,
    s2,
):
    n = mesh_shape["dp"] * mesh_shape["rep"]
    plane = rounds_of(mesh_shape)
    pairs = plane[0][-2:-1]
    me = lax.axis_index("dp") * mesh_shape["rep"] + lax.axis_index("rep")
    tables = np.concatenate([order_table(plane, n), np.arange(n, dtype=np.int32)[:, None]], 1)
    table = lax.dynamic_index_in_dim(jnp.asarray(tables), me, 0, False)
    qn, ql, h = q_tokens.shape
    pn, plen, _ = p_tokens.shape
    ff = wu.shape[2]
    qr, pr = qn * ql, pn * plen
    assert qn == 4 and pn == 4 and h == 512 and ff == 2048 and 24 <= n and 4 * n <= h
    q_x, p_x = q_tokens.reshape(qr, h), p_tokens.reshape(pr, h)
    q_cot, p_cot = q_cotangent.reshape(qr, h), p_cotangent.reshape(pr, h)
    order = Order()

    def whole(*dims):
        return pl.BlockSpec(dims, lambda b: (0,) * len(dims))

    one, wide = whole(2, h), whole(2, ff)
    seq_block = pl.BlockSpec((plen, h), lambda b: (b, 0))
    pq, pk, pv, qq, qk, qv, payload = order(
        front_kernel,
        positives, counts, bq, bv, bo, g1, s1, bu, bd, g2, s2, p_x, q_x, wq, wk, wv, wo, wu, wd,
        name="front",
        in_specs=[SMEM] * 2 + [VMEM] * 9 + [ANY] * 8,
        out_specs=[ANY] * 6 + [VMEM],
        out_shape=[shape((pr, h), B16)] * 3 + [shape((qr, h), B16)] * 3 + [shape((16, h), B16)],
        scratch_shapes=[
            pltpu.VMEM((pr, h), B16),
            pltpu.VMEM((qr, h), B16),
            pltpu.VMEM((2, 3, h, h), B16),
            pltpu.VMEM((2, h, h), B16),
            pltpu.VMEM((2, h, ff), B16),
            pltpu.VMEM((2, ff, h), B16),
            pltpu.VMEM((3, pr, h), B16),
            pltpu.VMEM((3, qr, h), B16),
            pltpu.VMEM((16, h), F32),
            sem(11),
            sem(6),
        ],
        compiler_params=params(62),
        cost_estimate=LONG,
    )
    gather = Gather(order, payload, n)

    def passages(kernel, name, at, count, operands, in_specs, outs, before, **kwargs):
        def spec(block):
            if not isinstance(block, tuple):
                return block
            axis = block.index(None) if None in block else len(block) - 2
            return pl.BlockSpec(
                block, lambda b: tuple(b + at if i == axis else 0 for i in range(len(block)))
            )

        n_in, n_before = len(operands), len(before)

        def body(*refs):
            kernel(*refs[:n_in], *refs[n_in + n_before :])

        return order(
            body,
            *operands,
            *before,
            name=name,
            grid=(count,),
            in_specs=[spec(x) for x in in_specs] + [ANY] * n_before,
            out_specs=[spec(block) for block, _ in outs],
            out_shape=[s for _, s in outs],
            input_output_aliases={n_in + i: i for i in range(n_before)},
            compiler_params=params(62),
            cost_estimate=LONG,
            **kwargs,
        )

    seq, seq_wide = (plen, h), (plen, ff)
    probs_block = (None, 2, 4 * plen, plen)

    def attention(at, count, before):
        return passages(
            passage_attention_kernel, "passage_attention", at, count,
            (pq, pk, pv, p_x, bo, wo),
            [seq] * 4 + [one, ANY],
            [
                (probs_block, shape((pn, 2, 4 * plen, plen), B16)),
                (seq, shape((pr, h), B16)),
                (seq, shape((pr, h))),
            ],
            before,
            scratch_shapes=[pltpu.VMEM((h, h), B16), pltpu.SemaphoreType.DMA],
        )

    part = attention(0, 2, [])
    gather.step()
    q_probs, q_att, q_first = order(
        functools.partial(question_attention_kernel, ql),
        qq, qk, qv, q_x, bo, wo,
        name="question_attention",
        grid=(1,),
        in_specs=[whole(qr, h)] * 4 + [one, pl.BlockSpec((None, h, h), lambda b: (0, 0, 0))],
        out_specs=[whole(2, 4 * qr, qr), whole(qr, h), whole(qr, h)],
        out_shape=[shape((2, 4 * qr, qr), B16), shape((qr, h), B16), shape((qr, h))],
        compiler_params=params(62),
        cost_estimate=LONG,
    )
    while gather.stages:
        gather.step()
    gathered = [x.reshape(-1, h) for x in gather.result()]

    rows = 2048 // n
    half = n // 2
    terms, d_cls_p, q_grad, small_q, q_out, q_keep, q_send = order(
        question_back_kernel,
        table, *gathered, q_x, q_cot, qq, qk, qv, q_probs, q_att, q_first,
        g1, s1, bu, bd, g2, s2, wq, wk, wv, wo, wu, wd,
        name="question_back",
        in_specs=[SMEM] + [VMEM] * 16 + [ANY] * 6,
        out_specs=[VMEM] * 5 + [ANY] * 2,
        out_shape=[
            shape((8, 128)),
            shape((8, h)),
            shape((qr, h)),
            shape((16, h)),
            shape((qr, h), B16),
            shape((half, 3 * rows, h), B16),
            shape((half, 3 * rows, h), B16),
        ],
        scratch_shapes=[
            pltpu.VMEM((3, h, h), B16),
            pltpu.VMEM((h, h), B16),
            pltpu.VMEM((h, ff), B16),
            pltpu.VMEM((ff, h), B16),
            pltpu.VMEM((qr, ff), B16),
            pltpu.VMEM((qr, ff), F32),
            pltpu.VMEM((qr, ff), B16),
            pltpu.VMEM((ff, h), B16),
            pltpu.VMEM((h, ff), B16),
            pltpu.VMEM((4 * h, h), B16),
            sem(6),
            sem(2),
        ],
        compiler_params=params(62),
        cost_estimate=LONG,
    )
    steps = steps_of(plane, pairs)
    q_sum = Sum(order, steps, steps, n, q_keep, q_send)
    advance(order, [], [q_sum])
    p_probs, p_att, p_first = attention(2, 2, part)
    advance(order, [q_sum])

    parts_of = 2
    two = (pr // parts_of, h)

    def rows_at(width):
        return pl.BlockSpec((pr // parts_of, width), lambda b: (jnp.minimum(b, parts_of - 1), 0))

    p_out, d_first, small_p, f_keep, f_send = order(
        functools.partial(passage_feed_kernel, parts_of),
        table, d_cls_p, p_cot, p_first, g1, s1, bu, bd, g2, s2, wu, wd,
        name="passage_feed",
        grid=(parts_of + 2,),
        in_specs=[SMEM, whole(8, h), rows_at(h), rows_at(h), one, one, wide, one, one, one, ANY, ANY],
        out_specs=[rows_at(h), rows_at(h), whole(16, h), ANY, ANY],
        out_shape=[shape((pr, h), B16), shape((pr, h)), shape((16, h))]
        + [shape((half, 2 * rows, h), B16)] * 2,
        scratch_shapes=[
            pltpu.VMEM((h, ff), B16),
            pltpu.VMEM((ff, h), B16),
            pltpu.VMEM((pr // parts_of, ff), F32),
            pltpu.VMEM((pr, ff), B16),
            pltpu.VMEM((pr, ff), B16),
            pltpu.VMEM((pr, h), B16),
            pltpu.VMEM((pr, h), B16),
            pltpu.VMEM((ff, h), B16),
            pltpu.VMEM((h, ff), B16),
            sem(2),
            sem(2),
        ],
        compiler_params=params(62),
        cost_estimate=LONG,
    )
    f_sum = Sum(order, steps, steps, n, f_keep, f_send)
    advance(order, [q_sum], [f_sum])
    p_grad, a_keep, a_send = order(
        passage_attention_back_kernel,
        table, small_q, small_p, d_first, pq, pk, pv, p_probs, p_x, p_att, wq, wk, wv, wo,
        name="passage_attention_back",
        grid=(pn,),
        in_specs=[SMEM, whole(16, h), whole(16, h)] + [seq_block] * 4
        + [pl.BlockSpec(probs_block, lambda b: (b, 0, 0, 0))] + [ANY] * 6,
        out_specs=[seq_block, ANY, ANY],
        out_shape=[shape((pr, h))] + [shape((half, rows + 16, h), B16)] * 2,
        scratch_shapes=[
            pltpu.VMEM((3, h, h), B16),
            pltpu.VMEM((h, h), B16),
            pltpu.VMEM((pr, h), B16),
            pltpu.VMEM((pr, h), B16),
            pltpu.VMEM((4, pr, h), B16),
            pltpu.VMEM((16, h), F32),
            pltpu.VMEM((n, 16, h), B16),
            pltpu.VMEM((4 * h, h), B16),
            sem(6),
            sem(2),
        ],
        compiler_params=params(62),
        cost_estimate=LONG,
    )
    a_sum = Sum(order, steps, steps, n, a_keep, a_send)
    advance(order, [q_sum, f_sum], [a_sum])

    def place(e, kinds, which, before, with_small):
        pieces = which.pieces
        starts, at = [], 0
        for piece in pieces:
            starts.append(at)
            at += piece.shape[0]
        dims = []
        for kind in kinds:
            dims += {"down": [(2, ff, h)], "up": [(2, h, ff)], "att": [(2, h, h)] * 4}[kind]
        outs = [shape(d) for d in dims]
        smalls = [shape((2, h))] * 8 + [shape((2, ff))] if with_small else []
        return order(
            functools.partial(
                place_kernel, e, kinds, tuple(starts), len(before), with_small
            ),
            table, *pieces, *before,
            name="place",
            in_specs=[SMEM] + [VMEM] * len(pieces) + [ANY] * len(before),
            out_specs=[ANY] * len(outs) + [VMEM] * len(smalls),
            out_shape=outs + smalls,
            input_output_aliases={1 + len(pieces) + i: i for i in range(len(before))},
            scratch_shapes=[pltpu.VMEM((n, rows, h), F32) for _ in kinds]
            + [sem(len(outs))]
            + ([pltpu.VMEM((n, 8, h), F32)] if with_small else []),
            compiler_params=params(40),
            cost_estimate=SHORT,
        )

    for name in tail_order(
        {"q": (q_sum, 3), "f": (f_sum, 2), "a": (a_sum, 1.25)}, {"q": 10.0, "f": 10.0, "a": 12.0}
    ):
        advance(order, [{"q": q_sum, "f": f_sum, "a": a_sum}[name]])
    down, up, gq, gk, gv, go = place(0, ("down", "up", "att"), q_sum, [], False)
    down, up = place(1, ("down", "up"), f_sum, [down, up], False)
    gq, gk, gv, go, *smalls = place(1, ("att",), a_sum, [gq, gk, gv, go], True)
    sbq, sbv, sbo, sg1, ss1, sbd, sg2, ss2, sbu = smalls
    return (
        q_out.reshape(qn, ql, h),
        p_out.reshape(pn, plen, h),
        terms[:qn, 0],
        q_grad.reshape(qn, ql, h),
        p_grad.reshape(pn, plen, h),
        gq, sbq, gk, gv, sbv, go, sbo, sg1, ss1, up, sbu, down, sbd, sg2, ss2,
    )


def solution(mesh):
    split = P(AXES)
    return jax.shard_map(
        functools.partial(shards, dict(mesh.shape)),
        mesh=mesh,
        in_specs=(split,) * 6 + (P(),) * 15,
        out_specs=(split,) * 5 + (P(),) * 15,
        check_vma=False,
    )
```

```python
import functools

import jax
import jax.numpy as jnp
import numpy as np
from jax import lax
from jax.experimental import pallas as pl
from jax.experimental.pallas import tpu as pltpu
from jax.sharding import PartitionSpec as P

HEADS = 8
HS = 64
EPS = 1e-06
F32 = jnp.float32
B16 = jnp.bfloat16
I32 = jnp.int32
HIGH = lax.Precision.HIGHEST
AXES = ("dp", "rep")
SCALE = 0.125
MIB = 1 << 20
FAR = -3e38
ANY = pl.BlockSpec(memory_space=pl.ANY)
SMEM = pl.BlockSpec(memory_space=pltpu.SMEM)
VMEM = pl.BlockSpec(memory_space=pltpu.VMEM)
PLAN = (
    "attention", "q", "feed", "q", "back", "q+f", "f", "q", "a", "f", "q", "a", "f", "q", "a", "f",
    "a", "a", "q", "f", "a", "q", "place_q", "f", "a", "f", "place_f", "a",
)
SMALL = ("b_query", "b_value", "b_out", "gain_one", "shift_one", "b_down", "gain_two", "shift_two")
NSMALL = 12


def dot(a, b):
    return lax.dot_general(a, b, (((1,), (0,)), ((), ())), preferred_element_type=F32)


def dot_nt(a, b):
    return lax.dot_general(a, b, (((1,), (1,)), ((), ())), preferred_element_type=F32)


def dot_tn(a, b):
    return lax.dot_general(a, b, (((0,), (0,)), ((), ())), preferred_element_type=F32)


def dot_high(a, b):
    return lax.dot_general(
        a, b, (((1,), (0,)), ((), ())), precision=HIGH, preferred_element_type=F32
    )


def centred(v):
    c = v - jnp.mean(v, -1, keepdims=True)
    r = lax.rsqrt(jnp.mean(c * c, -1, keepdims=True) + EPS)
    return c * r, r


def norm_back(hat, r, gain, d_out):
    g_gain = jnp.sum(d_out * hat, 0, keepdims=True)
    g_shift = jnp.sum(d_out, 0, keepdims=True)
    d_hat = d_out * gain
    mean_a = jnp.mean(d_hat, -1, keepdims=True)
    mean_b = jnp.mean(d_hat * hat, -1, keepdims=True)
    return r * (d_hat - mean_a - hat * mean_b), g_gain, g_shift


def gelu_pair(x):
    phi = 0.5 + 0.5 * lax.erf(x * 0.7071067811865476)
    return x * phi, phi + x * (jnp.exp(x * x * -0.5) * 0.3989422804014327)


def stacked(x, group):
    lane = lax.broadcasted_iota(I32, x.shape, 1) // HS
    zero = jnp.zeros_like(x)
    return jnp.concatenate([jnp.where(lane == g, x, zero) for g in range(group)], 0)


def diagonal(o, group):
    rows = o.shape[0] // group
    lane = lax.broadcasted_iota(I32, (rows, o.shape[1]), 1) // HS
    out = o[:rows]
    for g in range(1, group):
        out = jnp.where(lane == g, o[g * rows : (g + 1) * rows], out)
    return out


def softmax(s):
    e = jnp.exp(s - jnp.max(s, -1, keepdims=True))
    return e * (1.0 / jnp.sum(e, -1, keepdims=True))


def attend(q, k, v, group, keep_probs, length=None):
    wide = HS * group
    parts = []
    for t in range(HEADS // group):
        at = slice(t * wide, (t + 1) * wide)
        scores = dot_nt(stacked(q[:, at], group), k[:, at])
        if length:
            rows = lax.broadcasted_iota(I32, scores.shape, 0) % q.shape[0]
            apart = rows // length != lax.broadcasted_iota(I32, scores.shape, 1) // length
            scores = jnp.where(apart, FAR, scores)
        probs = softmax(scores).astype(B16)
        keep_probs(t, probs)
        parts.append(diagonal(dot(probs, v[:, at]), group))
    return jnp.concatenate(parts, 1).astype(B16)


def attend_back(q, k, v, d_att, group, probs_of):
    wide = HS * group
    dq, dk, dv = [], [], []
    for t in range(HEADS // group):
        at = slice(t * wide, (t + 1) * wide)
        probs = probs_of(t)
        d_stack = stacked(d_att[:, at], group)
        d_probs = dot_nt(d_stack, v[:, at])
        dv.append(dot_tn(probs, d_stack))
        p32 = probs.astype(F32)
        inside = jnp.sum(p32 * d_probs, -1, keepdims=True)
        d_scores = (p32 * (d_probs - inside)).astype(B16)
        dq.append(diagonal(dot(d_scores, k[:, at]), group) * SCALE)
        dk.append(dot_tn(d_scores, stacked(q[:, at], group)))
    return tuple(jnp.concatenate(x, 1).astype(B16) for x in (dq, dk, dv))


def feed(first, w_up, b_up, w_down, b_down, gain, shift, keep, tile=512):
    hat, r = centred(first)
    normed = hat * gain + shift
    low = normed.astype(B16)
    second = normed + b_down
    for j in range(w_up.shape[1] // tile):
        at = slice(j * tile, (j + 1) * tile)
        act, slope = gelu_pair(dot(low, w_up[:, at]) + b_up[:, at])
        act = act.astype(B16)
        keep(at, act, slope)
        second = second + dot(act, w_down[at, :])
    return second, hat, r, low


def feed_both(first, w_up, b_up, w_down, b_down, g1, s1, g2, s2, d_out, slopes, keep_act, keep_inner):
    def keep(at, act, slope):
        keep_act(at, act)
        slopes[:, at] = slope

    ff = w_up.shape[1]
    second, hat, r, low = feed(first, w_up, b_up, w_down, b_down, g1, s1, keep, ff)
    hat2, r2 = centred(second)
    out = (hat2 * g2 + s2).astype(B16)
    d_second, gg2, gs2 = norm_back(hat2, r2, g2, d_out)
    d_down = d_second.astype(B16)
    gb_down = jnp.sum(d_down.astype(F32), 0, keepdims=True)
    d = (dot_nt(d_down, w_down[...]) * slopes[...]).astype(B16)
    keep_inner(slice(0, ff), d)
    gb_up = jnp.sum(d.astype(F32), 0, keepdims=True)
    gb_up = [gb_up[:, j * 512 : (j + 1) * 512] for j in range(ff // 512)]
    d_normed = d_second + dot_nt(d, w_up[...])
    d_first, gg1, gs1 = norm_back(hat, r, g1, d_normed)
    return out, d_down, d_first, low, (gg1, gs1, gb_down, gg2, gs2, *gb_up)


def cls_rows(q, k, v, count):
    total, width = q.shape
    length = total // count
    rows = count * HEADS
    own = (
        lax.broadcasted_iota(I32, (rows, width), 1) // HS
        == lax.broadcasted_iota(I32, (rows, width), 0) % HEADS
    )
    first = [
        jnp.broadcast_to(q[i * length : i * length + 1, :].astype(F32), (HEADS, width))
        for i in range(count)
    ]
    q_rows = jnp.where(own, jnp.concatenate(first, 0), 0.0).astype(B16)
    scores = dot_nt(q_rows, k[...])
    apart = (
        lax.broadcasted_iota(I32, scores.shape, 0) // HEADS
        != lax.broadcasted_iota(I32, scores.shape, 1) // length
    )
    probs = softmax(jnp.where(apart, FAR, scores)).astype(B16)
    mixed = jnp.where(own, dot(probs, v[...]), 0.0)
    return jnp.concatenate(
        [
            jnp.sum(mixed[i * HEADS : (i + 1) * HEADS], 0, keepdims=True)
            for i in range(count)
        ],
        0,
    )


def row(ref, e):
    return ref[e : e + 1, :]


def front_kernel(
    positives, counts, bq, bv, bo, g1, s1, bu, bd, g2, s2, p_x, q_x, wq, wk, wv, wo, wu, wd,
    pq, pk, pv, qq, qk, qv, payload,
    p_s, q_s, wqkv_s, wo_s, wu_s, wd_s, p_out, q_out, pay_s, sems, out_sems,
):
    width = q_x.shape[1]
    count = 4

    def load(i, src, dst):
        return pltpu.make_async_copy(src, dst, sems.at[i])

    w_in = (wq, wk, wv)
    first_in = [load(0, p_x, p_s)]
    first_in += [load(1 + i, w.at[1], wqkv_s.at[1, i]) for i, w in enumerate(w_in)]
    q_in = [load(4, q_x, q_s)]
    q_in += [load(5 + i, w.at[0], wqkv_s.at[0, i]) for i, w in enumerate(w_in)]
    later = [load(8, wo, wo_s), load(9, wu, wu_s), load(10, wd, wd_s)]
    for c in first_in + q_in + later:
        c.start()

    def project(x, e, held, targets):
        copies = []
        for i, (bias, target) in enumerate(zip((bq, None, bv), targets)):
            y = dot(x[...], wqkv_s[e, i])
            y = (y if bias is None else y + row(bias, e)).astype(B16)
            held[i] = y * SCALE if i == 0 else y
            copies.append(pltpu.make_async_copy(held.at[i], target, out_sems.at[3 * e + i]))
            copies[-1].start()
        return copies

    for c in first_in:
        c.wait()
    out = project(p_s, 1, p_out, (pq, pk, pv))
    for c in q_in:
        c.wait()
    out += project(q_s, 0, q_out, (qq, qk, qv))

    pay_s[...] = jnp.zeros_like(pay_s)
    lanes = lax.broadcasted_iota(I32, (1, width), 1)
    for i in range(count):
        mask = jnp.zeros((1, width), F32)
        for j in range(positives.shape[1]):
            mask = jnp.where((lanes == positives[i, j]) & (j < counts[i]), 1.0, mask)
        pay_s[8 + i : 9 + i, :] = mask
    att = [cls_rows(held.at[0], held.at[1], held.at[2], count) for held in (p_out, q_out)]
    for c in later:
        c.wait()
    for e, start, mixed, x in ((1, 0, att[0], p_s), (0, 4, att[1], q_s)):
        length = x.shape[0] // count
        own = [x[i * length : i * length + 1, :].astype(F32) for i in range(count)]
        zero = [jnp.zeros((4, width), F32)]
        mixed = jnp.concatenate([mixed] + zero, 0).astype(B16)
        first = jnp.concatenate(own + zero, 0) + dot(mixed, wo_s[e]) + row(bo, e)
        second, _, _, _ = feed(
            first, wu_s.at[e], row(bu, e), wd_s.at[e], row(bd, e), row(g1, e), row(s1, e),
            lambda at, act, slope: None, 2048,
        )
        done = centred(second)[0] * row(g2, e) + row(s2, e)
        pay_s[start : start + 4, :] = done[:4]
    payload[...] = pay_s[...].astype(B16)
    for c in out:
        c.wait()


def passage_attention_kernel(q, k, v, x, bo, wo, probs, att, first, wo_s, sem):
    copy = pltpu.make_async_copy(wo.at[1], wo_s, sem)

    @pl.when(pl.program_id(0) == 0)
    def _():
        copy.start()

    def keep_probs(t, value):
        probs[t] = value

    a = attend(q[...], k[...], v[...], 4, keep_probs)
    att[...] = a

    @pl.when(pl.program_id(0) == 0)
    def _():
        copy.wait()

    first[...] = x[...].astype(F32) + dot(a, wo_s[...]) + row(bo, 1)


def question_attention_kernel(length, q, k, v, x, bo, wo, probs, att, first):
    def keep_probs(t, value):
        probs[t] = value

    a = attend(q[...], k[...], v[...], 4, keep_probs, length)
    att[...] = a
    first[...] = x[...].astype(F32) + dot(a, wo[...]) + row(bo, 0)


def send_unit(wide, grads, table, keep, send, offset, sem_keep, sem_send):
    half, _, width = keep.shape
    blocks = 2 * half
    rows = grads.shape[0] * grads.shape[1] // (width * blocks)
    across = grads.shape[1] // width

    def start(out, base, sem):
        def body(r, carry):
            c = table[base + r]
            src = grads.at[
                pl.ds(pl.multiple_of(c // across * rows, rows), rows),
                pl.ds(pl.multiple_of(c % across * width, width), width),
            ] if wide else grads.at[pl.ds(pl.multiple_of(c * rows, rows), rows), :]
            pltpu.make_async_copy(src, out.at[r, pl.ds(offset, rows), :], sem).start()
            return carry

        lax.fori_loop(0, half, body, 0)

    start(send, half, sem_send)
    start(keep, 0, sem_keep)


def wait_units(keep, send, sem_keep, sem_send):
    pltpu.make_async_copy(send, send, sem_send).wait()
    pltpu.make_async_copy(keep, keep, sem_keep).wait()


def contrast(gathered, me, scale):
    z = jnp.concatenate([g[...] for g in gathered], 0)
    n = z.shape[0] // 16
    total_rows = 4 * n
    base = me * 4
    place = lax.broadcasted_iota(I32, (total_rows, z.shape[0]), 1)
    index = lax.broadcasted_iota(I32, (total_rows, z.shape[0]), 0)
    apart = (index // 4) ^ me
    block = jnp.zeros_like(apart)
    depth = n.bit_length() - 1
    for i in range(depth):
        block = block + (((apart >> i) & 1) << (depth - 1 - i))
    sel = block * 16 + index % 4

    def rows_at(k):
        return dot(jnp.where(place == sel + k, 1.0, 0.0).astype(B16), z)

    all_p, all_q, mask = rows_at(0), rows_at(4), rows_at(8)[:, :total_rows]
    sim = dot_nt(all_q.astype(B16), all_p.astype(B16)) * scale
    expo = jnp.exp(sim - jnp.max(sim, -1, keepdims=True))
    total = jnp.sum(expo, -1, keepdims=True)
    hit = mask * expo
    pos_total = jnp.sum(hit, -1, keepdims=True)
    terms = jnp.log(total) - jnp.log(pos_total)
    coeff = expo / total - hit / pos_total
    mine = jnp.where(
        lax.broadcasted_iota(I32, (8, total_rows), 1)
        == base + lax.broadcasted_iota(I32, (8, total_rows), 0),
        1.0,
        0.0,
    )
    d_q = dot_high(dot_high(mine, coeff), all_p) * scale
    d_p = dot_high(dot_high(mine, coeff.T), all_q) * scale
    return dot_high(mine, jnp.broadcast_to(terms, (total_rows, 128))), d_q, d_p


def question_back_kernel(
    table, gathered_a, gathered_b, x, cot, q, k, v, probs, att, first,
    g1, s1, bu, bd, g2, s2, wq, wk, wv, wo, wu, wd,
    terms, d_cls_p, x_grad, small, out, keep, send,
    wqkv_s, wo_s, wu_s, wd_s, act_s, slope_s, inner_s, g_down, g_up, g_att, sems, out_sems,
):
    copies = [
        pltpu.make_async_copy(src.at[0], dst, sems.at[i])
        for i, (src, dst) in enumerate(
            (
                (wu, wu_s),
                (wd, wd_s),
                (wo, wo_s),
                (wq, wqkv_s.at[0]),
                (wk, wqkv_s.at[1]),
                (wv, wqkv_s.at[2]),
            )
        )
    ]
    for c in copies:
        c.start()
    n = keep.shape[0] * 2
    rows = 2048 // n
    count = 4
    length = x.shape[0] // count
    width = x.shape[1]
    loss, d_q, d_p = contrast(
        (gathered_a, gathered_b), table[n], 2.0 / float(np.sqrt(width))
    )
    terms[...] = loss
    d_cls_p[...] = d_p
    place = lax.broadcasted_iota(I32, x.shape, 0)
    d_out = cot[...].astype(F32)
    for i in range(count):
        d_out = d_out + jnp.where(place == i * length, d_q[i : i + 1], 0.0)
    for c in copies[:2]:
        c.wait()

    def keep_act(at, value):
        act_s[:, at] = value

    def keep_inner(at, value):
        inner_s[:, at] = value

    out[...], d_down, d_first, low, sums = feed_both(
        first[...], wu_s, row(bu, 0), wd_s, row(bd, 0), row(g1, 0), row(s1, 0), row(g2, 0),
        row(s2, 0), d_out, slope_s, keep_act, keep_inner,
    )
    sems_out = (out_sems.at[0], out_sems.at[1])
    g_down[...] = dot_tn(act_s[...], d_down).astype(B16)
    send_unit(False, g_down, table, keep, send, 0, *sems_out)
    g_up[...] = dot_tn(low, inner_s[...]).astype(B16)
    send_unit(True, g_up, table, keep, send, rows, *sems_out)
    for c in copies[2:]:
        c.wait()
    d_branch = d_first.astype(B16)
    d_att = dot_nt(d_branch, wo_s[...]).astype(B16)
    dq, dk, dv = attend_back(q[...], k[...], v[...], d_att, 4, lambda t: probs[t])
    rows_x = x[...]
    for i, d in enumerate((dq, dk, dv)):
        g_att[i * width : (i + 1) * width, :] = dot_tn(rows_x, d).astype(B16)
    g_att[3 * width :, :] = dot_tn(att[...], d_branch).astype(B16)
    send_unit(False, g_att, table, keep, send, 2 * rows, *sems_out)
    x_grad[...] = (
        d_first + dot_nt(dq, wqkv_s[0]) + dot_nt(dk, wqkv_s[1]) + dot_nt(dv, wqkv_s[2])
    )
    small[...] = jnp.zeros_like(small)
    values = [jnp.sum(d.astype(F32), 0, keepdims=True) for d in (dq, dv, d_branch)]
    for i, value in enumerate((*values, *sums)):
        small[i : i + 1, :] = value
    wait_units(keep, send, *sems_out)


def passage_feed_kernel(
    steps, table, d_cls, cot, first, g1, s1, bu, bd, g2, s2, wu, wd,
    out, d_first, small, keep, send,
    wu_s, wd_s, slope_s, act_s, inner_s, down_s, low_s, g_down, g_up, sems, out_sems,
):
    b = pl.program_id(0)
    sems_out = (out_sems.at[0], out_sems.at[1])
    rows = 2048 // (2 * keep.shape[0])
    total_rows = act_s.shape[0]
    per = 4 // steps

    @pl.when(b < steps)
    def _():
        copies = [
            pltpu.make_async_copy(src, dst, sems.at[i])
            for i, (src, dst) in enumerate(((wu.at[1], wu_s), (wd.at[1], wd_s)))
        ]

        @pl.when(b == 0)
        def _():
            for c in copies:
                c.start()
            small[...] = jnp.zeros_like(small)
            for c in copies:
                c.wait()

        place = lax.broadcasted_iota(I32, cot.shape, 0)
        d_out = cot[...].astype(F32)
        for i in range(per):
            mine = d_cls[pl.ds(b * per + i, 1), :]
            d_out = d_out + jnp.where(place == i * (cot.shape[0] // per), mine, 0.0)
        mine = pl.ds(pl.multiple_of(b * cot.shape[0], cot.shape[0]), cot.shape[0])

        def keep_act(at, value):
            act_s[mine, at] = value

        def keep_inner(at, value):
            inner_s[mine, at] = value

        out[...], down_s[mine, :], d_first[...], low_s[mine, :], sums = feed_both(
            first[...], wu_s, row(bu, 1), wd_s, row(bd, 1), row(g1, 1), row(s1, 1), row(g2, 1),
            row(s2, 1), d_out, slope_s, keep_act, keep_inner,
        )
        for i, value in enumerate(sums):
            small[3 + i : 4 + i, :] += value

    @pl.when(b == steps)
    def _():
        g_down[...] = dot_tn(act_s[...], down_s[...]).astype(B16)
        send_unit(False, g_down, table, keep, send, 0, *sems_out)

    @pl.when(b == steps + 1)
    def _():
        g_up[...] = dot_tn(low_s[...], inner_s[...]).astype(B16)
        send_unit(True, g_up, table, keep, send, rows, *sems_out)
        wait_units(keep, send, *sems_out)


def passage_attention_back_kernel(
    table, small_q, small_p, d_first, q, k, v, probs, x, att, wq, wk, wv, wo,
    x_grad, keep, send,
    wqkv_s, wo_s, x_s, att_s, d_s, small, sent_s, g_att, sems, out_sems,
):
    b = pl.program_id(0)
    nb = pl.num_programs(0)
    length, width = d_first.shape
    n = 2 * keep.shape[0]
    rows = 2048 // n
    copies = [
        pltpu.make_async_copy(src, dst, sems.at[i])
        for i, (src, dst) in enumerate(
            (
                (wo.at[1], wo_s),
                (wq.at[1], wqkv_s.at[0]),
                (wk.at[1], wqkv_s.at[1]),
                (wv.at[1], wqkv_s.at[2]),
                (x, x_s),
                (att, att_s),
            )
        )
    ]

    @pl.when(b == 0)
    def _():
        for c in copies:
            c.start()
        small[...] = small_p[...]
        for c in copies[:4]:
            c.wait()

    d_branch = d_first[...].astype(B16)
    d_att = dot_nt(d_branch, wo_s[...]).astype(B16)
    dq, dk, dv = attend_back(q[...], k[...], v[...], d_att, 4, lambda t: probs[t])
    mine = pl.ds(pl.multiple_of(b * length, length), length)
    for i, d in enumerate((dq, dk, dv, d_branch)):
        d_s[i, mine, :] = d
    for i, d in enumerate((dq, dv, d_branch)):
        small[i : i + 1, :] += jnp.sum(d.astype(F32), 0, keepdims=True)
    x_grad[...] = (
        d_first[...] + dot_nt(dq, wqkv_s[0]) + dot_nt(dk, wqkv_s[1]) + dot_nt(dv, wqkv_s[2])
    )

    @pl.when(b == nb - 1)
    def _():
        sent_s[...] = jnp.zeros_like(sent_s)
        top = lax.broadcasted_iota(I32, (16, width), 0) == 0
        for e, ref in enumerate((small_q, small)):
            for i in range(NSMALL):
                sent_s[e * NSMALL + i] = jnp.where(top, ref[i : i + 1, :], 0.0).astype(B16)
        for base, out, sem in ((n // 2, send, out_sems.at[1]), (0, keep, out_sems.at[0])):

            def body(r, carry, base=base, out=out, sem=sem):
                pltpu.make_async_copy(
                    sent_s.at[table[base + r]], out.at[r, pl.ds(rows, 16), :], sem
                ).start()
                return carry

            lax.fori_loop(0, n // 2, body, 0)
        for c in copies[4:]:
            c.wait()
        for i in range(3):
            g_att[i * width : (i + 1) * width, :] = dot_tn(x_s[...], d_s[i]).astype(B16)
        g_att[3 * width :, :] = dot_tn(att_s[...], d_s[3]).astype(B16)
        send_unit(False, g_att, table, keep, send, 0, out_sems.at[0], out_sems.at[1])
        wait_units(keep, send, out_sems.at[0], out_sems.at[1])


def place_kernel(e, kinds, starts, n_alias, with_small, *refs):
    table = refs[0]
    pieces = refs[1 : 1 + len(starts)]
    outs = refs[1 + len(starts) + n_alias :]
    n_out = sum(4 if kind == "att" else 1 for kind in kinds)
    n_small = 9 if with_small else 0
    targets, smalls = outs[:n_out], outs[n_out : n_out + n_small]
    scratch = outs[n_out + n_small :]
    stages, sems = scratch[: len(kinds)], scratch[len(kinds)]
    small_s = scratch[len(kinds) + 1] if with_small else None
    n = starts[-1] + pieces[-1].shape[0]
    rows = 2048 // n
    for piece, start in zip(pieces, starts):

        def body(r, carry, piece=piece, start=start):
            c = table[start + r]
            k = 0
            for u, kind in enumerate(kinds):
                stage = stages[u].at[start + r]
                stage[...] = piece[r, u * rows : (u + 1) * rows, :].astype(F32)
                if kind == "down":
                    pltpu.make_async_copy(
                        stage,
                        targets[k].at[e, pl.ds(pl.multiple_of(c * rows, rows), rows), :],
                        sems.at[k],
                    ).start()
                    k += 1
                elif kind == "up":
                    pltpu.make_async_copy(
                        stage,
                        targets[k].at[
                            e,
                            pl.ds(pl.multiple_of(c // 4 * rows, rows), rows),
                            pl.ds(pl.multiple_of(c % 4 * 512, 512), 512),
                        ],
                        sems.at[k],
                    ).start()
                    k += 1
                else:
                    quarter = n // 4
                    for m in range(4):

                        @pl.when(c // quarter == m)
                        def _(m=m, k=k, stage=stage):
                            at = pl.ds(pl.multiple_of(c % quarter * rows, rows), rows)
                            pltpu.make_async_copy(
                                stage, targets[k + m].at[e, at, :], sems.at[k + m]
                            ).start()

                    k += 4
            if with_small:
                block = piece[r, len(kinds) * rows : len(kinds) * rows + 16, :].astype(F32)
                small_s[c] = block[0:8]
            return carry

        lax.fori_loop(0, piece.shape[0], body, 0)
    if with_small:
        for f in range(2):
            for i in range(8):
                smalls[i][f : f + 1, :] = small_s[f * NSMALL + i, 0:1, :]
            for j in range(4):
                smalls[8][f : f + 1, j * 512 : (j + 1) * 512] = small_s[f * NSMALL + 8 + j, 0:1, :]
    for k, target in enumerate(targets):
        pltpu.make_async_copy(target.at[e], target.at[e], sems.at[k]).wait()


def rounds_of(mesh_shape):
    dp, rep = mesh_shape["dp"], mesh_shape["rep"]
    core, *x = [1 << i for i in range(rep.bit_length() - 1)]
    y, *z = [rep << i for i in range(dp.bit_length() - 1)]
    return [core, *x, y, *z], [core, y, *x, *z]


def order_table(rounds, n):
    depth = len(rounds[0])
    table = np.zeros((n, n), np.int32)
    for d in range(n):
        for r in range(n):
            c = d ^ (rounds[0][0] if r >> (depth - 1) & 1 else 0)
            for k in range(1, depth):
                if r >> (depth - 1 - k) & 1:
                    c ^= rounds[c & 1][k]
            table[d, r] = c
    return table


def exchange(x, masks, n):
    return lax.ppermute(x, AXES, [(d, d ^ masks[d & 1]) for d in range(n)])


def total(parts):
    return sum(p.astype(F32) for p in parts).astype(B16)


def steps_of(rounds, pairs):
    even, odd = rounds
    steps, k = [], 0
    while k < len(even):
        if even[k] in pairs:
            steps.append(((even[k], odd[k]), (even[k + 1], odd[k + 1])))
            k += 2
        else:
            steps.append(((even[k], odd[k]),))
            k += 1
    return steps


def partners(step):
    if len(step) == 1:
        return [step[0]]
    high, low = step
    return [low, high, (low[0] ^ high[0], low[1] ^ high[1])]


def join_kernel(*refs):
    *parts, out = refs
    m = parts[0].shape[0]
    for i, part in enumerate(parts):
        out[i * m : (i + 1) * m] = part[...]


def joined(order, pieces, limit=24):
    m, rows, width = pieces[0].shape
    count = len(pieces)
    return order(
        join_kernel,
        *pieces,
        name="join",
        in_specs=[VMEM] * count,
        out_specs=[VMEM],
        out_shape=[shape((count * m, rows, width), B16)],
        compiler_params=params(limit),
        cost_estimate=SHORT,
    )


class Order:
    def __init__(self):
        self.token = None

    def fence(self, arrays):
        *arrays, self.token = lax.optimization_barrier((*arrays, self.token))
        return arrays

    def __call__(self, kernel, *operands, in_specs, out_specs, out_shape, **kwargs):
        skip = 0 if self.token is None else 1
        last = skip + len(operands) + len(out_shape)

        def body(*refs):
            kernel(*refs[skip:last], *refs[last + 1 :])

        aliases = kwargs.pop("input_output_aliases", {})
        call = pl.pallas_call(
            body,
            in_specs=[ANY] * skip + in_specs,
            out_specs=list(out_specs) + [ANY],
            out_shape=list(out_shape) + [shape((8, 128))],
            input_output_aliases={k + skip: v for k, v in aliases.items()},
            **kwargs,
        )
        *outs, self.token = call(*([self.token] if skip else []), *operands)
        return outs


class Sum:
    def __init__(self, order, halving, doubling, n, keep, send):
        self.order, self.n = order, n
        self.halving, self.doubling = list(halving), list(doubling)
        self.parts, self.m, self.pieces = [keep], keep.shape[0], None
        self.got, self.out, self.now = None, [send], self.halving.pop(0)
        self.going = True

    def start(self):
        masks = partners(self.now)
        if self.pieces is None:
            self.got = [exchange(x, m, self.n) for x, m in zip(self.out, masks)]
        else:
            self.got = [exchange(x, m, self.n) for m in masks for x in self.out]

    def take(self):
        if self.pieces is None:
            self.parts += self.got
            if self.halving:
                self.now = self.halving.pop(0)
                ways = 2 ** len(self.now)
                q = self.m // ways
                self.out = [
                    total([p[i * q : (i + 1) * q] for p in self.parts]) for i in range(1, ways)
                ]
                self.m = q
                return True
            self.out = self.pieces = [total([p[:1] for p in self.parts])]
        else:
            self.pieces = self.pieces + self.got
            if not self.doubling:
                return False
            if len(self.doubling) > 1:
                self.pieces = [jnp.concatenate(self.pieces, 0)]
            self.out = self.pieces
        self.now = self.doubling.pop()
        return True


class Plan:
    def __init__(self, order):
        self.order, self.sums, self.starting = order, {}, []
        self.fresh = True

    def add(self, name, item):
        self.sums[name] = item
        self.starting.append(item)

    def flush(self):
        if not self.starting:
            return
        flat = self.order.fence([x for s in self.starting for x in s.out])
        for s in self.starting:
            s.out, flat = flat[: len(s.out)], flat[len(s.out) :]
            if s.pieces is not None:
                s.pieces = s.out
        for s in self.starting:
            s.start()
        self.starting = []

    def step(self, names):
        if not self.fresh:
            self.flush()
        items = [self.sums[name] for name in names if self.sums[name].going]
        flat = self.order.fence([x for s in items for x in s.got])
        for s in items:
            s.got, flat = flat[: len(s.got)], flat[len(s.got) :]
        for s in items:
            s.going = s.take()
            if s.going:
                self.starting.append(s)
        self.fresh = False

    def run(self, names, kernels, places):
        for name in names:
            if name in kernels:
                self.flush()
                kernels[name]()
                self.fresh = True
            elif name in places:
                self.flush()
                if not self.sums[name[-1]].going:
                    places.pop(name)()
            else:
                self.step(name.split("+"))
        while any(s.going for s in self.sums.values()):
            for name, item in self.sums.items():
                if item.going:
                    self.step([name])
        self.flush()
        for place in places.values():
            place()


class Gather:
    def __init__(self, order, x, n):
        bits = [1 << i for i in reversed(range(n.bit_length() - 1))]
        assert len(bits) % 2 == 1
        self.order, self.n = order, n
        self.stages = [bits[i : i + 2] for i in range(0, len(bits), 2)]
        self.pieces = [x[None]]
        self.issue()

    def issue(self):
        (mine,) = self.order.fence(self.pieces)
        now = self.stages.pop(0)
        masks = now if len(now) == 1 else [now[0], now[1], now[0] | now[1]]
        self.pieces = [mine] + [
            lax.ppermute(mine, AXES, [(d, d ^ m) for d in range(self.n)]) for m in masks
        ]

    def step(self):
        self.pieces = joined(self.order, self.order.fence(self.pieces), 62)
        self.issue()

    def result(self):
        return self.order.fence(self.pieces)


def params(limit):
    return pltpu.CompilerParams(vmem_limit_bytes=limit * MIB)


LONG = pl.CostEstimate(flops=200_000_000_000, bytes_accessed=1000, transcendentals=0)


SHORT = pl.CostEstimate(flops=1000, bytes_accessed=1000, transcendentals=0)


def shape(dims, dtype=F32):
    return jax.ShapeDtypeStruct(dims, dtype)


def sem(count):
    return pltpu.SemaphoreType.DMA((count,))


def shards(
    mesh_shape,
    q_tokens,
    p_tokens,
    q_cotangent,
    p_cotangent,
    positives,
    counts,
    wq,
    bq,
    wk,
    wv,
    bv,
    wo,
    bo,
    g1,
    s1,
    wu,
    bu,
    wd,
    bd,
    g2,
    s2,
):
    n = mesh_shape["dp"] * mesh_shape["rep"]
    plane = rounds_of(mesh_shape)
    pairs = plane[0][-2:-1]
    me = lax.axis_index("dp") * mesh_shape["rep"] + lax.axis_index("rep")
    tables = np.concatenate([order_table(plane, n), np.arange(n, dtype=np.int32)[:, None]], 1)
    table = lax.dynamic_index_in_dim(jnp.asarray(tables), me, 0, False)
    qn, ql, h = q_tokens.shape
    pn, plen, _ = p_tokens.shape
    ff = wu.shape[2]
    qr, pr = qn * ql, pn * plen
    assert qn == 4 and pn == 4 and h == 512 and ff == 2048 and 24 <= n and 4 * n <= h
    q_x, p_x = q_tokens.reshape(qr, h), p_tokens.reshape(pr, h)
    q_cot, p_cot = q_cotangent.reshape(qr, h), p_cotangent.reshape(pr, h)
    order = Order()

    def whole(*dims):
        return pl.BlockSpec(dims, lambda b: (0,) * len(dims))

    one, wide = whole(2, h), whole(2, ff)
    seq_block = pl.BlockSpec((plen, h), lambda b: (b, 0))
    pq, pk, pv, qq, qk, qv, payload = order(
        front_kernel,
        positives, counts, bq, bv, bo, g1, s1, bu, bd, g2, s2, p_x, q_x, wq, wk, wv, wo, wu, wd,
        name="front",
        in_specs=[SMEM] * 2 + [VMEM] * 9 + [ANY] * 8,
        out_specs=[ANY] * 6 + [VMEM],
        out_shape=[shape((pr, h), B16)] * 3 + [shape((qr, h), B16)] * 3 + [shape((16, h), B16)],
        scratch_shapes=[
            pltpu.VMEM((pr, h), B16),
            pltpu.VMEM((qr, h), B16),
            pltpu.VMEM((2, 3, h, h), B16),
            pltpu.VMEM((2, h, h), B16),
            pltpu.VMEM((2, h, ff), B16),
            pltpu.VMEM((2, ff, h), B16),
            pltpu.VMEM((3, pr, h), B16),
            pltpu.VMEM((3, qr, h), B16),
            pltpu.VMEM((16, h), F32),
            sem(11),
            sem(6),
        ],
        compiler_params=params(62),
        cost_estimate=LONG,
    )
    gather = Gather(order, payload, n)

    def passages(kernel, name, at, count, operands, in_specs, outs, before, **kwargs):
        def spec(block):
            if not isinstance(block, tuple):
                return block
            axis = block.index(None) if None in block else len(block) - 2
            return pl.BlockSpec(
                block, lambda b: tuple(b + at if i == axis else 0 for i in range(len(block)))
            )

        n_in, n_before = len(operands), len(before)

        def body(*refs):
            kernel(*refs[:n_in], *refs[n_in + n_before :])

        return order(
            body,
            *operands,
            *before,
            name=name,
            grid=(count,),
            in_specs=[spec(x) for x in in_specs] + [ANY] * n_before,
            out_specs=[spec(block) for block, _ in outs],
            out_shape=[s for _, s in outs],
            input_output_aliases={n_in + i: i for i in range(n_before)},
            compiler_params=params(62),
            cost_estimate=LONG,
            **kwargs,
        )

    seq, seq_wide = (plen, h), (plen, ff)
    probs_block = (None, 2, 4 * plen, plen)

    def attention(at, count, before):
        return passages(
            passage_attention_kernel, "passage_attention", at, count,
            (pq, pk, pv, p_x, bo, wo),
            [seq] * 4 + [one, ANY],
            [
                (probs_block, shape((pn, 2, 4 * plen, plen), B16)),
                (seq, shape((pr, h), B16)),
                (seq, shape((pr, h))),
            ],
            before,
            scratch_shapes=[pltpu.VMEM((h, h), B16), pltpu.SemaphoreType.DMA],
        )

    part = attention(0, 2, [])
    gather.step()
    q_probs, q_att, q_first = order(
        functools.partial(question_attention_kernel, ql),
        qq, qk, qv, q_x, bo, wo,
        name="question_attention",
        grid=(1,),
        in_specs=[whole(qr, h)] * 4 + [one, pl.BlockSpec((None, h, h), lambda b: (0, 0, 0))],
        out_specs=[whole(2, 4 * qr, qr), whole(qr, h), whole(qr, h)],
        out_shape=[shape((2, 4 * qr, qr), B16), shape((qr, h), B16), shape((qr, h))],
        compiler_params=params(62),
        cost_estimate=LONG,
    )
    while gather.stages:
        gather.step()
    gathered = [x.reshape(-1, h) for x in gather.result()]

    rows = 2048 // n
    half = n // 2
    terms, d_cls_p, q_grad, small_q, q_out, q_keep, q_send = order(
        question_back_kernel,
        table, *gathered, q_x, q_cot, qq, qk, qv, q_probs, q_att, q_first,
        g1, s1, bu, bd, g2, s2, wq, wk, wv, wo, wu, wd,
        name="question_back",
        in_specs=[SMEM] + [VMEM] * 16 + [ANY] * 6,
        out_specs=[VMEM] * 5 + [ANY] * 2,
        out_shape=[
            shape((8, 128)),
            shape((8, h)),
            shape((qr, h)),
            shape((16, h)),
            shape((qr, h), B16),
            shape((half, 3 * rows, h), B16),
            shape((half, 3 * rows, h), B16),
        ],
        scratch_shapes=[
            pltpu.VMEM((3, h, h), B16),
            pltpu.VMEM((h, h), B16),
            pltpu.VMEM((h, ff), B16),
            pltpu.VMEM((ff, h), B16),
            pltpu.VMEM((qr, ff), B16),
            pltpu.VMEM((qr, ff), F32),
            pltpu.VMEM((qr, ff), B16),
            pltpu.VMEM((ff, h), B16),
            pltpu.VMEM((h, ff), B16),
            pltpu.VMEM((4 * h, h), B16),
            sem(6),
            sem(2),
        ],
        compiler_params=params(62),
        cost_estimate=LONG,
    )
    steps = steps_of(plane, pairs)
    plan = Plan(order)
    plan.add("q", Sum(order, steps, steps, n, q_keep, q_send))
    r = {}

    def run_attention():
        r["p_probs"], r["p_att"], r["p_first"] = attention(2, 2, part)

    parts_of = 2
    two = (pr // parts_of, h)

    def rows_at(width):
        return pl.BlockSpec((pr // parts_of, width), lambda b: (jnp.minimum(b, parts_of - 1), 0))

    def run_feed():
        r["p_out"], r["d_first"], r["small_p"], *out = order(
            functools.partial(passage_feed_kernel, parts_of),
            table, d_cls_p, p_cot, r["p_first"], g1, s1, bu, bd, g2, s2, wu, wd,
            name="passage_feed",
            grid=(parts_of + 2,),
            in_specs=[SMEM, whole(8, h), rows_at(h), rows_at(h), one, one, wide, one, one, one, ANY, ANY],
            out_specs=[rows_at(h), rows_at(h), whole(16, h), ANY, ANY],
            out_shape=[shape((pr, h), B16), shape((pr, h)), shape((16, h))]
            + [shape((half, 2 * rows, h), B16)] * 2,
            scratch_shapes=[
                pltpu.VMEM((h, ff), B16),
                pltpu.VMEM((ff, h), B16),
                pltpu.VMEM((pr // parts_of, ff), F32),
                pltpu.VMEM((pr, ff), B16),
                pltpu.VMEM((pr, ff), B16),
                pltpu.VMEM((pr, h), B16),
                pltpu.VMEM((pr, h), B16),
                pltpu.VMEM((ff, h), B16),
                pltpu.VMEM((h, ff), B16),
                sem(2),
                sem(2),
            ],
            compiler_params=params(62),
            cost_estimate=LONG,
        )
        plan.add("f", Sum(order, steps, steps, n, *out))

    def run_back():
        r["p_grad"], *out = order(
            passage_attention_back_kernel,
            table, small_q, r["small_p"], r["d_first"], pq, pk, pv, r["p_probs"], p_x, r["p_att"], wq, wk, wv, wo,
            name="passage_attention_back",
            grid=(pn,),
            in_specs=[SMEM, whole(16, h), whole(16, h)] + [seq_block] * 4
            + [pl.BlockSpec(probs_block, lambda b: (b, 0, 0, 0))] + [ANY] * 6,
            out_specs=[seq_block, ANY, ANY],
            out_shape=[shape((pr, h))] + [shape((half, rows + 16, h), B16)] * 2,
            scratch_shapes=[
                pltpu.VMEM((3, h, h), B16),
                pltpu.VMEM((h, h), B16),
                pltpu.VMEM((pr, h), B16),
                pltpu.VMEM((pr, h), B16),
                pltpu.VMEM((4, pr, h), B16),
                pltpu.VMEM((16, h), F32),
                pltpu.VMEM((n, 16, h), B16),
                pltpu.VMEM((4 * h, h), B16),
                sem(6),
                sem(2),
            ],
            compiler_params=params(62),
            cost_estimate=LONG,
        )
        plan.add("a", Sum(order, steps, steps, n, *out))

    def place(e, kinds, which, before, with_small):
        pieces = plan.sums[which].pieces
        starts, at = [], 0
        for piece in pieces:
            starts.append(at)
            at += piece.shape[0]
        dims = []
        for kind in kinds:
            dims += {"down": [(2, ff, h)], "up": [(2, h, ff)], "att": [(2, h, h)] * 4}[kind]
        outs = [shape(d) for d in dims]
        smalls = [shape((2, h))] * 8 + [shape((2, ff))] if with_small else []
        return order(
            functools.partial(
                place_kernel, e, kinds, tuple(starts), len(before), with_small
            ),
            table, *pieces, *before,
            name="place",
            in_specs=[SMEM] + [VMEM] * len(pieces) + [ANY] * len(before),
            out_specs=[ANY] * len(outs) + [VMEM] * len(smalls),
            out_shape=outs + smalls,
            input_output_aliases={1 + len(pieces) + i: i for i in range(len(before))},
            scratch_shapes=[pltpu.VMEM((n, rows, h), F32) for _ in kinds]
            + [sem(len(outs))]
            + ([pltpu.VMEM((n, 8, h), F32)] if with_small else []),
            compiler_params=params(40),
            cost_estimate=SHORT,
        )

    def place_q():
        r["q_down"], r["q_up"], *r["q_att"] = place(0, ("down", "up", "att"), "q", [], False)

    def place_f():
        r["down"], r["up"] = place(1, ("down", "up"), "f", [r["q_down"], r["q_up"]], False)

    def place_a():
        r["att"] = place(1, ("att",), "a", r["q_att"], True)

    kernels = {"attention": run_attention, "feed": run_feed, "back": run_back}
    plan.run(PLAN, kernels, {"place_q": place_q, "place_f": place_f, "place_a": place_a})
    down, up = r["down"], r["up"]
    gq, gk, gv, go, *smalls = r["att"]
    sbq, sbv, sbo, sg1, ss1, sbd, sg2, ss2, sbu = smalls
    return (
        q_out.reshape(qn, ql, h),
        r["p_out"].reshape(pn, plen, h),
        terms[:qn, 0],
        q_grad.reshape(qn, ql, h),
        r["p_grad"].reshape(pn, plen, h),
        gq, sbq, gk, gv, sbv, go, sbo, sg1, ss1, up, sbu, down, sbd, sg2, ss2,
    )


def solution(mesh):
    split = P(AXES)
    return jax.shard_map(
        functools.partial(shards, dict(mesh.shape)),
        mesh=mesh,
        in_specs=(split,) * 6 + (P(),) * 15,
        out_specs=(split,) * 5 + (P(),) * 15,
        check_vma=False,
    )
```

```python
import functools

import jax
import jax.numpy as jnp
import numpy as np
from jax import lax
from jax.experimental import pallas as pl
from jax.experimental.pallas import tpu as pltpu
from jax.sharding import PartitionSpec as P

HEADS = 8
HS = 64
EPS = 1e-06
F32 = jnp.float32
B16 = jnp.bfloat16
I32 = jnp.int32
HIGH = lax.Precision.HIGHEST
AXES = ("dp", "rep")
SCALE = 0.125
MIB = 1 << 20
FAR = -3e38
ANY = pl.BlockSpec(memory_space=pl.ANY)
SMEM = pl.BlockSpec(memory_space=pltpu.SMEM)
VMEM = pl.BlockSpec(memory_space=pltpu.VMEM)
PLAN = (
    "attention", "q", "feed", "q", "back", "q+f", "q", "f", "a", "q", "f", "q", "a", "f", "q", "a",
    "f", "a", "f", "a", "q", "a", "f", "q", "place_q", "a", "f", "place_f", "a",
)
SMALL = ("b_query", "b_value", "b_out", "gain_one", "shift_one", "b_down", "gain_two", "shift_two")
NSMALL = 12


def dot(a, b):
    return lax.dot_general(a, b, (((1,), (0,)), ((), ())), preferred_element_type=F32)


def dot_nt(a, b):
    return lax.dot_general(a, b, (((1,), (1,)), ((), ())), preferred_element_type=F32)


def dot_tn(a, b):
    return lax.dot_general(a, b, (((0,), (0,)), ((), ())), preferred_element_type=F32)


def dot_high(a, b):
    return lax.dot_general(
        a, b, (((1,), (0,)), ((), ())), precision=HIGH, preferred_element_type=F32
    )


def centred(v):
    c = v - jnp.mean(v, -1, keepdims=True)
    r = lax.rsqrt(jnp.mean(c * c, -1, keepdims=True) + EPS)
    return c * r, r


def norm_back(hat, r, gain, d_out):
    g_gain = jnp.sum(d_out * hat, 0, keepdims=True)
    g_shift = jnp.sum(d_out, 0, keepdims=True)
    d_hat = d_out * gain
    mean_a = jnp.mean(d_hat, -1, keepdims=True)
    mean_b = jnp.mean(d_hat * hat, -1, keepdims=True)
    return r * (d_hat - mean_a - hat * mean_b), g_gain, g_shift


def gelu_pair(x):
    phi = 0.5 + 0.5 * lax.erf(x * 0.7071067811865476)
    return x * phi, phi + x * (jnp.exp(x * x * -0.5) * 0.3989422804014327)


def stacked(x, group):
    lane = lax.broadcasted_iota(I32, x.shape, 1) // HS
    zero = jnp.zeros_like(x)
    return jnp.concatenate([jnp.where(lane == g, x, zero) for g in range(group)], 0)


def diagonal(o, group):
    rows = o.shape[0] // group
    lane = lax.broadcasted_iota(I32, (rows, o.shape[1]), 1) // HS
    out = o[:rows]
    for g in range(1, group):
        out = jnp.where(lane == g, o[g * rows : (g + 1) * rows], out)
    return out


def softmax(s):
    e = jnp.exp(s - jnp.max(s, -1, keepdims=True))
    return e * (1.0 / jnp.sum(e, -1, keepdims=True))


def attend(q, k, v, group, keep_probs, length=None):
    wide = HS * group
    parts = []
    for t in range(HEADS // group):
        at = slice(t * wide, (t + 1) * wide)
        scores = dot_nt(stacked(q[:, at], group), k[:, at])
        if length:
            rows = lax.broadcasted_iota(I32, scores.shape, 0) % q.shape[0]
            apart = rows // length != lax.broadcasted_iota(I32, scores.shape, 1) // length
            scores = jnp.where(apart, FAR, scores)
        probs = softmax(scores).astype(B16)
        keep_probs(t, probs)
        parts.append(diagonal(dot(probs, v[:, at]), group))
    return jnp.concatenate(parts, 1).astype(B16)


def attend_back(q, k, v, d_att, group, probs_of):
    wide = HS * group
    dq, dk, dv = [], [], []
    for t in range(HEADS // group):
        at = slice(t * wide, (t + 1) * wide)
        probs = probs_of(t)
        d_stack = stacked(d_att[:, at], group)
        d_probs = dot_nt(d_stack, v[:, at])
        dv.append(dot_tn(probs, d_stack))
        p32 = probs.astype(F32)
        inside = jnp.sum(p32 * d_probs, -1, keepdims=True)
        d_scores = (p32 * (d_probs - inside)).astype(B16)
        dq.append(diagonal(dot(d_scores, k[:, at]), group) * SCALE)
        dk.append(dot_tn(d_scores, stacked(q[:, at], group)))
    return tuple(jnp.concatenate(x, 1).astype(B16) for x in (dq, dk, dv))


def feed(first, w_up, b_up, w_down, b_down, gain, shift, keep, tile=512):
    hat, r = centred(first)
    normed = hat * gain + shift
    low = normed.astype(B16)
    second = normed + b_down
    for j in range(w_up.shape[1] // tile):
        at = slice(j * tile, (j + 1) * tile)
        act, slope = gelu_pair(dot(low, w_up[:, at]) + b_up[:, at])
        act = act.astype(B16)
        keep(at, act, slope)
        second = second + dot(act, w_down[at, :])
    return second, hat, r, low


def feed_both(first, w_up, b_up, w_down, b_down, g1, s1, g2, s2, d_out, slopes, keep_act, keep_inner):
    def keep(at, act, slope):
        keep_act(at, act)
        slopes[:, at] = slope

    ff = w_up.shape[1]
    second, hat, r, low = feed(first, w_up, b_up, w_down, b_down, g1, s1, keep, ff)
    hat2, r2 = centred(second)
    out = (hat2 * g2 + s2).astype(B16)
    d_second, gg2, gs2 = norm_back(hat2, r2, g2, d_out)
    d_down = d_second.astype(B16)
    gb_down = jnp.sum(d_down.astype(F32), 0, keepdims=True)
    d = (dot_nt(d_down, w_down[...]) * slopes[...]).astype(B16)
    keep_inner(slice(0, ff), d)
    gb_up = jnp.sum(d.astype(F32), 0, keepdims=True)
    gb_up = [gb_up[:, j * 512 : (j + 1) * 512] for j in range(ff // 512)]
    d_normed = d_second + dot_nt(d, w_up[...])
    d_first, gg1, gs1 = norm_back(hat, r, g1, d_normed)
    return out, d_down, d_first, low, (gg1, gs1, gb_down, gg2, gs2, *gb_up)


def cls_rows(q, k, v, count):
    total, width = q.shape
    length = total // count
    rows = count * HEADS
    own = (
        lax.broadcasted_iota(I32, (rows, width), 1) // HS
        == lax.broadcasted_iota(I32, (rows, width), 0) % HEADS
    )
    first = [
        jnp.broadcast_to(q[i * length : i * length + 1, :].astype(F32), (HEADS, width))
        for i in range(count)
    ]
    q_rows = jnp.where(own, jnp.concatenate(first, 0), 0.0).astype(B16)
    scores = dot_nt(q_rows, k[...])
    apart = (
        lax.broadcasted_iota(I32, scores.shape, 0) // HEADS
        != lax.broadcasted_iota(I32, scores.shape, 1) // length
    )
    probs = softmax(jnp.where(apart, FAR, scores)).astype(B16)
    mixed = jnp.where(own, dot(probs, v[...]), 0.0)
    return jnp.concatenate(
        [
            jnp.sum(mixed[i * HEADS : (i + 1) * HEADS], 0, keepdims=True)
            for i in range(count)
        ],
        0,
    )


def own_index(n):
    return lax.axis_index("dp") * lax.axis_size("rep") + lax.axis_index("rep")


def row(ref, e):
    return ref[e : e + 1, :]


def front_kernel(
    positives, counts, bq, bv, bo, g1, s1, bu, bd, g2, s2, p_x, q_x, wq, wk, wv, wo, wu, wd,
    pq, pk, pv, qq, qk, qv, payload,
    p_s, q_s, wqkv_s, wo_s, wu_s, wd_s, p_out, q_out, pay_s, sems, out_sems,
):
    width = q_x.shape[1]
    count = 4

    def load(i, src, dst):
        return pltpu.make_async_copy(src, dst, sems.at[i])

    w_in = (wq, wk, wv)
    first_in = [load(0, p_x, p_s)]
    first_in += [load(1 + i, w.at[1], wqkv_s.at[1, i]) for i, w in enumerate(w_in)]
    q_in = [load(4, q_x, q_s)]
    q_in += [load(5 + i, w.at[0], wqkv_s.at[0, i]) for i, w in enumerate(w_in)]
    later = [load(8, wo, wo_s), load(9, wu, wu_s), load(10, wd, wd_s)]
    for c in first_in + q_in + later:
        c.start()

    def project(x, e, held, targets):
        copies = []
        for i, (bias, target) in enumerate(zip((bq, None, bv), targets)):
            y = dot(x[...], wqkv_s[e, i])
            y = (y if bias is None else y + row(bias, e)).astype(B16)
            held[i] = y * SCALE if i == 0 else y
            copies.append(pltpu.make_async_copy(held.at[i], target, out_sems.at[3 * e + i]))
            copies[-1].start()
        return copies

    for c in first_in:
        c.wait()
    out = project(p_s, 1, p_out, (pq, pk, pv))
    for c in q_in:
        c.wait()
    out += project(q_s, 0, q_out, (qq, qk, qv))

    pay_s[...] = jnp.zeros_like(pay_s)
    lanes = lax.broadcasted_iota(I32, (1, width), 1)
    for i in range(count):
        mask = jnp.zeros((1, width), F32)
        for j in range(positives.shape[1]):
            mask = jnp.where((lanes == positives[i, j]) & (j < counts[i]), 1.0, mask)
        pay_s[8 + i : 9 + i, :] = mask
    att = [cls_rows(held.at[0], held.at[1], held.at[2], count) for held in (p_out, q_out)]
    for c in later:
        c.wait()
    for e, start, mixed, x in ((1, 0, att[0], p_s), (0, 4, att[1], q_s)):
        length = x.shape[0] // count
        own = [x[i * length : i * length + 1, :].astype(F32) for i in range(count)]
        zero = [jnp.zeros((4, width), F32)]
        mixed = jnp.concatenate([mixed] + zero, 0).astype(B16)
        first = jnp.concatenate(own + zero, 0) + dot(mixed, wo_s[e]) + row(bo, e)
        second, _, _, _ = feed(
            first, wu_s.at[e], row(bu, e), wd_s.at[e], row(bd, e), row(g1, e), row(s1, e),
            lambda at, act, slope: None, 2048,
        )
        done = centred(second)[0] * row(g2, e) + row(s2, e)
        pay_s[start : start + 4, :] = done[:4]
    payload[...] = pay_s[...].astype(B16)
    for c in out:
        c.wait()


def passage_attention_kernel(q, k, v, x, bo, wo, probs, att, first, wo_s, sem):
    copy = pltpu.make_async_copy(wo.at[1], wo_s, sem)

    @pl.when(pl.program_id(0) == 0)
    def _():
        copy.start()

    def keep_probs(t, value):
        probs[t] = value

    a = attend(q[...], k[...], v[...], 4, keep_probs)
    att[...] = a

    @pl.when(pl.program_id(0) == 0)
    def _():
        copy.wait()

    first[...] = x[...].astype(F32) + dot(a, wo_s[...]) + row(bo, 1)


def question_attention_kernel(length, q, k, v, x, bo, wo, probs, att, first):
    def keep_probs(t, value):
        probs[t] = value

    a = attend(q[...], k[...], v[...], 4, keep_probs, length)
    att[...] = a
    first[...] = x[...].astype(F32) + dot(a, wo[...]) + row(bo, 0)


def send_unit(wide, grads, table, keep, send, offset, sem_keep, sem_send):
    half, _, width = keep.shape
    blocks = 2 * half
    rows = grads.shape[0] * grads.shape[1] // (width * blocks)
    across = grads.shape[1] // width
    me = own_index(blocks)

    def start(out, base, sem):
        def body(r, carry):
            c = table[me, base + r]
            src = grads.at[
                pl.ds(pl.multiple_of(c // across * rows, rows), rows),
                pl.ds(pl.multiple_of(c % across * width, width), width),
            ] if wide else grads.at[pl.ds(pl.multiple_of(c * rows, rows), rows), :]
            pltpu.make_async_copy(src, out.at[r, pl.ds(offset, rows), :], sem).start()
            return carry

        lax.fori_loop(0, half, body, 0, unroll=True)

    start(send, half, sem_send)
    start(keep, 0, sem_keep)


def wait_units(keep, send, sem_keep, sem_send):
    pltpu.make_async_copy(send, send, sem_send).wait()
    pltpu.make_async_copy(keep, keep, sem_keep).wait()


def contrast(gathered, me, scale):
    z = jnp.concatenate([g[...] for g in gathered], 0)
    n = z.shape[0] // 16
    total_rows = 4 * n
    base = me * 4
    place = lax.broadcasted_iota(I32, (total_rows, z.shape[0]), 1)
    index = lax.broadcasted_iota(I32, (total_rows, z.shape[0]), 0)
    apart = (index // 4) ^ me
    block = jnp.zeros_like(apart)
    depth = n.bit_length() - 1
    for i in range(depth):
        block = block + (((apart >> i) & 1) << (depth - 1 - i))
    sel = block * 16 + index % 4

    def rows_at(k):
        return dot(jnp.where(place == sel + k, 1.0, 0.0).astype(B16), z)

    all_p, all_q, mask = rows_at(0), rows_at(4), rows_at(8)[:, :total_rows]
    sim = dot_nt(all_q.astype(B16), all_p.astype(B16)) * scale
    expo = jnp.exp(sim - jnp.max(sim, -1, keepdims=True))
    total = jnp.sum(expo, -1, keepdims=True)
    hit = mask * expo
    pos_total = jnp.sum(hit, -1, keepdims=True)
    terms = jnp.log(total) - jnp.log(pos_total)
    coeff = expo / total - hit / pos_total
    mine = jnp.where(
        lax.broadcasted_iota(I32, (8, total_rows), 1)
        == base + lax.broadcasted_iota(I32, (8, total_rows), 0),
        1.0,
        0.0,
    )
    d_q = dot_high(dot_high(mine, coeff), all_p) * scale
    d_p = dot_high(dot_high(mine, coeff.T), all_q) * scale
    return dot_high(mine, jnp.broadcast_to(terms, (total_rows, 128))), d_q, d_p


def question_back_kernel(
    table, gathered_a, gathered_b, x, cot, q, k, v, probs, att, first,
    g1, s1, bu, bd, g2, s2, wq, wk, wv, wo, wu, wd,
    terms, d_cls_p, x_grad, small, out, keep, send,
    wqkv_s, wo_s, wu_s, wd_s, act_s, slope_s, inner_s, g_down, g_up, g_att, sems, out_sems,
):
    copies = [
        pltpu.make_async_copy(src.at[0], dst, sems.at[i])
        for i, (src, dst) in enumerate(
            (
                (wu, wu_s),
                (wd, wd_s),
                (wo, wo_s),
                (wq, wqkv_s.at[0]),
                (wk, wqkv_s.at[1]),
                (wv, wqkv_s.at[2]),
            )
        )
    ]
    for c in copies:
        c.start()
    n = keep.shape[0] * 2
    rows = 2048 // n
    count = 4
    length = x.shape[0] // count
    width = x.shape[1]
    loss, d_q, d_p = contrast(
        (gathered_a, gathered_b), own_index(n), 2.0 / float(np.sqrt(width))
    )
    terms[...] = loss
    d_cls_p[...] = d_p
    place = lax.broadcasted_iota(I32, x.shape, 0)
    d_out = cot[...].astype(F32)
    for i in range(count):
        d_out = d_out + jnp.where(place == i * length, d_q[i : i + 1], 0.0)
    for c in copies[:2]:
        c.wait()

    def keep_act(at, value):
        act_s[:, at] = value

    def keep_inner(at, value):
        inner_s[:, at] = value

    out[...], d_down, d_first, low, sums = feed_both(
        first[...], wu_s, row(bu, 0), wd_s, row(bd, 0), row(g1, 0), row(s1, 0), row(g2, 0),
        row(s2, 0), d_out, slope_s, keep_act, keep_inner,
    )
    sems_out = (out_sems.at[0], out_sems.at[1])
    g_down[...] = dot_tn(act_s[...], d_down).astype(B16)
    send_unit(False, g_down, table, keep, send, 0, *sems_out)
    g_up[...] = dot_tn(low, inner_s[...]).astype(B16)
    send_unit(True, g_up, table, keep, send, rows, *sems_out)
    for c in copies[2:]:
        c.wait()
    d_branch = d_first.astype(B16)
    d_att = dot_nt(d_branch, wo_s[...]).astype(B16)
    dq, dk, dv = attend_back(q[...], k[...], v[...], d_att, 4, lambda t: probs[t])
    rows_x = x[...]
    for i, d in enumerate((dq, dk, dv)):
        g_att[i * width : (i + 1) * width, :] = dot_tn(rows_x, d).astype(B16)
    g_att[3 * width :, :] = dot_tn(att[...], d_branch).astype(B16)
    send_unit(False, g_att, table, keep, send, 2 * rows, *sems_out)
    x_grad[...] = (
        d_first + dot_nt(dq, wqkv_s[0]) + dot_nt(dk, wqkv_s[1]) + dot_nt(dv, wqkv_s[2])
    )
    small[...] = jnp.zeros_like(small)
    values = [jnp.sum(d.astype(F32), 0, keepdims=True) for d in (dq, dv, d_branch)]
    for i, value in enumerate((*values, *sums)):
        small[i : i + 1, :] = value
    wait_units(keep, send, *sems_out)


def passage_feed_kernel(
    steps, table, d_cls, g1, s1, bu, bd, g2, s2, cot, first, wu, wd,
    out, d_first, small, keep, send,
    cot_s, first_s, out_s, d_first_s,
    wu_s, wd_s, slope_s, act_s, inner_s, down_s, low_s, g_down, g_up, sems, back_sems, out_sems,
):
    b = pl.program_id(0)
    sems_out = (out_sems.at[0], out_sems.at[1])
    rows = 2048 // (2 * keep.shape[0])
    total_rows = act_s.shape[0]
    per = 4 // steps
    length = total_rows // steps

    def part(i):
        return pl.ds(pl.multiple_of(i * length, length), length)

    def load(i):
        return [
            pltpu.make_async_copy(first.at[part(i), :], first_s.at[part(i), :], sems.at[2 + 2 * i]),
            pltpu.make_async_copy(cot.at[part(i), :], cot_s.at[part(i), :], sems.at[3 + 2 * i]),
        ]

    def store(i):
        return [
            pltpu.make_async_copy(out_s.at[part(i), :], out.at[part(i), :], back_sems.at[2 * i]),
            pltpu.make_async_copy(
                d_first_s.at[part(i), :], d_first.at[part(i), :], back_sems.at[2 * i + 1]
            ),
        ]

    @pl.when(b < steps)
    def _():
        weights = [
            pltpu.make_async_copy(src, dst, sems.at[i])
            for i, (src, dst) in enumerate(((wu.at[1], wu_s), (wd.at[1], wd_s)))
        ]

        @pl.when(b == 0)
        def _():
            begin = load(0)
            for c in begin + weights + [c for i in range(1, steps) for c in load(i)]:
                c.start()
            small[...] = jnp.zeros_like(small)
            for c in begin + weights:
                c.wait()

        @pl.when(b > 0)
        def _():
            for c in load(b):
                c.wait()

        mine = part(b)
        place = lax.broadcasted_iota(I32, (length, cot_s.shape[1]), 0)
        d_out = cot_s[mine, :].astype(F32)
        for i in range(per):
            extra = d_cls[pl.ds(b * per + i, 1), :]
            d_out = d_out + jnp.where(place == i * (length // per), extra, 0.0)

        def keep_act(at, value):
            act_s[mine, at] = value

        def keep_inner(at, value):
            inner_s[mine, at] = value

        out_s[mine, :], down_s[mine, :], d_first_s[mine, :], low_s[mine, :], sums = feed_both(
            first_s[mine, :], wu_s, row(bu, 1), wd_s, row(bd, 1), row(g1, 1), row(s1, 1),
            row(g2, 1), row(s2, 1), d_out, slope_s, keep_act, keep_inner,
        )
        for i, value in enumerate(sums):
            small[3 + i : 4 + i, :] += value
        for c in store(b):
            c.start()

    @pl.when(b == steps)
    def _():
        g_down[...] = dot_tn(act_s[...], down_s[...]).astype(B16)
        send_unit(False, g_down, table, keep, send, 0, *sems_out)

    @pl.when(b == steps + 1)
    def _():
        g_up[...] = dot_tn(low_s[...], inner_s[...]).astype(B16)
        send_unit(True, g_up, table, keep, send, rows, *sems_out)
        for i in range(steps):
            for c in store(i):
                c.wait()
        wait_units(keep, send, *sems_out)


def passage_attention_back_kernel(
    table, small_q, small_p, d_first, q, k, v, probs, x, att, wq, wk, wv, wo,
    x_grad, keep, send,
    wqkv_s, wo_s, x_s, att_s, d_s, small, sent_s, g_att, sems, out_sems,
):
    b = pl.program_id(0)
    nb = pl.num_programs(0)
    length, width = d_first.shape
    n = 2 * keep.shape[0]
    rows = 2048 // n
    copies = [
        pltpu.make_async_copy(src, dst, sems.at[i])
        for i, (src, dst) in enumerate(
            (
                (wo.at[1], wo_s),
                (wq.at[1], wqkv_s.at[0]),
                (wk.at[1], wqkv_s.at[1]),
                (wv.at[1], wqkv_s.at[2]),
                (x, x_s),
                (att, att_s),
            )
        )
    ]

    @pl.when(b == 0)
    def _():
        for c in copies:
            c.start()
        small[...] = small_p[...]
        for c in copies[:4]:
            c.wait()

    d_branch = d_first[...].astype(B16)
    d_att = dot_nt(d_branch, wo_s[...]).astype(B16)
    dq, dk, dv = attend_back(q[...], k[...], v[...], d_att, 4, lambda t: probs[t])
    mine = pl.ds(pl.multiple_of(b * length, length), length)
    for i, d in enumerate((dq, dk, dv, d_branch)):
        d_s[i, mine, :] = d
    for i, d in enumerate((dq, dv, d_branch)):
        small[i : i + 1, :] += jnp.sum(d.astype(F32), 0, keepdims=True)
    x_grad[...] = (
        d_first[...] + dot_nt(dq, wqkv_s[0]) + dot_nt(dk, wqkv_s[1]) + dot_nt(dv, wqkv_s[2])
    )

    @pl.when(b == nb - 1)
    def _():
        sent_s[...] = jnp.zeros_like(sent_s)
        top = lax.broadcasted_iota(I32, (16, width), 0) == 0
        for e, ref in enumerate((small_q, small)):
            for i in range(NSMALL):
                sent_s[e * NSMALL + i] = jnp.where(top, ref[i : i + 1, :], 0.0).astype(B16)
        me = own_index(n)
        for base, out, sem in ((n // 2, send, out_sems.at[1]), (0, keep, out_sems.at[0])):

            def body(r, carry, base=base, out=out, sem=sem):
                pltpu.make_async_copy(
                    sent_s.at[table[me, base + r]], out.at[r, pl.ds(rows, 16), :], sem
                ).start()
                return carry

            lax.fori_loop(0, n // 2, body, 0, unroll=True)
        for c in copies[4:]:
            c.wait()
        for i in range(3):
            g_att[i * width : (i + 1) * width, :] = dot_tn(x_s[...], d_s[i]).astype(B16)
        g_att[3 * width :, :] = dot_tn(att_s[...], d_s[3]).astype(B16)
        send_unit(False, g_att, table, keep, send, 0, out_sems.at[0], out_sems.at[1])
        wait_units(keep, send, out_sems.at[0], out_sems.at[1])


def place_kernel(e, kinds, starts, n_alias, with_small, *refs):
    table = refs[0]
    pieces = refs[1 : 1 + len(starts)]
    outs = refs[1 + len(starts) + n_alias :]
    n_out = sum(4 if kind == "att" else 1 for kind in kinds)
    n_small = 9 if with_small else 0
    targets, smalls = outs[:n_out], outs[n_out : n_out + n_small]
    scratch = outs[n_out + n_small :]
    stages, sems = scratch[: len(kinds)], scratch[len(kinds)]
    small_s = scratch[len(kinds) + 1] if with_small else None
    n = starts[-1] + pieces[-1].shape[0]
    rows = 2048 // n
    me = own_index(n)
    for piece, start in zip(pieces, starts):

        def body(r, carry, piece=piece, start=start):
            c = table[me, start + r]
            k = 0
            for u, kind in enumerate(kinds):
                stage = stages[u].at[start + r]
                stage[...] = piece[r, u * rows : (u + 1) * rows, :].astype(F32)
                if kind == "down":
                    pltpu.make_async_copy(
                        stage,
                        targets[k].at[e, pl.ds(pl.multiple_of(c * rows, rows), rows), :],
                        sems.at[k],
                    ).start()
                    k += 1
                elif kind == "up":
                    pltpu.make_async_copy(
                        stage,
                        targets[k].at[
                            e,
                            pl.ds(pl.multiple_of(c // 4 * rows, rows), rows),
                            pl.ds(pl.multiple_of(c % 4 * 512, 512), 512),
                        ],
                        sems.at[k],
                    ).start()
                    k += 1
                else:
                    quarter = n // 4
                    for m in range(4):

                        @pl.when(c // quarter == m)
                        def _(m=m, k=k, stage=stage):
                            at = pl.ds(pl.multiple_of(c % quarter * rows, rows), rows)
                            pltpu.make_async_copy(
                                stage, targets[k + m].at[e, at, :], sems.at[k + m]
                            ).start()

                    k += 4
            if with_small:
                block = piece[r, len(kinds) * rows : len(kinds) * rows + 16, :].astype(F32)
                small_s[c] = block[0:8]
            return carry

        lax.fori_loop(0, piece.shape[0], body, 0, unroll=True)
    if with_small:
        for f in range(2):
            for i in range(8):
                smalls[i][f : f + 1, :] = small_s[f * NSMALL + i, 0:1, :]
            for j in range(4):
                smalls[8][f : f + 1, j * 512 : (j + 1) * 512] = small_s[f * NSMALL + 8 + j, 0:1, :]
    for k, target in enumerate(targets):
        pltpu.make_async_copy(target.at[e], target.at[e], sems.at[k]).wait()


def rounds_of(mesh_shape):
    dp, rep = mesh_shape["dp"], mesh_shape["rep"]
    core, *x = [1 << i for i in range(rep.bit_length() - 1)]
    y, *z = [rep << i for i in range(dp.bit_length() - 1)]
    return ([core, *x, y, *z], [core, y, *x, *z]), ([core, *x, y, *z], [core, y, *z, *x])


def order_table(rounds, n):
    depth = len(rounds[0])
    table = np.zeros((n, n), np.int32)
    for d in range(n):
        for r in range(n):
            c = d ^ (rounds[0][0] if r >> (depth - 1) & 1 else 0)
            for k in range(1, depth):
                if r >> (depth - 1 - k) & 1:
                    c ^= rounds[c & 1][k]
            table[d, r] = c
    return table


def exchange(x, masks, n):
    return lax.ppermute(x, AXES, [(d, d ^ masks[d & 1]) for d in range(n)])


def total(parts):
    return sum(p.astype(F32) for p in parts).astype(B16)


def steps_of(rounds, pairs):
    even, odd = rounds
    steps, k = [], 0
    while k < len(even):
        if even[k] in pairs:
            steps.append(((even[k], odd[k]), (even[k + 1], odd[k + 1])))
            k += 2
        else:
            steps.append(((even[k], odd[k]),))
            k += 1
    return steps


def partners(step):
    if len(step) == 1:
        return [step[0]]
    high, low = step
    return [low, high, (low[0] ^ high[0], low[1] ^ high[1])]


def join_kernel(*refs):
    *parts, out = refs
    m = parts[0].shape[0]
    for i, part in enumerate(parts):
        out[i * m : (i + 1) * m] = part[...]


def joined(order, pieces, limit=24):
    m, rows, width = pieces[0].shape
    count = len(pieces)
    return order(
        join_kernel,
        *pieces,
        name="join",
        in_specs=[VMEM] * count,
        out_specs=[VMEM],
        out_shape=[shape((count * m, rows, width), B16)],
        compiler_params=params(limit),
        cost_estimate=SHORT,
    )


class Order:
    def __init__(self):
        self.token = None

    def fence(self, arrays):
        *arrays, self.token = lax.optimization_barrier((*arrays, self.token))
        return arrays

    def __call__(self, kernel, *operands, in_specs, out_specs, out_shape, **kwargs):
        skip = 0 if self.token is None else 1
        last = skip + len(operands) + len(out_shape)

        def body(*refs):
            kernel(*refs[skip:last], *refs[last + 1 :])

        aliases = kwargs.pop("input_output_aliases", {})
        call = pl.pallas_call(
            body,
            in_specs=[ANY] * skip + in_specs,
            out_specs=list(out_specs) + [ANY],
            out_shape=list(out_shape) + [shape((8, 128))],
            input_output_aliases={k + skip: v for k, v in aliases.items()},
            **kwargs,
        )
        *outs, self.token = call(*([self.token] if skip else []), *operands)
        return outs


class Sum:
    def __init__(self, order, halving, doubling, n, keep, send):
        self.order, self.n = order, n
        self.halving, self.doubling = list(halving), list(doubling)
        self.parts, self.m, self.pieces = [keep], keep.shape[0], None
        self.got, self.out, self.now = None, [send], self.halving.pop(0)
        self.going = True

    def start(self):
        masks = partners(self.now)
        if self.pieces is None:
            self.got = [exchange(x, m, self.n) for x, m in zip(self.out, masks)]
        else:
            self.got = [exchange(x, m, self.n) for m in masks for x in self.out]

    def take(self):
        if self.pieces is None:
            self.parts += self.got
            if self.halving:
                self.now = self.halving.pop(0)
                ways = 2 ** len(self.now)
                q = self.m // ways
                self.out = [
                    total([p[i * q : (i + 1) * q] for p in self.parts]) for i in range(1, ways)
                ]
                self.m = q
                return True
            self.out = self.pieces = [total([p[:1] for p in self.parts])]
        else:
            self.pieces = self.pieces + self.got
            if not self.doubling:
                return False
            if len(self.doubling) > 1:
                self.pieces = [jnp.concatenate(self.pieces, 0)]
            self.out = self.pieces
        self.now = self.doubling.pop()
        return True


class Plan:
    def __init__(self, order):
        self.order, self.sums, self.starting = order, {}, []
        self.fresh = True

    def add(self, name, item):
        self.sums[name] = item
        self.starting.append(item)

    def flush(self):
        if not self.starting:
            return
        flat = self.order.fence([x for s in self.starting for x in s.out])
        for s in self.starting:
            s.out, flat = flat[: len(s.out)], flat[len(s.out) :]
            if s.pieces is not None:
                s.pieces = s.out
        for s in self.starting:
            s.start()
        self.starting = []

    def step(self, names):
        if not self.fresh:
            self.flush()
        items = [self.sums[name] for name in names if self.sums[name].going]
        flat = self.order.fence([x for s in items for x in s.got])
        for s in items:
            s.got, flat = flat[: len(s.got)], flat[len(s.got) :]
        for s in items:
            s.going = s.take()
            if s.going:
                self.starting.append(s)
        self.fresh = False

    def run(self, names, kernels, places):
        for name in names:
            if name in kernels:
                self.flush()
                kernels[name]()
                self.fresh = True
            elif name in places:
                self.flush()
                if not self.sums[name[-1]].going:
                    places.pop(name)()
            else:
                self.step(name.split("+"))
        while any(s.going for s in self.sums.values()):
            for name, item in self.sums.items():
                if item.going:
                    self.step([name])
        self.flush()
        for place in places.values():
            place()


class Gather:
    def __init__(self, order, x, n):
        bits = [1 << i for i in reversed(range(n.bit_length() - 1))]
        assert len(bits) % 2 == 1
        self.order, self.n = order, n
        self.stages = [bits[i : i + 2] for i in range(0, len(bits), 2)]
        self.pieces = [x[None]]
        self.issue()

    def issue(self):
        (mine,) = self.order.fence(self.pieces)
        now = self.stages.pop(0)
        masks = now if len(now) == 1 else [now[0], now[1], now[0] | now[1]]
        self.pieces = [mine] + [
            lax.ppermute(mine, AXES, [(d, d ^ m) for d in range(self.n)]) for m in masks
        ]

    def step(self):
        self.pieces = joined(self.order, self.order.fence(self.pieces), 62)
        self.issue()

    def result(self):
        return self.order.fence(self.pieces)


def params(limit):
    return pltpu.CompilerParams(vmem_limit_bytes=limit * MIB)


LONG = pl.CostEstimate(flops=200_000_000_000, bytes_accessed=1000, transcendentals=0)


SHORT = pl.CostEstimate(flops=1000, bytes_accessed=1000, transcendentals=0)


def shape(dims, dtype=F32):
    return jax.ShapeDtypeStruct(dims, dtype)


def sem(count):
    return pltpu.SemaphoreType.DMA((count,))


def shards(
    mesh_shape,
    q_tokens,
    p_tokens,
    q_cotangent,
    p_cotangent,
    positives,
    counts,
    wq,
    bq,
    wk,
    wv,
    bv,
    wo,
    bo,
    g1,
    s1,
    wu,
    bu,
    wd,
    bd,
    g2,
    s2,
):
    n = mesh_shape["dp"] * mesh_shape["rep"]
    plane, mixed = rounds_of(mesh_shape)
    pairs = plane[0][-2:-1]
    table = jnp.asarray(order_table(plane, n))
    mixed_table = jnp.asarray(order_table(mixed, n))
    qn, ql, h = q_tokens.shape
    pn, plen, _ = p_tokens.shape
    ff = wu.shape[2]
    qr, pr = qn * ql, pn * plen
    assert qn == 4 and pn == 4 and h == 512 and ff == 2048 and 24 <= n and 4 * n <= h
    q_x, p_x = q_tokens.reshape(qr, h), p_tokens.reshape(pr, h)
    q_cot, p_cot = q_cotangent.reshape(qr, h), p_cotangent.reshape(pr, h)
    order = Order()

    def whole(*dims):
        return pl.BlockSpec(dims, lambda b: (0,) * len(dims))

    one, wide = whole(2, h), whole(2, ff)
    seq_block = pl.BlockSpec((plen, h), lambda b: (b, 0))
    pq, pk, pv, qq, qk, qv, payload = order(
        front_kernel,
        positives, counts, bq, bv, bo, g1, s1, bu, bd, g2, s2, p_x, q_x, wq, wk, wv, wo, wu, wd,
        name="front",
        in_specs=[SMEM] * 2 + [VMEM] * 9 + [ANY] * 8,
        out_specs=[ANY] * 6 + [VMEM],
        out_shape=[shape((pr, h), B16)] * 3 + [shape((qr, h), B16)] * 3 + [shape((16, h), B16)],
        scratch_shapes=[
            pltpu.VMEM((pr, h), B16),
            pltpu.VMEM((qr, h), B16),
            pltpu.VMEM((2, 3, h, h), B16),
            pltpu.VMEM((2, h, h), B16),
            pltpu.VMEM((2, h, ff), B16),
            pltpu.VMEM((2, ff, h), B16),
            pltpu.VMEM((3, pr, h), B16),
            pltpu.VMEM((3, qr, h), B16),
            pltpu.VMEM((16, h), F32),
            sem(11),
            sem(6),
        ],
        compiler_params=params(62),
        cost_estimate=LONG,
    )
    gather = Gather(order, payload, n)

    def passages(kernel, name, at, count, operands, in_specs, outs, before, **kwargs):
        def spec(block):
            if not isinstance(block, tuple):
                return block
            axis = block.index(None) if None in block else len(block) - 2
            return pl.BlockSpec(
                block, lambda b: tuple(b + at if i == axis else 0 for i in range(len(block)))
            )

        n_in, n_before = len(operands), len(before)

        def body(*refs):
            kernel(*refs[:n_in], *refs[n_in + n_before :])

        return order(
            body,
            *operands,
            *before,
            name=name,
            grid=(count,),
            in_specs=[spec(x) for x in in_specs] + [ANY] * n_before,
            out_specs=[spec(block) for block, _ in outs],
            out_shape=[s for _, s in outs],
            input_output_aliases={n_in + i: i for i in range(n_before)},
            compiler_params=params(62),
            cost_estimate=LONG,
            **kwargs,
        )

    seq, seq_wide = (plen, h), (plen, ff)
    probs_block = (None, 2, 4 * plen, plen)

    def attention(at, count, before):
        return passages(
            passage_attention_kernel, "passage_attention", at, count,
            (pq, pk, pv, p_x, bo, wo),
            [seq] * 4 + [one, ANY],
            [
                (probs_block, shape((pn, 2, 4 * plen, plen), B16)),
                (seq, shape((pr, h), B16)),
                (seq, shape((pr, h))),
            ],
            before,
            scratch_shapes=[pltpu.VMEM((h, h), B16), pltpu.SemaphoreType.DMA],
        )

    part = attention(0, 2, [])
    gather.step()
    q_probs, q_att, q_first = order(
        functools.partial(question_attention_kernel, ql),
        qq, qk, qv, q_x, bo, wo,
        name="question_attention",
        grid=(1,),
        in_specs=[whole(qr, h)] * 4 + [one, pl.BlockSpec((None, h, h), lambda b: (0, 0, 0))],
        out_specs=[whole(2, 4 * qr, qr), whole(qr, h), whole(qr, h)],
        out_shape=[shape((2, 4 * qr, qr), B16), shape((qr, h), B16), shape((qr, h))],
        compiler_params=params(62),
        cost_estimate=LONG,
    )
    while gather.stages:
        gather.step()
    gathered = [x.reshape(-1, h) for x in gather.result()]

    rows = 2048 // n
    half = n // 2
    terms, d_cls_p, q_grad, small_q, q_out, q_keep, q_send = order(
        question_back_kernel,
        mixed_table, *gathered, q_x, q_cot, qq, qk, qv, q_probs, q_att, q_first,
        g1, s1, bu, bd, g2, s2, wq, wk, wv, wo, wu, wd,
        name="question_back",
        in_specs=[SMEM] + [VMEM] * 16 + [ANY] * 6,
        out_specs=[VMEM] * 5 + [ANY] * 2,
        out_shape=[
            shape((8, 128)),
            shape((8, h)),
            shape((qr, h)),
            shape((16, h)),
            shape((qr, h), B16),
            shape((half, 3 * rows, h), B16),
            shape((half, 3 * rows, h), B16),
        ],
        scratch_shapes=[
            pltpu.VMEM((3, h, h), B16),
            pltpu.VMEM((h, h), B16),
            pltpu.VMEM((h, ff), B16),
            pltpu.VMEM((ff, h), B16),
            pltpu.VMEM((qr, ff), B16),
            pltpu.VMEM((qr, ff), F32),
            pltpu.VMEM((qr, ff), B16),
            pltpu.VMEM((ff, h), B16),
            pltpu.VMEM((h, ff), B16),
            pltpu.VMEM((4 * h, h), B16),
            sem(6),
            sem(2),
        ],
        compiler_params=params(62),
        cost_estimate=LONG,
    )
    steps = steps_of(plane, pairs)
    plan = Plan(order)
    plan.add("q", Sum(order, steps_of(mixed, ()), steps, n, q_keep, q_send))
    r = {}

    def run_attention():
        r["p_probs"], r["p_att"], r["p_first"] = attention(2, 2, part)

    parts_of = 2
    def run_feed():
        r["p_out"], r["d_first"], r["small_p"], *out = order(
            functools.partial(passage_feed_kernel, parts_of),
            table, d_cls_p, g1, s1, bu, bd, g2, s2, p_cot, r["p_first"], wu, wd,
            name="passage_feed",
            grid=(parts_of + 2,),
            in_specs=[SMEM, whole(8, h), one, one, wide, one, one, one] + [ANY] * 4,
            out_specs=[ANY, ANY, whole(16, h), ANY, ANY],
            out_shape=[shape((pr, h), B16), shape((pr, h)), shape((16, h))]
            + [shape((half, 2 * rows, h), B16)] * 2,
            scratch_shapes=[
                pltpu.VMEM((pr, h), B16),
                pltpu.VMEM((pr, h), F32),
                pltpu.VMEM((pr, h), B16),
                pltpu.VMEM((pr, h), F32),
                pltpu.VMEM((h, ff), B16),
                pltpu.VMEM((ff, h), B16),
                pltpu.VMEM((pr // parts_of, ff), F32),
                pltpu.VMEM((pr, ff), B16),
                pltpu.VMEM((pr, ff), B16),
                pltpu.VMEM((pr, h), B16),
                pltpu.VMEM((pr, h), B16),
                pltpu.VMEM((ff, h), B16),
                pltpu.VMEM((h, ff), B16),
                sem(2 + 2 * parts_of),
                sem(2 * parts_of),
                sem(2),
            ],
            compiler_params=params(62),
            cost_estimate=LONG,
        )
        plan.add("f", Sum(order, steps, steps, n, *out))

    def run_back():
        r["p_grad"], *out = order(
            passage_attention_back_kernel,
            table, small_q, r["small_p"], r["d_first"], pq, pk, pv, r["p_probs"], p_x, r["p_att"], wq, wk, wv, wo,
            name="passage_attention_back",
            grid=(pn,),
            in_specs=[SMEM, whole(16, h), whole(16, h)] + [seq_block] * 4
            + [pl.BlockSpec(probs_block, lambda b: (b, 0, 0, 0))] + [ANY] * 6,
            out_specs=[seq_block, ANY, ANY],
            out_shape=[shape((pr, h))] + [shape((half, rows + 16, h), B16)] * 2,
            scratch_shapes=[
                pltpu.VMEM((3, h, h), B16),
                pltpu.VMEM((h, h), B16),
                pltpu.VMEM((pr, h), B16),
                pltpu.VMEM((pr, h), B16),
                pltpu.VMEM((4, pr, h), B16),
                pltpu.VMEM((16, h), F32),
                pltpu.VMEM((n, 16, h), B16),
                pltpu.VMEM((4 * h, h), B16),
                sem(6),
                sem(2),
            ],
            compiler_params=params(62),
            cost_estimate=LONG,
        )
        plan.add("a", Sum(order, steps, steps, n, *out))

    def place(e, kinds, which, before, with_small):
        pieces = plan.sums[which].pieces
        starts, at = [], 0
        for piece in pieces:
            starts.append(at)
            at += piece.shape[0]
        dims = []
        for kind in kinds:
            dims += {"down": [(2, ff, h)], "up": [(2, h, ff)], "att": [(2, h, h)] * 4}[kind]
        outs = [shape(d) for d in dims]
        smalls = [shape((2, h))] * 8 + [shape((2, ff))] if with_small else []
        return order(
            functools.partial(
                place_kernel, e, kinds, tuple(starts), len(before), with_small
            ),
            table, *pieces, *before,
            name="place",
            in_specs=[SMEM] + [VMEM] * len(pieces) + [ANY] * len(before),
            out_specs=[ANY] * len(outs) + [VMEM] * len(smalls),
            out_shape=outs + smalls,
            input_output_aliases={1 + len(pieces) + i: i for i in range(len(before))},
            scratch_shapes=[pltpu.VMEM((n, rows, h), F32) for _ in kinds]
            + [sem(len(outs))]
            + ([pltpu.VMEM((n, 8, h), F32)] if with_small else []),
            compiler_params=params(40),
            cost_estimate=SHORT,
        )

    def place_q():
        r["q_down"], r["q_up"], *r["q_att"] = place(0, ("down", "up", "att"), "q", [], False)

    def place_f():
        r["down"], r["up"] = place(1, ("down", "up"), "f", [r["q_down"], r["q_up"]], False)

    def place_a():
        r["att"] = place(1, ("att",), "a", r["q_att"], True)

    kernels = {"attention": run_attention, "feed": run_feed, "back": run_back}
    plan.run(PLAN, kernels, {"place_q": place_q, "place_f": place_f, "place_a": place_a})
    down, up = r["down"], r["up"]
    gq, gk, gv, go, *smalls = r["att"]
    sbq, sbv, sbo, sg1, ss1, sbd, sg2, ss2, sbu = smalls
    return (
        q_out.reshape(qn, ql, h),
        r["p_out"].reshape(pn, plen, h),
        terms[:qn, 0],
        q_grad.reshape(qn, ql, h),
        r["p_grad"].reshape(pn, plen, h),
        gq, sbq, gk, gv, sbv, go, sbo, sg1, ss1, up, sbu, down, sbd, sg2, ss2,
    )


def solution(mesh):
    split = P(AXES)
    return jax.shard_map(
        functools.partial(shards, dict(mesh.shape)),
        mesh=mesh,
        in_specs=(split,) * 6 + (P(),) * 15,
        out_specs=(split,) * 5 + (P(),) * 15,
        check_vma=False,
    )
```

```python
import functools

import jax
import jax.numpy as jnp
import numpy as np
from jax import lax
from jax.experimental import pallas as pl
from jax.experimental.pallas import tpu as pltpu
from jax.sharding import PartitionSpec as P

HEADS = 8
HS = 64
EPS = 1e-06
F32 = jnp.float32
B16 = jnp.bfloat16
I32 = jnp.int32
HIGH = lax.Precision.HIGHEST
AXES = ("dp", "rep")
SCALE = 0.125
MIB = 1 << 20
FAR = -3e38
ANY = pl.BlockSpec(memory_space=pl.ANY)
SMEM = pl.BlockSpec(memory_space=pltpu.SMEM)
VMEM = pl.BlockSpec(memory_space=pltpu.VMEM)
PLAN = (
    "attention", "q", "feed", "q", "back", "q+f", "q", "f", "a", "q", "f", "q", "a", "f", "q", "a",
    "f", "a", "f", "a", "q", "a", "f", "q", "place_q", "a", "f", "place_f", "a",
)
SMALL = ("b_query", "b_value", "b_out", "gain_one", "shift_one", "b_down", "gain_two", "shift_two")
NSMALL = 12


def dot(a, b):
    return lax.dot_general(a, b, (((1,), (0,)), ((), ())), preferred_element_type=F32)


def dot_nt(a, b):
    return lax.dot_general(a, b, (((1,), (1,)), ((), ())), preferred_element_type=F32)


def dot_tn(a, b):
    return lax.dot_general(a, b, (((0,), (0,)), ((), ())), preferred_element_type=F32)


def dot_high(a, b):
    return lax.dot_general(
        a, b, (((1,), (0,)), ((), ())), precision=HIGH, preferred_element_type=F32
    )


def centred(v):
    c = v - jnp.mean(v, -1, keepdims=True)
    r = lax.rsqrt(jnp.mean(c * c, -1, keepdims=True) + EPS)
    return c * r, r


def norm_back(hat, r, gain, d_out):
    g_gain = jnp.sum(d_out * hat, 0, keepdims=True)
    g_shift = jnp.sum(d_out, 0, keepdims=True)
    d_hat = d_out * gain
    mean_a = jnp.mean(d_hat, -1, keepdims=True)
    mean_b = jnp.mean(d_hat * hat, -1, keepdims=True)
    return r * (d_hat - mean_a - hat * mean_b), g_gain, g_shift


def gelu_pair(x):
    phi = 0.5 + 0.5 * lax.erf(x * 0.7071067811865476)
    return x * phi, phi + x * (jnp.exp(x * x * -0.5) * 0.3989422804014327)


def stacked(x, group):
    lane = lax.broadcasted_iota(I32, x.shape, 1) // HS
    zero = jnp.zeros_like(x)
    return jnp.concatenate([jnp.where(lane == g, x, zero) for g in range(group)], 0)


def diagonal(o, group):
    rows = o.shape[0] // group
    lane = lax.broadcasted_iota(I32, (rows, o.shape[1]), 1) // HS
    out = o[:rows]
    for g in range(1, group):
        out = jnp.where(lane == g, o[g * rows : (g + 1) * rows], out)
    return out


def softmax(s):
    e = jnp.exp(s - jnp.max(s, -1, keepdims=True))
    return e * (1.0 / jnp.sum(e, -1, keepdims=True))


def attend(q, k, v, group, keep_probs, length=None):
    wide = HS * group
    parts = []
    for t in range(HEADS // group):
        at = slice(t * wide, (t + 1) * wide)
        scores = dot_nt(stacked(q[:, at], group), k[:, at])
        if length:
            rows = lax.broadcasted_iota(I32, scores.shape, 0) % q.shape[0]
            apart = rows // length != lax.broadcasted_iota(I32, scores.shape, 1) // length
            scores = jnp.where(apart, FAR, scores)
        probs = softmax(scores).astype(B16)
        keep_probs(t, probs)
        parts.append(diagonal(dot(probs, v[:, at]), group))
    return jnp.concatenate(parts, 1).astype(B16)


def attend_back(q, k, v, d_att, group, probs_of):
    wide = HS * group
    dq, dk, dv = [], [], []
    for t in range(HEADS // group):
        at = slice(t * wide, (t + 1) * wide)
        probs = probs_of(t)
        d_stack = stacked(d_att[:, at], group)
        d_probs = dot_nt(d_stack, v[:, at])
        dv.append(dot_tn(probs, d_stack))
        p32 = probs.astype(F32)
        inside = jnp.sum(p32 * d_probs, -1, keepdims=True)
        d_scores = (p32 * (d_probs - inside)).astype(B16)
        dq.append(diagonal(dot(d_scores, k[:, at]), group) * SCALE)
        dk.append(dot_tn(d_scores, stacked(q[:, at], group)))
    return tuple(jnp.concatenate(x, 1).astype(B16) for x in (dq, dk, dv))


def feed(first, w_up, b_up, w_down, b_down, gain, shift, keep, tile=512):
    hat, r = centred(first)
    normed = hat * gain + shift
    low = normed.astype(B16)
    second = normed + b_down
    for j in range(w_up.shape[1] // tile):
        at = slice(j * tile, (j + 1) * tile)
        act, slope = gelu_pair(dot(low, w_up[:, at]) + b_up[:, at])
        act = act.astype(B16)
        keep(at, act, slope)
        second = second + dot(act, w_down[at, :])
    return second, hat, r, low


def feed_both(first, w_up, b_up, w_down, b_down, g1, s1, g2, s2, d_out, slopes, keep_act, keep_inner):
    def keep(at, act, slope):
        keep_act(at, act)
        slopes[:, at] = slope

    ff = w_up.shape[1]
    second, hat, r, low = feed(first, w_up, b_up, w_down, b_down, g1, s1, keep, ff)
    hat2, r2 = centred(second)
    out = (hat2 * g2 + s2).astype(B16)
    d_second, gg2, gs2 = norm_back(hat2, r2, g2, d_out)
    d_down = d_second.astype(B16)
    gb_down = jnp.sum(d_down.astype(F32), 0, keepdims=True)
    d = (dot_nt(d_down, w_down[...]) * slopes[...]).astype(B16)
    keep_inner(slice(0, ff), d)
    gb_up = jnp.sum(d.astype(F32), 0, keepdims=True)
    gb_up = [gb_up[:, j * 512 : (j + 1) * 512] for j in range(ff // 512)]
    d_normed = d_second + dot_nt(d, w_up[...])
    d_first, gg1, gs1 = norm_back(hat, r, g1, d_normed)
    return out, d_down, d_first, low, (gg1, gs1, gb_down, gg2, gs2, *gb_up)


def cls_rows(q, k, v, count):
    total, width = q.shape
    length = total // count
    rows = count * HEADS
    own = (
        lax.broadcasted_iota(I32, (rows, width), 1) // HS
        == lax.broadcasted_iota(I32, (rows, width), 0) % HEADS
    )
    first = [
        jnp.broadcast_to(q[i * length : i * length + 1, :].astype(F32), (HEADS, width))
        for i in range(count)
    ]
    q_rows = jnp.where(own, jnp.concatenate(first, 0), 0.0).astype(B16)
    scores = dot_nt(q_rows, k[...])
    apart = (
        lax.broadcasted_iota(I32, scores.shape, 0) // HEADS
        != lax.broadcasted_iota(I32, scores.shape, 1) // length
    )
    probs = softmax(jnp.where(apart, FAR, scores)).astype(B16)
    mixed = jnp.where(own, dot(probs, v[...]), 0.0)
    return jnp.concatenate(
        [
            jnp.sum(mixed[i * HEADS : (i + 1) * HEADS], 0, keepdims=True)
            for i in range(count)
        ],
        0,
    )


def own_index(n):
    return lax.axis_index("dp") * lax.axis_size("rep") + lax.axis_index("rep")


def row(ref, e):
    return ref[e : e + 1, :]


def front_kernel(
    positives, counts, bq, bv, bo, g1, s1, bu, bd, g2, s2, p_x, q_x, wq, wk, wv, wo, wu, wd,
    pq, pk, pv, qq, qk, qv, payload,
    p_s, q_s, wqkv_s, wo_s, wu_s, wd_s, p_out, q_out, pay_s, sems, out_sems,
):
    width = q_x.shape[1]
    count = 4

    def load(i, src, dst):
        return pltpu.make_async_copy(src, dst, sems.at[i])

    w_in = (wq, wk, wv)
    first_in = [load(0, p_x, p_s)]
    first_in += [load(1 + i, w.at[1], wqkv_s.at[1, i]) for i, w in enumerate(w_in)]
    q_in = [load(4, q_x, q_s)]
    q_in += [load(5 + i, w.at[0], wqkv_s.at[0, i]) for i, w in enumerate(w_in)]
    later = [load(8, wo, wo_s), load(9, wu, wu_s), load(10, wd, wd_s)]
    for c in first_in + q_in + later:
        c.start()

    def project(x, e, held, targets):
        copies = []
        for i, (bias, target) in enumerate(zip((bq, None, bv), targets)):
            y = dot(x[...], wqkv_s[e, i])
            y = (y if bias is None else y + row(bias, e)).astype(B16)
            held[i] = y * SCALE if i == 0 else y
            copies.append(pltpu.make_async_copy(held.at[i], target, out_sems.at[3 * e + i]))
            copies[-1].start()
        return copies

    for c in first_in:
        c.wait()
    out = project(p_s, 1, p_out, (pq, pk, pv))
    for c in q_in:
        c.wait()
    out += project(q_s, 0, q_out, (qq, qk, qv))

    pay_s[...] = jnp.zeros_like(pay_s)
    lanes = lax.broadcasted_iota(I32, (1, width), 1)
    for i in range(count):
        mask = jnp.zeros((1, width), F32)
        for j in range(positives.shape[1]):
            mask = jnp.where((lanes == positives[i, j]) & (j < counts[i]), 1.0, mask)
        pay_s[8 + i : 9 + i, :] = mask
    att = [cls_rows(held.at[0], held.at[1], held.at[2], count) for held in (p_out, q_out)]
    for c in later:
        c.wait()
    for e, start, mixed, x in ((1, 0, att[0], p_s), (0, 4, att[1], q_s)):
        length = x.shape[0] // count
        own = [x[i * length : i * length + 1, :].astype(F32) for i in range(count)]
        zero = [jnp.zeros((4, width), F32)]
        mixed = jnp.concatenate([mixed] + zero, 0).astype(B16)
        first = jnp.concatenate(own + zero, 0) + dot(mixed, wo_s[e]) + row(bo, e)
        second, _, _, _ = feed(
            first, wu_s.at[e], row(bu, e), wd_s.at[e], row(bd, e), row(g1, e), row(s1, e),
            lambda at, act, slope: None, 2048,
        )
        done = centred(second)[0] * row(g2, e) + row(s2, e)
        pay_s[start : start + 4, :] = done[:4]
    payload[...] = pay_s[...].astype(B16)
    for c in out:
        c.wait()


def passage_attention_kernel(q, k, v, x, bo, wo, probs, att, first, wo_s, sem):
    copy = pltpu.make_async_copy(wo.at[1], wo_s, sem)

    @pl.when(pl.program_id(0) == 0)
    def _():
        copy.start()

    def keep_probs(t, value):
        probs[t] = value

    a = attend(q[...], k[...], v[...], 4, keep_probs)
    att[...] = a

    @pl.when(pl.program_id(0) == 0)
    def _():
        copy.wait()

    first[...] = x[...].astype(F32) + dot(a, wo_s[...]) + row(bo, 1)


def question_attention_kernel(length, q, k, v, x, bo, wo, probs, att, first):
    def keep_probs(t, value):
        probs[t] = value

    a = attend(q[...], k[...], v[...], 4, keep_probs, length)
    att[...] = a
    first[...] = x[...].astype(F32) + dot(a, wo[...]) + row(bo, 0)


def send_unit(wide, grads, table, keep, send, offset, sem_keep, sem_send):
    half, _, width = keep.shape
    blocks = 2 * half
    rows = grads.shape[0] * grads.shape[1] // (width * blocks)
    across = grads.shape[1] // width
    me = own_index(blocks)

    def start(out, base, sem):
        def body(r, carry):
            c = table[me, base + r]
            src = grads.at[
                pl.ds(pl.multiple_of(c // across * rows, rows), rows),
                pl.ds(pl.multiple_of(c % across * width, width), width),
            ] if wide else grads.at[pl.ds(pl.multiple_of(c * rows, rows), rows), :]
            pltpu.make_async_copy(src, out.at[r, pl.ds(offset, rows), :], sem).start()
            return carry

        lax.fori_loop(0, half, body, 0, unroll=True)

    start(send, half, sem_send)
    start(keep, 0, sem_keep)


def wait_units(keep, send, sem_keep, sem_send):
    pltpu.make_async_copy(send, send, sem_send).wait()
    pltpu.make_async_copy(keep, keep, sem_keep).wait()


def contrast(gathered, me, scale):
    z = jnp.concatenate([g[...] for g in gathered], 0)
    n = z.shape[0] // 16
    total_rows = 4 * n
    base = me * 4
    place = lax.broadcasted_iota(I32, (total_rows, z.shape[0]), 1)
    index = lax.broadcasted_iota(I32, (total_rows, z.shape[0]), 0)
    apart = (index // 4) ^ me
    block = jnp.zeros_like(apart)
    depth = n.bit_length() - 1
    for i in range(depth):
        block = block + (((apart >> i) & 1) << (depth - 1 - i))
    sel = block * 16 + index % 4

    def rows_at(k):
        return dot(jnp.where(place == sel + k, 1.0, 0.0).astype(B16), z)

    all_p, all_q, mask = rows_at(0), rows_at(4), rows_at(8)[:, :total_rows]
    sim = dot_nt(all_q.astype(B16), all_p.astype(B16)) * scale
    expo = jnp.exp(sim - jnp.max(sim, -1, keepdims=True))
    total = jnp.sum(expo, -1, keepdims=True)
    hit = mask * expo
    pos_total = jnp.sum(hit, -1, keepdims=True)
    terms = jnp.log(total) - jnp.log(pos_total)
    coeff = expo / total - hit / pos_total
    mine = jnp.where(
        lax.broadcasted_iota(I32, (8, total_rows), 1)
        == base + lax.broadcasted_iota(I32, (8, total_rows), 0),
        1.0,
        0.0,
    )
    d_q = dot_high(dot_high(mine, coeff), all_p) * scale
    d_p = dot_high(dot_high(mine, coeff.T), all_q) * scale
    return dot_high(mine, jnp.broadcast_to(terms, (total_rows, 128))), d_q, d_p


def question_back_kernel(
    table, gathered_a, gathered_b, x, cot, q, k, v, probs, att, first,
    g1, s1, bu, bd, g2, s2, wq, wk, wv, wo, wu, wd,
    terms, d_cls_p, x_grad, small, out, keep, send,
    wqkv_s, wo_s, wu_s, wd_s, act_s, slope_s, inner_s, g_down, g_up, g_att, sems, out_sems,
):
    copies = [
        pltpu.make_async_copy(src.at[0], dst, sems.at[i])
        for i, (src, dst) in enumerate(
            (
                (wu, wu_s),
                (wd, wd_s),
                (wo, wo_s),
                (wq, wqkv_s.at[0]),
                (wk, wqkv_s.at[1]),
                (wv, wqkv_s.at[2]),
            )
        )
    ]
    for c in copies:
        c.start()
    n = keep.shape[0] * 2
    rows = 2048 // n
    count = 4
    length = x.shape[0] // count
    width = x.shape[1]
    loss, d_q, d_p = contrast(
        (gathered_a, gathered_b), own_index(n), 2.0 / float(np.sqrt(width))
    )
    terms[...] = loss
    d_cls_p[...] = d_p
    place = lax.broadcasted_iota(I32, x.shape, 0)
    d_out = cot[...].astype(F32)
    for i in range(count):
        d_out = d_out + jnp.where(place == i * length, d_q[i : i + 1], 0.0)
    for c in copies[:2]:
        c.wait()

    def keep_act(at, value):
        act_s[:, at] = value

    def keep_inner(at, value):
        inner_s[:, at] = value

    out[...], d_down, d_first, low, sums = feed_both(
        first[...], wu_s, row(bu, 0), wd_s, row(bd, 0), row(g1, 0), row(s1, 0), row(g2, 0),
        row(s2, 0), d_out, slope_s, keep_act, keep_inner,
    )
    sems_out = (out_sems.at[0], out_sems.at[1])
    g_down[...] = dot_tn(act_s[...], d_down).astype(B16)
    send_unit(False, g_down, table, keep, send, 0, *sems_out)
    g_up[...] = dot_tn(low, inner_s[...]).astype(B16)
    send_unit(True, g_up, table, keep, send, rows, *sems_out)
    for c in copies[2:]:
        c.wait()
    d_branch = d_first.astype(B16)
    d_att = dot_nt(d_branch, wo_s[...]).astype(B16)
    dq, dk, dv = attend_back(q[...], k[...], v[...], d_att, 4, lambda t: probs[t])
    rows_x = x[...]
    for i, d in enumerate((dq, dk, dv)):
        g_att[i * width : (i + 1) * width, :] = dot_tn(rows_x, d).astype(B16)
    g_att[3 * width :, :] = dot_tn(att[...], d_branch).astype(B16)
    send_unit(False, g_att, table, keep, send, 2 * rows, *sems_out)
    x_grad[...] = (
        d_first + dot_nt(dq, wqkv_s[0]) + dot_nt(dk, wqkv_s[1]) + dot_nt(dv, wqkv_s[2])
    )
    small[...] = jnp.zeros_like(small)
    values = [jnp.sum(d.astype(F32), 0, keepdims=True) for d in (dq, dv, d_branch)]
    for i, value in enumerate((*values, *sums)):
        small[i : i + 1, :] = value
    wait_units(keep, send, *sems_out)


def passage_feed_kernel(
    steps, table, d_cls, g1, s1, bu, bd, g2, s2, cot, first, wu, wd,
    out, d_first, small, keep, send,
    cot_s, first_s, out_s, d_first_s,
    wu_s, wd_s, slope_s, act_s, inner_s, down_s, low_s, g_down, g_up, sems, back_sems, out_sems,
):
    b = pl.program_id(0)
    sems_out = (out_sems.at[0], out_sems.at[1])
    rows = 2048 // (2 * keep.shape[0])
    total_rows = act_s.shape[0]
    per = 4 // steps
    length = total_rows // steps

    def part(i):
        return pl.ds(pl.multiple_of(i * length, length), length)

    def load(i):
        return [
            pltpu.make_async_copy(first.at[part(i), :], first_s.at[part(i), :], sems.at[2 + 2 * i]),
            pltpu.make_async_copy(cot.at[part(i), :], cot_s.at[part(i), :], sems.at[3 + 2 * i]),
        ]

    def store(i):
        return [
            pltpu.make_async_copy(out_s.at[part(i), :], out.at[part(i), :], back_sems.at[2 * i]),
            pltpu.make_async_copy(
                d_first_s.at[part(i), :], d_first.at[part(i), :], back_sems.at[2 * i + 1]
            ),
        ]

    @pl.when(b < steps)
    def _():
        weights = [
            pltpu.make_async_copy(src, dst, sems.at[i])
            for i, (src, dst) in enumerate(((wu.at[1], wu_s), (wd.at[1], wd_s)))
        ]

        @pl.when(b == 0)
        def _():
            begin = load(0)
            for c in begin + weights + [c for i in range(1, steps) for c in load(i)]:
                c.start()
            small[...] = jnp.zeros_like(small)
            for c in begin + weights:
                c.wait()

        @pl.when(b > 0)
        def _():
            for c in load(b):
                c.wait()

        mine = part(b)
        place = lax.broadcasted_iota(I32, (length, cot_s.shape[1]), 0)
        d_out = cot_s[mine, :].astype(F32)
        for i in range(per):
            extra = d_cls[pl.ds(b * per + i, 1), :]
            d_out = d_out + jnp.where(place == i * (length // per), extra, 0.0)

        def keep_act(at, value):
            act_s[mine, at] = value

        def keep_inner(at, value):
            inner_s[mine, at] = value

        out_s[mine, :], down_s[mine, :], d_first_s[mine, :], low_s[mine, :], sums = feed_both(
            first_s[mine, :], wu_s, row(bu, 1), wd_s, row(bd, 1), row(g1, 1), row(s1, 1),
            row(g2, 1), row(s2, 1), d_out, slope_s, keep_act, keep_inner,
        )
        for i, value in enumerate(sums):
            small[3 + i : 4 + i, :] += value
        for c in store(b):
            c.start()

    @pl.when(b == steps)
    def _():
        g_down[...] = dot_tn(act_s[...], down_s[...]).astype(B16)
        send_unit(False, g_down, table, keep, send, 0, *sems_out)

    @pl.when(b == steps + 1)
    def _():
        g_up[...] = dot_tn(low_s[...], inner_s[...]).astype(B16)
        send_unit(True, g_up, table, keep, send, rows, *sems_out)
        for i in range(steps):
            for c in store(i):
                c.wait()
        wait_units(keep, send, *sems_out)


def passage_attention_back_kernel(
    table, small_q, small_p, d_first, q, k, v, probs, x, att, wq, wk, wv, wo,
    x_grad, keep, send,
    wqkv_s, wo_s, x_s, att_s, d_s, small, sent_s, g_att, sems, out_sems,
):
    b = pl.program_id(0)
    nb = pl.num_programs(0)
    length, width = d_first.shape
    n = 2 * keep.shape[0]
    rows = 2048 // n
    copies = [
        pltpu.make_async_copy(src, dst, sems.at[i])
        for i, (src, dst) in enumerate(
            (
                (wo.at[1], wo_s),
                (wq.at[1], wqkv_s.at[0]),
                (wk.at[1], wqkv_s.at[1]),
                (wv.at[1], wqkv_s.at[2]),
                (x, x_s),
                (att, att_s),
            )
        )
    ]

    @pl.when(b == 0)
    def _():
        for c in copies:
            c.start()
        small[...] = small_p[...]
        for c in copies[:4]:
            c.wait()

    d_branch = d_first[...].astype(B16)
    d_att = dot_nt(d_branch, wo_s[...]).astype(B16)
    dq, dk, dv = attend_back(q[...], k[...], v[...], d_att, 4, lambda t: probs[t])
    mine = pl.ds(pl.multiple_of(b * length, length), length)
    for i, d in enumerate((dq, dk, dv, d_branch)):
        d_s[i, mine, :] = d
    for i, d in enumerate((dq, dv, d_branch)):
        small[i : i + 1, :] += jnp.sum(d.astype(F32), 0, keepdims=True)
    x_grad[...] = (
        d_first[...] + dot_nt(dq, wqkv_s[0]) + dot_nt(dk, wqkv_s[1]) + dot_nt(dv, wqkv_s[2])
    )

    @pl.when(b == nb - 1)
    def _():
        sent_s[...] = jnp.zeros_like(sent_s)
        top = lax.broadcasted_iota(I32, (16, width), 0) == 0
        for e, ref in enumerate((small_q, small)):
            for i in range(NSMALL):
                sent_s[e * NSMALL + i] = jnp.where(top, ref[i : i + 1, :], 0.0).astype(B16)
        me = own_index(n)
        for base, out, sem in ((n // 2, send, out_sems.at[1]), (0, keep, out_sems.at[0])):

            def body(r, carry, base=base, out=out, sem=sem):
                pltpu.make_async_copy(
                    sent_s.at[table[me, base + r]], out.at[r, pl.ds(rows, 16), :], sem
                ).start()
                return carry

            lax.fori_loop(0, n // 2, body, 0, unroll=True)
        for c in copies[4:]:
            c.wait()
        for i in range(3):
            g_att[i * width : (i + 1) * width, :] = dot_tn(x_s[...], d_s[i]).astype(B16)
        g_att[3 * width :, :] = dot_tn(att_s[...], d_s[3]).astype(B16)
        send_unit(False, g_att, table, keep, send, 0, out_sems.at[0], out_sems.at[1])
        wait_units(keep, send, out_sems.at[0], out_sems.at[1])


def place_kernel(e, kinds, starts, n_alias, with_small, *refs):
    table = refs[0]
    pieces = refs[1 : 1 + len(starts)]
    outs = refs[1 + len(starts) + n_alias :]
    n_out = sum(4 if kind == "att" else 1 for kind in kinds)
    n_small = 9 if with_small else 0
    targets, smalls = outs[:n_out], outs[n_out : n_out + n_small]
    scratch = outs[n_out + n_small :]
    stages, sems = scratch[: len(kinds)], scratch[len(kinds)]
    small_s = scratch[len(kinds) + 1] if with_small else None
    n = starts[-1] + pieces[-1].shape[0]
    rows = 2048 // n
    me = own_index(n)
    for piece, start in zip(pieces, starts):

        def body(r, carry, piece=piece, start=start):
            c = table[me, start + r]
            k = 0
            for u, kind in enumerate(kinds):
                stage = stages[u].at[start + r]
                stage[...] = piece[r, u * rows : (u + 1) * rows, :].astype(F32)
                if kind == "down":
                    pltpu.make_async_copy(
                        stage,
                        targets[k].at[e, pl.ds(pl.multiple_of(c * rows, rows), rows), :],
                        sems.at[k],
                    ).start()
                    k += 1
                elif kind == "up":
                    pltpu.make_async_copy(
                        stage,
                        targets[k].at[
                            e,
                            pl.ds(pl.multiple_of(c // 4 * rows, rows), rows),
                            pl.ds(pl.multiple_of(c % 4 * 512, 512), 512),
                        ],
                        sems.at[k],
                    ).start()
                    k += 1
                else:
                    quarter = n // 4
                    for m in range(4):

                        @pl.when(c // quarter == m)
                        def _(m=m, k=k, stage=stage):
                            at = pl.ds(pl.multiple_of(c % quarter * rows, rows), rows)
                            pltpu.make_async_copy(
                                stage, targets[k + m].at[e, at, :], sems.at[k + m]
                            ).start()

                    k += 4
            if with_small:
                block = piece[r, len(kinds) * rows : len(kinds) * rows + 16, :].astype(F32)
                small_s[c] = block[0:8]
            return carry

        lax.fori_loop(0, piece.shape[0], body, 0)
    if with_small:
        for f in range(2):
            for i in range(8):
                smalls[i][f : f + 1, :] = small_s[f * NSMALL + i, 0:1, :]
            for j in range(4):
                smalls[8][f : f + 1, j * 512 : (j + 1) * 512] = small_s[f * NSMALL + 8 + j, 0:1, :]
    for k, target in enumerate(targets):
        pltpu.make_async_copy(target.at[e], target.at[e], sems.at[k]).wait()


def rounds_of(mesh_shape):
    dp, rep = mesh_shape["dp"], mesh_shape["rep"]
    core, *x = [1 << i for i in range(rep.bit_length() - 1)]
    y, *z = [rep << i for i in range(dp.bit_length() - 1)]
    return ([core, *x, y, *z], [core, y, *x, *z]), ([core, *x, y, *z], [core, y, *z, *x])


def order_table(rounds, n):
    depth = len(rounds[0])
    table = np.zeros((n, n), np.int32)
    for d in range(n):
        for r in range(n):
            c = d ^ (rounds[0][0] if r >> (depth - 1) & 1 else 0)
            for k in range(1, depth):
                if r >> (depth - 1 - k) & 1:
                    c ^= rounds[c & 1][k]
            table[d, r] = c
    return table


def exchange(x, masks, n):
    return lax.ppermute(x, AXES, [(d, d ^ masks[d & 1]) for d in range(n)])


def total(parts):
    return sum(p.astype(F32) for p in parts).astype(B16)


def steps_of(rounds, pairs):
    even, odd = rounds
    steps, k = [], 0
    while k < len(even):
        if even[k] in pairs:
            steps.append(((even[k], odd[k]), (even[k + 1], odd[k + 1])))
            k += 2
        else:
            steps.append(((even[k], odd[k]),))
            k += 1
    return steps


def partners(step):
    if len(step) == 1:
        return [step[0]]
    high, low = step
    return [low, high, (low[0] ^ high[0], low[1] ^ high[1])]


def join_kernel(*refs):
    *parts, out = refs
    m = parts[0].shape[0]
    for i, part in enumerate(parts):
        out[i * m : (i + 1) * m] = part[...]


def joined(order, pieces, limit=24):
    m, rows, width = pieces[0].shape
    count = len(pieces)
    return order(
        join_kernel,
        *pieces,
        name="join",
        in_specs=[VMEM] * count,
        out_specs=[VMEM],
        out_shape=[shape((count * m, rows, width), B16)],
        compiler_params=params(limit),
        cost_estimate=SHORT,
    )


class Order:
    def __init__(self):
        self.token = None

    def fence(self, arrays):
        *arrays, self.token = lax.optimization_barrier((*arrays, self.token))
        return arrays

    def __call__(self, kernel, *operands, in_specs, out_specs, out_shape, **kwargs):
        skip = 0 if self.token is None else 1
        last = skip + len(operands) + len(out_shape)

        def body(*refs):
            kernel(*refs[skip:last], *refs[last + 1 :])

        aliases = kwargs.pop("input_output_aliases", {})
        call = pl.pallas_call(
            body,
            in_specs=[ANY] * skip + in_specs,
            out_specs=list(out_specs) + [ANY],
            out_shape=list(out_shape) + [shape((8, 128))],
            input_output_aliases={k + skip: v for k, v in aliases.items()},
            **kwargs,
        )
        *outs, self.token = call(*([self.token] if skip else []), *operands)
        return outs


class Sum:
    def __init__(self, order, halving, doubling, n, keep, send):
        self.order, self.n = order, n
        self.halving, self.doubling = list(halving), list(doubling)
        self.parts, self.m, self.pieces = [keep], keep.shape[0], None
        self.got, self.out, self.now = None, [send], self.halving.pop(0)
        self.going = True

    def start(self):
        masks = partners(self.now)
        if self.pieces is None:
            self.got = [exchange(x, m, self.n) for x, m in zip(self.out, masks)]
        else:
            self.got = [exchange(x, m, self.n) for m in masks for x in self.out]

    def take(self):
        if self.pieces is None:
            self.parts += self.got
            if self.halving:
                self.now = self.halving.pop(0)
                ways = 2 ** len(self.now)
                q = self.m // ways
                self.out = [
                    total([p[i * q : (i + 1) * q] for p in self.parts]) for i in range(1, ways)
                ]
                self.m = q
                return True
            self.out = self.pieces = [total([p[:1] for p in self.parts])]
        else:
            self.pieces = self.pieces + self.got
            if not self.doubling:
                return False
            if len(self.doubling) > 1:
                self.pieces = [jnp.concatenate(self.pieces, 0)]
            self.out = self.pieces
        self.now = self.doubling.pop()
        return True


class Plan:
    def __init__(self, order):
        self.order, self.sums, self.starting = order, {}, []
        self.fresh = True

    def add(self, name, item):
        self.sums[name] = item
        self.starting.append(item)

    def flush(self):
        if not self.starting:
            return
        flat = self.order.fence([x for s in self.starting for x in s.out])
        for s in self.starting:
            s.out, flat = flat[: len(s.out)], flat[len(s.out) :]
            if s.pieces is not None:
                s.pieces = s.out
        for s in self.starting:
            s.start()
        self.starting = []

    def step(self, names):
        if not self.fresh:
            self.flush()
        items = [self.sums[name] for name in names if self.sums[name].going]
        flat = self.order.fence([x for s in items for x in s.got])
        for s in items:
            s.got, flat = flat[: len(s.got)], flat[len(s.got) :]
        for s in items:
            s.going = s.take()
            if s.going:
                self.starting.append(s)
        self.fresh = False

    def run(self, names, kernels, places):
        for name in names:
            if name in kernels:
                self.flush()
                kernels[name]()
                self.fresh = True
            elif name in places:
                self.flush()
                if not self.sums[name[-1]].going:
                    places.pop(name)()
            else:
                self.step(name.split("+"))
        while any(s.going for s in self.sums.values()):
            for name, item in self.sums.items():
                if item.going:
                    self.step([name])
        self.flush()
        for place in places.values():
            place()


class Gather:
    def __init__(self, order, x, n):
        bits = [1 << i for i in reversed(range(n.bit_length() - 1))]
        assert len(bits) % 2 == 1
        self.order, self.n = order, n
        self.stages = [bits[i : i + 2] for i in range(0, len(bits), 2)]
        self.pieces = [x[None]]
        self.issue()

    def issue(self):
        (mine,) = self.order.fence(self.pieces)
        now = self.stages.pop(0)
        masks = now if len(now) == 1 else [now[0], now[1], now[0] | now[1]]
        self.pieces = [mine] + [
            lax.ppermute(mine, AXES, [(d, d ^ m) for d in range(self.n)]) for m in masks
        ]

    def step(self):
        self.pieces = joined(self.order, self.order.fence(self.pieces), 62)
        self.issue()

    def result(self):
        return self.order.fence(self.pieces)


def params(limit):
    return pltpu.CompilerParams(vmem_limit_bytes=limit * MIB)


LONG = pl.CostEstimate(flops=200_000_000_000, bytes_accessed=1000, transcendentals=0)


SHORT = pl.CostEstimate(flops=1000, bytes_accessed=1000, transcendentals=0)


def shape(dims, dtype=F32):
    return jax.ShapeDtypeStruct(dims, dtype)


def sem(count):
    return pltpu.SemaphoreType.DMA((count,))


def shards(
    mesh_shape,
    q_tokens,
    p_tokens,
    q_cotangent,
    p_cotangent,
    positives,
    counts,
    wq,
    bq,
    wk,
    wv,
    bv,
    wo,
    bo,
    g1,
    s1,
    wu,
    bu,
    wd,
    bd,
    g2,
    s2,
):
    n = mesh_shape["dp"] * mesh_shape["rep"]
    plane, mixed = rounds_of(mesh_shape)
    pairs = plane[0][-2:-1]
    table = jnp.asarray(order_table(plane, n))
    mixed_table = jnp.asarray(order_table(mixed, n))
    qn, ql, h = q_tokens.shape
    pn, plen, _ = p_tokens.shape
    ff = wu.shape[2]
    qr, pr = qn * ql, pn * plen
    assert qn == 4 and pn == 4 and h == 512 and ff == 2048 and 24 <= n and 4 * n <= h
    q_x, p_x = q_tokens.reshape(qr, h), p_tokens.reshape(pr, h)
    q_cot, p_cot = q_cotangent.reshape(qr, h), p_cotangent.reshape(pr, h)
    order = Order()

    def whole(*dims):
        return pl.BlockSpec(dims, lambda b: (0,) * len(dims))

    one, wide = whole(2, h), whole(2, ff)
    seq_block = pl.BlockSpec((plen, h), lambda b: (b, 0))
    pq, pk, pv, qq, qk, qv, payload = order(
        front_kernel,
        positives, counts, bq, bv, bo, g1, s1, bu, bd, g2, s2, p_x, q_x, wq, wk, wv, wo, wu, wd,
        name="front",
        in_specs=[SMEM] * 2 + [VMEM] * 9 + [ANY] * 8,
        out_specs=[ANY] * 6 + [VMEM],
        out_shape=[shape((pr, h), B16)] * 3 + [shape((qr, h), B16)] * 3 + [shape((16, h), B16)],
        scratch_shapes=[
            pltpu.VMEM((pr, h), B16),
            pltpu.VMEM((qr, h), B16),
            pltpu.VMEM((2, 3, h, h), B16),
            pltpu.VMEM((2, h, h), B16),
            pltpu.VMEM((2, h, ff), B16),
            pltpu.VMEM((2, ff, h), B16),
            pltpu.VMEM((3, pr, h), B16),
            pltpu.VMEM((3, qr, h), B16),
            pltpu.VMEM((16, h), F32),
            sem(11),
            sem(6),
        ],
        compiler_params=params(62),
        cost_estimate=LONG,
    )
    gather = Gather(order, payload, n)

    def passages(kernel, name, at, count, operands, in_specs, outs, before, **kwargs):
        def spec(block):
            if not isinstance(block, tuple):
                return block
            axis = block.index(None) if None in block else len(block) - 2
            return pl.BlockSpec(
                block, lambda b: tuple(b + at if i == axis else 0 for i in range(len(block)))
            )

        n_in, n_before = len(operands), len(before)

        def body(*refs):
            kernel(*refs[:n_in], *refs[n_in + n_before :])

        return order(
            body,
            *operands,
            *before,
            name=name,
            grid=(count,),
            in_specs=[spec(x) for x in in_specs] + [ANY] * n_before,
            out_specs=[spec(block) for block, _ in outs],
            out_shape=[s for _, s in outs],
            input_output_aliases={n_in + i: i for i in range(n_before)},
            compiler_params=params(62),
            cost_estimate=LONG,
            **kwargs,
        )

    seq, seq_wide = (plen, h), (plen, ff)
    probs_block = (None, 2, 4 * plen, plen)

    def attention(at, count, before):
        return passages(
            passage_attention_kernel, "passage_attention", at, count,
            (pq, pk, pv, p_x, bo, wo),
            [seq] * 4 + [one, ANY],
            [
                (probs_block, shape((pn, 2, 4 * plen, plen), B16)),
                (seq, shape((pr, h), B16)),
                (seq, shape((pr, h))),
            ],
            before,
            scratch_shapes=[pltpu.VMEM((h, h), B16), pltpu.SemaphoreType.DMA],
        )

    part = attention(0, 2, [])
    gather.step()
    q_probs, q_att, q_first = order(
        functools.partial(question_attention_kernel, ql),
        qq, qk, qv, q_x, bo, wo,
        name="question_attention",
        grid=(1,),
        in_specs=[whole(qr, h)] * 4 + [one, pl.BlockSpec((None, h, h), lambda b: (0, 0, 0))],
        out_specs=[whole(2, 4 * qr, qr), whole(qr, h), whole(qr, h)],
        out_shape=[shape((2, 4 * qr, qr), B16), shape((qr, h), B16), shape((qr, h))],
        compiler_params=params(62),
        cost_estimate=LONG,
    )
    while gather.stages:
        gather.step()
    gathered = [x.reshape(-1, h) for x in gather.result()]

    rows = 2048 // n
    half = n // 2
    terms, d_cls_p, q_grad, small_q, q_out, q_keep, q_send = order(
        question_back_kernel,
        mixed_table, *gathered, q_x, q_cot, qq, qk, qv, q_probs, q_att, q_first,
        g1, s1, bu, bd, g2, s2, wq, wk, wv, wo, wu, wd,
        name="question_back",
        in_specs=[SMEM] + [VMEM] * 16 + [ANY] * 6,
        out_specs=[VMEM] * 5 + [ANY] * 2,
        out_shape=[
            shape((8, 128)),
            shape((8, h)),
            shape((qr, h)),
            shape((16, h)),
            shape((qr, h), B16),
            shape((half, 3 * rows, h), B16),
            shape((half, 3 * rows, h), B16),
        ],
        scratch_shapes=[
            pltpu.VMEM((3, h, h), B16),
            pltpu.VMEM((h, h), B16),
            pltpu.VMEM((h, ff), B16),
            pltpu.VMEM((ff, h), B16),
            pltpu.VMEM((qr, ff), B16),
            pltpu.VMEM((qr, ff), F32),
            pltpu.VMEM((qr, ff), B16),
            pltpu.VMEM((ff, h), B16),
            pltpu.VMEM((h, ff), B16),
            pltpu.VMEM((4 * h, h), B16),
            sem(6),
            sem(2),
        ],
        compiler_params=params(62),
        cost_estimate=LONG,
    )
    steps = steps_of(plane, pairs)
    plan = Plan(order)
    plan.add("q", Sum(order, steps_of(mixed, ()), steps, n, q_keep, q_send))
    r = {}

    def run_attention():
        r["p_probs"], r["p_att"], r["p_first"] = attention(2, 2, part)

    parts_of = 2
    def run_feed():
        r["p_out"], r["d_first"], r["small_p"], *out = order(
            functools.partial(passage_feed_kernel, parts_of),
            table, d_cls_p, g1, s1, bu, bd, g2, s2, p_cot, r["p_first"], wu, wd,
            name="passage_feed",
            grid=(parts_of + 2,),
            in_specs=[SMEM, whole(8, h), one, one, wide, one, one, one] + [ANY] * 4,
            out_specs=[ANY, ANY, whole(16, h), ANY, ANY],
            out_shape=[shape((pr, h), B16), shape((pr, h)), shape((16, h))]
            + [shape((half, 2 * rows, h), B16)] * 2,
            scratch_shapes=[
                pltpu.VMEM((pr, h), B16),
                pltpu.VMEM((pr, h), F32),
                pltpu.VMEM((pr, h), B16),
                pltpu.VMEM((pr, h), F32),
                pltpu.VMEM((h, ff), B16),
                pltpu.VMEM((ff, h), B16),
                pltpu.VMEM((pr // parts_of, ff), F32),
                pltpu.VMEM((pr, ff), B16),
                pltpu.VMEM((pr, ff), B16),
                pltpu.VMEM((pr, h), B16),
                pltpu.VMEM((pr, h), B16),
                pltpu.VMEM((ff, h), B16),
                pltpu.VMEM((h, ff), B16),
                sem(2 + 2 * parts_of),
                sem(2 * parts_of),
                sem(2),
            ],
            compiler_params=params(62),
            cost_estimate=LONG,
        )
        plan.add("f", Sum(order, steps, steps, n, *out))

    def run_back():
        r["p_grad"], *out = order(
            passage_attention_back_kernel,
            table, small_q, r["small_p"], r["d_first"], pq, pk, pv, r["p_probs"], p_x, r["p_att"], wq, wk, wv, wo,
            name="passage_attention_back",
            grid=(pn,),
            in_specs=[SMEM, whole(16, h), whole(16, h)] + [seq_block] * 4
            + [pl.BlockSpec(probs_block, lambda b: (b, 0, 0, 0))] + [ANY] * 6,
            out_specs=[seq_block, ANY, ANY],
            out_shape=[shape((pr, h))] + [shape((half, rows + 16, h), B16)] * 2,
            scratch_shapes=[
                pltpu.VMEM((3, h, h), B16),
                pltpu.VMEM((h, h), B16),
                pltpu.VMEM((pr, h), B16),
                pltpu.VMEM((pr, h), B16),
                pltpu.VMEM((4, pr, h), B16),
                pltpu.VMEM((16, h), F32),
                pltpu.VMEM((n, 16, h), B16),
                pltpu.VMEM((4 * h, h), B16),
                sem(6),
                sem(2),
            ],
            compiler_params=params(62),
            cost_estimate=LONG,
        )
        plan.add("a", Sum(order, steps, steps, n, *out))

    def place(e, kinds, which, before, with_small):
        pieces = plan.sums[which].pieces
        starts, at = [], 0
        for piece in pieces:
            starts.append(at)
            at += piece.shape[0]
        dims = []
        for kind in kinds:
            dims += {"down": [(2, ff, h)], "up": [(2, h, ff)], "att": [(2, h, h)] * 4}[kind]
        outs = [shape(d) for d in dims]
        smalls = [shape((2, h))] * 8 + [shape((2, ff))] if with_small else []
        return order(
            functools.partial(
                place_kernel, e, kinds, tuple(starts), len(before), with_small
            ),
            table, *pieces, *before,
            name="place",
            in_specs=[SMEM] + [VMEM] * len(pieces) + [ANY] * len(before),
            out_specs=[ANY] * len(outs) + [VMEM] * len(smalls),
            out_shape=outs + smalls,
            input_output_aliases={1 + len(pieces) + i: i for i in range(len(before))},
            scratch_shapes=[pltpu.VMEM((n, rows, h), F32) for _ in kinds]
            + [sem(len(outs))]
            + ([pltpu.VMEM((n, 8, h), F32)] if with_small else []),
            compiler_params=params(40),
            cost_estimate=SHORT,
        )

    def place_q():
        r["q_down"], r["q_up"], *r["q_att"] = place(0, ("down", "up", "att"), "q", [], False)

    def place_f():
        r["down"], r["up"] = place(1, ("down", "up"), "f", [r["q_down"], r["q_up"]], False)

    def place_a():
        r["att"] = place(1, ("att",), "a", r["q_att"], True)

    kernels = {"attention": run_attention, "feed": run_feed, "back": run_back}
    plan.run(PLAN, kernels, {"place_q": place_q, "place_f": place_f, "place_a": place_a})
    down, up = r["down"], r["up"]
    gq, gk, gv, go, *smalls = r["att"]
    sbq, sbv, sbo, sg1, ss1, sbd, sg2, ss2, sbu = smalls
    return (
        q_out.reshape(qn, ql, h),
        r["p_out"].reshape(pn, plen, h),
        terms[:qn, 0],
        q_grad.reshape(qn, ql, h),
        r["p_grad"].reshape(pn, plen, h),
        gq, sbq, gk, gv, sbv, go, sbo, sg1, ss1, up, sbu, down, sbd, sg2, ss2,
    )


def solution(mesh):
    split = P(AXES)
    return jax.shard_map(
        functools.partial(shards, dict(mesh.shape)),
        mesh=mesh,
        in_specs=(split,) * 6 + (P(),) * 15,
        out_specs=(split,) * 5 + (P(),) * 15,
        check_vma=False,
    )
```
